32 devices in a mesh: group: 4 (over y, x), member: 8 (over z, core).
Axes of the slice: x: 2, y: 2, z: 4, core: 2. Of those that a mesh axis runs over, the one named last changes fastest.
Arguments:
- source_vectors: bfloat16 [32768, 256], P(('group', 'member')), may hold values from -4 to 4
- target_vectors: bfloat16 [32768, 256], P(('group', 'member')), may hold values from -4 to 4
- source_mass: float32 [32768], P(('group', 'member')), may hold values from -1 to 1
- target_mass: float32 [32768], P(('group', 'member')), may hold values from -1 to 1
- candidates: int32 [128, 8], P(('group', 'member')), may hold values from 0 to 127, as said below
Outputs:
- source_potential: float32 [32768], P(('group', 'member'))
- target_potential: float32 [32768], P(('group', 'member'))
The draws below stay inside these ranges and needn't reach their ends.
Inputs may be any that keep to these rules, and one draw needn't show every extreme that they name: Target block t lies on device t // 4, devices counted group-major (group index times 8 plus member index). Candidates 0 to 6 of a source block lie on devices of its own group; of these 4 * (7) candidates of one device, at most 4 lie on any one device, and in each group one device holds exactly 4 of them for every device of the group. The last candidate of each source block on the device of group g and member m is block g of the device of group g2 and member m, the 4 source blocks of one device taking 4 different g2.
All inputs are finite; a program needn't handle non-finite values.
Results may differ from the reference program's by a relative error of at most 0.0003.
Values may be sent and summed in bfloat16 or wider, within the bound.
No kernel may reach another device: no remote copies, remote signals or barrier semaphores. Data moves between devices by JAX's collectives and lax.ppermute only.
A program may use at most 64 MiB of HBM per device.

```python
import jax
import jax.numpy as jnp
from jax import lax

BLOCK_ENTITIES = 256
WIDTH = 256
SOURCE_DEV = 4
CANDIDATE_BLOCKS = 8
ITERS = 2
TARGET_DEV = 4
CAPACITY = 4
SOURCE_BLOCKS = 128
TARGET_BLOCKS = 128
SOURCE_ROWS = 32768
TARGET_ROWS = 32768
N_GROUP = 4
N_MEMBER = 8
DEVICES = 32


def candidate_table(key):
    members = N_MEMBER
    groups = N_GROUP
    device_count = DEVICES
    wanted = SOURCE_DEV * (CANDIDATE_BLOCKS - 1)
    spots = members * CAPACITY
    seeds = jax.random.split(key, 5)
    hubs = jax.random.randint(seeds[0], (groups,), 0, members)
    device = jnp.arange(device_count, dtype=jnp.int32)
    group_of = device // members
    member_of = device % members
    ranking = jax.vmap(lambda sub: jax.random.permutation(sub, spots))(jax.random.split(seeds[1], device_count))
    spot_peer = jnp.arange(spots, dtype=jnp.int32) // CAPACITY
    is_hub = spot_peer[None, :] == hubs[group_of][:, None]
    ordering = jnp.where(is_hub, 0, spots) + ranking
    chosen = jnp.argsort(ordering, axis=1)[:, :wanted]
    shuffle = jax.vmap(lambda sub: jax.random.permutation(sub, wanted))(jax.random.split(seeds[2], device_count))
    chosen = jnp.take_along_axis(chosen, shuffle, axis=1)
    partner = chosen // CAPACITY
    local_block = jax.random.randint(seeds[3], (device_count, wanted), 0, TARGET_DEV)
    inside = ((group_of[:, None] * members + partner) * TARGET_DEV + local_block).reshape(device_count, SOURCE_DEV, CANDIDATE_BLOCKS - 1)
    mirror = jax.vmap(lambda sub: jax.random.permutation(sub, groups))(jax.random.split(seeds[4], device_count))
    across = (mirror * members + member_of[:, None]) * TARGET_DEV + group_of[:, None]
    table = jnp.concatenate([inside, across[:, :, None]], axis=2)
    return table.reshape(device_count * SOURCE_DEV, CANDIDATE_BLOCKS).astype(jnp.int32)


def target_table(key):
    seeds = jax.random.split(key, 4)
    table = jnp.clip(0.25 * jax.random.normal(seeds[3], (TARGET_ROWS, WIDTH), jnp.float32), -3.0, 3.0)
    return table


def draw_target_vectors(key, part):
    return target_table(jax.random.fold_in(key, 101)).astype(jnp.bfloat16)


def draw_candidates(key, part):
    return candidate_table(jax.random.fold_in(key, 202))


def draw_source_vectors(key, part):
    seeds = jax.random.split(jax.random.fold_in(key, 303), 1)
    values = jnp.clip(0.25 * jax.random.normal(seeds[0], (SOURCE_ROWS, WIDTH), jnp.float32), -3.0, 3.0)
    return values.astype(jnp.bfloat16)


def steps_of(stream_key, dims, cuts, least, high):
    def one(dim, parts):
        steps = jax.random.uniform(jax.random.fold_in(jax.random.fold_in(stream_key, 6), dim), (parts,), jnp.float32, least / len(cuts), high / len(cuts))
        return jnp.repeat(jnp.exp(steps), dims[dim] // parts).reshape((-1,) + (1,) * (len(dims) - dim - 1))

    level = one(*cuts[0])
    for cut in cuts[1:]:
        level = level * one(*cut)
    return level


def setup_inputs(seed: int = 0) -> dict:
    key_list = jax.random.split(jax.random.key(seed), 6)
    source_vectors = draw_source_vectors(jax.random.fold_in(key_list[5], 71), 0)
    target_vectors = draw_target_vectors(jax.random.fold_in(key_list[5], 71), 0)
    source_mass = jnp.clip(jax.random.uniform(key_list[2], (SOURCE_ROWS,), jnp.float32, -1.0, 1.0) * steps_of(key_list[2], (SOURCE_ROWS,), ((0, 32),), -0.4, 0.0), -1.0, 1.0)
    target_mass = jnp.clip(jax.random.uniform(key_list[3], (TARGET_ROWS,), jnp.float32, -1.0, 1.0) * steps_of(key_list[3], (TARGET_ROWS,), ((0, 32),), -0.4, 0.0), -1.0, 1.0)
    candidates = draw_candidates(jax.random.fold_in(key_list[5], 71), 0)
    return dict(source_vectors=source_vectors, target_vectors=target_vectors, source_mass=source_mass, target_mass=target_mass, candidates=candidates)


entropy_strength = 0.3


def log_partition(values, axis):
    largest_score = jnp.max(values, axis=axis, keepdims=True)
    return jnp.squeeze(largest_score, axis) + jnp.log(jnp.sum(jnp.exp(values - largest_score), axis=axis))


def reference(source_vectors, target_vectors, source_mass, target_mass, candidates):
    source_blocks = source_vectors.reshape(SOURCE_BLOCKS, BLOCK_ENTITIES, WIDTH)
    target_blocks = target_vectors.reshape(TARGET_BLOCKS, BLOCK_ENTITIES, WIDTH)
    source_marginal = source_mass.reshape(SOURCE_BLOCKS, BLOCK_ENTITIES)
    target_marginal = target_mass.reshape(TARGET_BLOCKS, BLOCK_ENTITIES)
    target_current = jnp.zeros((TARGET_BLOCKS, BLOCK_ENTITIES), jnp.float32)
    source_current = jnp.zeros((SOURCE_BLOCKS, BLOCK_ENTITIES), jnp.float32)
    for step in range(ITERS):
        def visit(carry, item, potentials=target_current):
            largest_score, running_sum = carry
            block_rows, weight_values, picks = item
            key_entries = jnp.take(target_blocks, picks, axis=0).reshape(CANDIDATE_BLOCKS * BLOCK_ENTITIES, WIDTH)
            score_matrix = jnp.dot(block_rows, key_entries.T, preferred_element_type=jnp.float32)
            column_potential = jnp.take(potentials, picks, axis=0).reshape(CANDIDATE_BLOCKS * BLOCK_ENTITIES)
            updated_value = entropy_strength * weight_values - entropy_strength * log_partition((score_matrix + column_potential[None, :]) / entropy_strength, 1)
            centered_scores = ((score_matrix + updated_value[:, None]) / entropy_strength).reshape(BLOCK_ENTITIES, CANDIDATE_BLOCKS, BLOCK_ENTITIES)
            column_top = jnp.max(centered_scores, axis=0)
            column_sum = jnp.sum(jnp.exp(centered_scores - column_top[None]), axis=0)
            for cand in range(CANDIDATE_BLOCKS):
                target = picks[cand]
                old_top = largest_score[target]
                new_top = jnp.maximum(old_top, column_top[cand])
                new_total = running_sum[target] * jnp.exp(old_top - new_top) + column_sum[cand] * jnp.exp(column_top[cand] - new_top)
                largest_score = largest_score.at[target].set(new_top)
                running_sum = running_sum.at[target].set(new_total)
            return (largest_score, running_sum), updated_value

        start = (jnp.full((TARGET_BLOCKS, BLOCK_ENTITIES), -jnp.inf, jnp.float32), jnp.zeros((TARGET_BLOCKS, BLOCK_ENTITIES), jnp.float32))
        (largest_score, running_sum), source_current = lax.scan(visit, start, (source_blocks, source_marginal, candidates.astype(jnp.int32)))
        target_current = entropy_strength * target_marginal - entropy_strength * (largest_score + jnp.log(running_sum))
    return source_current.reshape(SOURCE_ROWS), target_current.reshape(TARGET_ROWS)
```

```python
import functools

import jax
import jax.numpy as jnp
from jax import lax
from jax.experimental import pallas as pl
from jax.experimental.pallas import tpu as pltpu
from jax.sharding import PartitionSpec as P

ITERS = 2


entropy_strength = 0.3
very_low = -1e30


def log_partition(values, axis):
    largest_score = jnp.max(values, axis=axis, keepdims=True)
    return jnp.squeeze(largest_score, axis) + jnp.log(
        jnp.sum(jnp.exp(values - largest_score), axis=axis)
    )


def slot_layout(lists, per_device, members, capacity):
    owner = lists // per_device
    partner = owner % members
    local_block = lists % per_device
    ordering = jnp.arange(lists.shape[-1], dtype=jnp.int32)
    matching = partner[..., :, None] == partner[..., None, :]
    earlier = ordering[None, :] < ordering[:, None]
    position = jnp.sum(jnp.logical_and(matching, earlier).astype(jnp.int32), axis=-1)
    return (partner * capacity + position, local_block)


def trade_member(values):
    return lax.all_to_all(values, "member", split_axis=0, concat_axis=0, tiled=True)


def trade_group(values):
    return lax.all_to_all(values, "group", split_axis=0, concat_axis=0, tiled=True)


def tile_terms(sources, target_blocks, picks, side, by_rows):
    tile_count, block_rows, width = sources.shape
    batch = 4
    grouped = (
        sources.reshape(tile_count // batch, batch, block_rows, width),
        picks.reshape(tile_count // batch, batch),
        side.reshape(tile_count // batch, batch, block_rows),
    )

    def visit(grouped_part):
        source_portion, pick_part, side_portion = grouped_part
        key_entries = jnp.take(target_blocks, pick_part, axis=0)
        score_matrix = jnp.einsum(
            "umk,ugk->umg", source_portion, key_entries, preferred_element_type=jnp.float32
        )
        if by_rows:
            return log_partition((score_matrix + side_portion[:, None, :]) / entropy_strength, 2)
        return log_partition((score_matrix + side_portion[:, :, None]) / entropy_strength, 1)

    return lax.map(visit, grouped).reshape(tile_count, block_rows)


def owner_update(slot_terms, mirror_terms, incoming, target_marginal):
    output_list = []
    for local_block in range(target_marginal.shape[0]):
        masked = jnp.where((incoming == local_block)[:, None], slot_terms, very_low)
        stacked = jnp.concatenate([masked, mirror_terms[local_block][None, :]], axis=0)
        output_list.append(log_partition(stacked, 0))
    return entropy_strength * target_marginal - entropy_strength * jnp.stack(output_list)


def shards_any(source_vectors, target_vectors, source_mass, target_mass, candidates):
    members = lax.axis_size("member")
    groups = lax.axis_size("group")
    own_member = lax.axis_index("member")
    source_count, cand_count = candidates.shape
    inside_count = cand_count - 1
    block_rows = source_vectors.shape[0] // source_count
    width = source_vectors.shape[1]
    target_count = target_vectors.shape[0] // block_rows
    capacity = (source_count * inside_count + members - 1) // members
    spots = members * capacity
    source_blocks = source_vectors.reshape(source_count, block_rows, width)
    target_blocks = target_vectors.reshape(target_count, block_rows, width)
    source_marginal = source_mass.reshape(source_count, block_rows)
    target_marginal = target_mass.reshape(target_count, block_rows)
    own_lists = candidates[:, :inside_count]
    own_spots, own_local = slot_layout(
        own_lists.reshape(1, source_count * inside_count), target_count, members, capacity
    )
    own_spots = own_spots[0]
    all_lists = lax.all_gather(own_lists, "member", axis=0, tiled=True)
    their_spots, their_local = slot_layout(
        all_lists.reshape(members, source_count * inside_count), target_count, members, capacity
    )
    wanted_spots = own_member * capacity + jnp.arange(capacity, dtype=jnp.int32)
    hits = their_spots[:, :, None] == wanted_spots[None, None, :]
    incoming = (jnp.sum(jnp.where(hits, their_local[:, :, None] + 1, 0), axis=1) - 1).reshape(spots)
    picks = jnp.maximum(incoming, 0)
    mirror_group = candidates[:, inside_count] // target_count // members
    spot_range = jnp.arange(spots, dtype=jnp.int32)
    group_range = jnp.arange(groups, dtype=jnp.int32)
    source_of = jnp.arange(source_count * inside_count, dtype=jnp.int32) // inside_count
    slot_index = jnp.sum(
        jnp.where(own_spots[:, None] == spot_range[None, :], source_of[:, None], 0), axis=0
    )
    mirror_index = jnp.sum(
        jnp.where(
            mirror_group[:, None] == group_range[None, :],
            jnp.arange(source_count, dtype=jnp.int32)[:, None],
            0,
        ),
        axis=0,
    )
    slot_payload = jnp.take(source_blocks, slot_index, axis=0)
    mirror_payload = jnp.take(source_blocks, mirror_index, axis=0)
    arrived = lax.all_to_all(
        slot_payload.reshape(members, capacity, block_rows, width),
        "member",
        split_axis=0,
        concat_axis=0,
        tiled=True,
    ).reshape(spots, block_rows, width)
    arrived_mirror = lax.all_to_all(
        mirror_payload, "group", split_axis=0, concat_axis=0, tiled=True
    )
    target_current = jnp.zeros((target_count, block_rows), jnp.float32)
    for step in range(ITERS):
        row_slots = tile_terms(
            arrived, target_blocks, picks, jnp.take(target_current, picks, axis=0), True
        )
        row_mirror = tile_terms(arrived_mirror, target_blocks, group_range, target_current, True)
        slot_back = trade_member(row_slots.reshape(members, capacity, block_rows)).reshape(
            spots, block_rows
        )
        mirror_back = trade_group(row_mirror)
        collected_rows = jnp.concatenate(
            [
                jnp.take(slot_back, own_spots, axis=0).reshape(
                    source_count, inside_count, block_rows
                ),
                jnp.take(mirror_back, mirror_group, axis=0)[:, None],
            ],
            axis=1,
        )
        source_current = entropy_strength * source_marginal - entropy_strength * log_partition(
            collected_rows, 1
        )
        slot_sides = trade_member(
            jnp.take(source_current, slot_index, axis=0).reshape(members, capacity, block_rows)
        ).reshape(spots, block_rows)
        mirror_sides = trade_group(jnp.take(source_current, mirror_index, axis=0))
        column_slots = tile_terms(arrived, target_blocks, picks, slot_sides, False)
        column_mirror = tile_terms(arrived_mirror, target_blocks, group_range, mirror_sides, False)
        target_current = owner_update(column_slots, column_mirror, incoming, target_marginal)
    return (
        source_current.reshape(source_count * block_rows),
        target_current.reshape(target_count * block_rows),
    )


LOG2E = 1.4426950408889634
TO_LOGIT = LOG2E / entropy_strength
TO_POTENTIAL = entropy_strength / LOG2E
TILE_SLOTS = 40
UNROLL = 4
SOURCE_SLOTS = 16
TARGET_SLOTS = 11


def merge(parts):
    top = functools.reduce(jnp.maximum, parts)
    return top + LOG2E * jnp.log(sum(jnp.exp2(part - top) for part in parts))


def swapped(rows, size):
    pieces = [rows[start : start + size] for start in range(0, rows.shape[0], size)]
    return jnp.concatenate([pieces[index ^ 1] for index in range(len(pieces))], axis=0)


def source_bias(mass_refs, part_refs):
    own, core, near, cross = (ref[...] for ref in part_refs)
    core = swapped(core, 4)
    near = swapped(near, 8)
    cross = swapped(swapped(cross, 4), 8)
    mass = jnp.concatenate([ref[0:4] for ref in mass_refs], axis=0)
    return mass - merge([own, core, near, cross])


def target_bias(scalars, columns, partner, mirrors, scratch):
    group = scalars[2, 1]
    scratch[...] = jnp.full(scratch.shape, very_low, jnp.float32)
    for offset, ref in enumerate(mirrors, 1):
        scratch[pl.ds(group ^ offset, 1), :] = ref[0:1]
        scratch[pl.ds(4 + (group ^ offset), 1), :] = ref[1:2]
    theirs = jnp.concatenate([partner[4:8], partner[0:4]], axis=0)
    mass = jnp.concatenate([columns[12:16], partner[12:16]], axis=0)
    inside = mass - merge([columns[0:8], theirs, scratch[0:8]])
    across = [
        ref[3:4] - merge([ref[2:3], columns[7 + offset : 8 + offset]])
        for offset, ref in enumerate(mirrors, 1)
    ]
    return jnp.concatenate([inside, *across, jnp.zeros((5, inside.shape[1]), jnp.float32)], axis=0)


def load_blocks(block_refs, source_buffer, target_buffer, semaphores):
    copies = []
    for index in range(4):
        copies.append((block_refs[index], source_buffer.at[pl.ds(4 * index, 4)]))
    for index in range(2):
        copies.append((block_refs[4 + index], target_buffer.at[pl.ds(4 * index, 4)]))
    for index in range(3):
        copies.append((block_refs[6 + index], target_buffer.at[pl.ds(8 + index, 1)]))
    started = []
    for index, (origin, place) in enumerate(copies):
        copy = pltpu.make_async_copy(origin, place, semaphores.at[index])
        copy.start()
        started.append(copy)
    return started


def run_tiles(scalars, ids, summed, summed_row, kept, kept_row, kept_count, bias, tops, sums):
    def visit(step, carry):
        for inner in range(UNROLL):
            slot = step * UNROLL + inner
            first = scalars[summed_row, slot]
            second = scalars[kept_row, slot]
            score = lax.dot_general(
                summed[first], kept[second], (((1,), (1,)), ((), ())), preferred_element_type=jnp.float32
            )
            logits = score * TO_LOGIT
            if bias is not None:
                shift = bias[first]
                logits = logits + jnp.concatenate([shift, shift], axis=1)
            top = jnp.max(logits, axis=0, keepdims=True)
            tops[pl.ds(slot, 1), :] = top
            sums[pl.ds(slot, 1), :] = jnp.sum(jnp.exp2(logits - top), axis=0, keepdims=True)
        return carry

    lax.fori_loop(0, (scalars[2, 0] + UNROLL - 1) // UNROLL, visit, 0)
    id_rows = jnp.concatenate([ids[...], ids[...]], axis=1)
    top_rows = tops[...]
    sum_rows = sums[...]
    best, total = [], []
    for block in range(kept_count):
        mine = id_rows == block
        top = jnp.max(jnp.where(mine, top_rows, very_low), axis=0, keepdims=True)
        best.append(top)
        total.append(jnp.sum(jnp.where(mine, sum_rows * jnp.exp2(top_rows - top), 0.0), axis=0, keepdims=True))
    best = jnp.concatenate(best, axis=0)
    total = jnp.concatenate(total, axis=0)
    return jnp.where(total > 0, best + LOG2E * jnp.log(jnp.where(total > 0, total, 1.0)), very_low)


def fill_bias(rows, bias):
    turned = rows.T
    for slot in range(bias.shape[0]):
        bias[slot] = jnp.broadcast_to(turned[:, slot : slot + 1], bias.shape[1:])


def rows_kernel(first_pass, *refs):
    scalars, ids = refs[:2]
    block_refs = refs[2:11]
    rest = refs[11:]
    if first_pass:
        out, source_buffer, target_buffer, tops, sums, semaphores = rest
        bias = None
    else:
        columns, partner, *mirrors = rest[:5]
        out, source_buffer, target_buffer, tops, sums, semaphores, bias, scratch = rest[5:]
    started = load_blocks(block_refs, source_buffer, target_buffer, semaphores)
    if not first_pass:
        fill_bias(target_bias(scalars, columns, partner, mirrors, scratch), bias)
    for copy in started:
        copy.wait()
    out[...] = run_tiles(
        scalars, ids, target_buffer, 1, source_buffer, 0, SOURCE_SLOTS, bias, tops, sums
    )


def columns_kernel(last_pass, *refs):
    scalars, ids = refs[:2]
    block_refs = refs[2:11]
    masses, parts, target_mass = refs[11:15], refs[15:19], refs[19]
    out = refs[20]
    rest = refs[21:]
    if last_pass:
        potential, *rest = rest
    source_buffer, target_buffer, tops, sums, semaphores, bias = rest
    started = load_blocks(block_refs, source_buffer, target_buffer, semaphores)
    rows = source_bias(masses, parts)
    fill_bias(rows, bias)
    if last_pass:
        for block in range(4):
            for half in range(2):
                potential[2 * block + half : 2 * block + half + 1, :] = (
                    TO_POTENTIAL * rows[block : block + 1, 128 * half : 128 * (half + 1)]
                )
    for copy in started:
        copy.wait()
    out[0:TARGET_SLOTS, :] = run_tiles(
        scalars, ids, source_buffer, 0, target_buffer, 1, TARGET_SLOTS, bias, tops, sums
    )
    out[TARGET_SLOTS : TARGET_SLOTS + 1, :] = jnp.zeros((1, out.shape[1]), jnp.float32)
    out[12:16, :] = target_mass[0:4]


def forward_kernel(scalars, columns, partner, *outs):
    group = scalars[2, 1]
    for offset, out in enumerate(outs, 1):
        block = group ^ offset
        out[0:1, :] = columns[7 + offset : 8 + offset]
        out[1:2, :] = partner[7 + offset : 8 + offset]
        out[2:3, :] = merge([columns[pl.ds(block, 1), :], partner[pl.ds(4 + block, 1), :]])
        out[3:4, :] = columns[pl.ds(12 + block, 1), :]


def finish_kernel(scalars, columns, partner, *rest):
    *mirrors, out, scratch = rest
    group = scalars[2, 1]
    scratch[...] = jnp.full(scratch.shape, very_low, jnp.float32)
    for offset, ref in enumerate(mirrors, 1):
        scratch[pl.ds(group ^ offset, 1), :] = ref[7 + offset : 8 + offset]
    rows = columns[12:16] - merge([columns[0:4], partner[4:8], scratch[0:4]])
    for block in range(4):
        for half in range(2):
            out[2 * block + half : 2 * block + half + 1, :] = (
                TO_POTENTIAL * rows[block : block + 1, 128 * half : 128 * (half + 1)]
            )


def spaces(*kinds):
    return [pl.BlockSpec(memory_space=kind) for kind in kinds]


SMEM, VMEM = pltpu.SMEM, pltpu.VMEM


def call(kernel, inputs, kinds, outs, scratch, flops=0):
    return pl.pallas_call(
        kernel,
        out_shape=[jax.ShapeDtypeStruct(shape, jnp.float32) for shape in outs],
        in_specs=spaces(*kinds),
        out_specs=spaces(*(VMEM for _ in outs)),
        scratch_shapes=scratch,
        compiler_params=pltpu.CompilerParams(vmem_limit_bytes=32 << 20),
    )(*inputs)


def swap(values, axis, size, bit):
    return lax.ppermute(values, axis, [(index, index ^ bit) for index in range(size)])


def tile_lists(candidates, own_group, own_member, members, per_device):
    owner = candidates // per_device
    local = candidates % per_device
    apart = (owner % members) ^ own_member
    last = candidates.shape[1] - 1
    mirror = (owner // members) ^ own_group
    is_last = jnp.arange(last + 1)[None, :] == last
    source = jnp.broadcast_to(jnp.arange(SOURCE_SLOTS, dtype=jnp.int32)[:, None], candidates.shape)
    inside = jnp.logical_and(~is_last, jnp.logical_or(apart == 0, apart == 4))
    taken = jnp.logical_or(inside, jnp.logical_and(is_last, source < per_device))
    target = jnp.where(
        is_last, jnp.where(mirror == 0, local, 7 + mirror), local + jnp.where(apart == 4, per_device, 0)
    )
    taken, source, target = (values.reshape(-1) for values in (taken, source, target))
    order = jnp.arange(taken.shape[0], dtype=jnp.int32)
    earlier = jnp.logical_and(order[None, :] < order[:, None], taken[None, :])
    position = jnp.sum(earlier.astype(jnp.int32), axis=1)
    slots = jnp.arange(TILE_SLOTS, dtype=jnp.int32)
    hits = jnp.logical_and(position[None, :] == slots[:, None], taken[None, :])
    count = jnp.sum(taken.astype(jnp.int32))
    sources = jnp.sum(jnp.where(hits, source[None, :], 0), axis=1)
    targets = jnp.sum(jnp.where(hits, target[None, :], 0), axis=1)
    used = slots < count
    extra = jnp.where(slots == 0, count, jnp.where(slots == 1, own_group, 0))
    scalars = jnp.stack([sources, targets, extra.astype(jnp.int32)])
    by_source, by_target = (
        jnp.broadcast_to(jnp.where(used, ids, -1)[:, None], (TILE_SLOTS, 128))
        for ids in (sources, targets)
    )
    return scalars, by_source, by_target


def shards_quad(source_vectors, target_vectors, source_mass, target_mass, candidates):
    members = lax.axis_size("member")
    groups = lax.axis_size("group")
    own_group = lax.axis_index("group")
    own_member = lax.axis_index("member")
    per_device, cand_count = candidates.shape
    block_rows = source_vectors.shape[0] // per_device
    width = source_vectors.shape[1]
    blocked = (per_device, block_rows, width)
    member_swap = lambda values, bit: swap(values, "member", members, bit)
    group_swap = lambda values, bit: swap(values, "group", groups, bit)

    source_own = source_vectors.reshape(blocked)
    target_own = target_vectors.reshape(blocked)
    source_near = member_swap(source_own, 2)
    target_far = member_swap(target_own, 4)
    note = jnp.concatenate(
        [
            LOG2E * source_mass.reshape(per_device, block_rows),
            jnp.pad(
                candidates.astype(jnp.float32).reshape(1, per_device * cand_count),
                ((0, 3), (0, block_rows - per_device * cand_count)),
            ),
        ]
    )
    notes = [note] + [member_swap(note, bit) for bit in (1, 2, 3)]
    mirrors = [
        group_swap(lax.dynamic_slice_in_dim(target_own, own_group ^ bit, 1, 0), bit) for bit in (1, 2, 3)
    ]
    source_core = member_swap(source_own, 1)
    source_cross = member_swap(source_near, 1)
    lists = jnp.stack([values[4, : per_device * cand_count] for values in notes])
    lists = lists.reshape(4 * per_device, cand_count).astype(jnp.int32)
    scalars, by_source, by_target = tile_lists(lists, own_group, own_member, members, per_device)
    own_mass = LOG2E * target_mass.reshape(per_device, block_rows)
    blocks = [source_own, source_core, source_near, source_cross, target_own, target_far, *mirrors]

    buffers = [
        VMEM((SOURCE_SLOTS, block_rows, width), source_vectors.dtype),
        VMEM((TARGET_SLOTS, block_rows, width), target_vectors.dtype),
        VMEM((TILE_SLOTS, block_rows), jnp.float32),
        VMEM((TILE_SLOTS, block_rows), jnp.float32),
        pltpu.SemaphoreType.DMA((9,)),
    ]
    source_bias_buffer = VMEM((SOURCE_SLOTS, block_rows, 128), jnp.float32)
    target_bias_buffer = VMEM((TARGET_SLOTS, block_rows, 128), jnp.float32)
    side = (16, block_rows)
    start = (SMEM, VMEM) + (pl.ANY,) * 9

    (parts,) = call(
        functools.partial(rows_kernel, True), [scalars, by_source, *blocks], start, [side], buffers
    )
    for step in range(ITERS):
        last_pass = step == ITERS - 1
        theirs = [member_swap(parts, bit) for bit in (1, 2, 3)]
        columns, *potential = call(
            functools.partial(columns_kernel, last_pass),
            [scalars, by_target, *blocks, *notes, parts, *theirs, own_mass],
            start + (VMEM,) * 9,
            [side, (8, 128)] if last_pass else [side],
            buffers + [source_bias_buffer],
        )
        partner = member_swap(columns, 4)
        if last_pass:
            break
        sent = call(
            forward_kernel,
            [scalars, columns, partner],
            (SMEM, VMEM, VMEM),
            [(4, block_rows)] * 3,
            [],
        )
        received = [group_swap(values, bit) for bit, values in enumerate(sent, 1)]
        (parts,) = call(
            functools.partial(rows_kernel, False),
            [scalars, by_source, *blocks, columns, partner, *received],
            start + (VMEM,) * 5,
            [side],
            buffers + [target_bias_buffer, VMEM((8, block_rows), jnp.float32)],
        )
    received = [group_swap(columns, bit) for bit in (1, 2, 3)]
    (final,) = call(
        finish_kernel,
        [scalars, columns, partner, *received],
        (SMEM,) + (VMEM,) * 5,
        [(8, 128)],
        [VMEM((8, block_rows), jnp.float32)],
    )
    return potential[0].reshape(source_mass.shape), final.reshape(target_mass.shape)


def shards(source_vectors, target_vectors, source_mass, target_mass, candidates):
    quad = lax.axis_size("member") == 8 and lax.axis_size("group") == 4 and candidates.shape == (4, 8)
    plan = shards_quad if quad else shards_any
    return plan(source_vectors, target_vectors, source_mass, target_mass, candidates)


def solution(mesh):
    placed = (
        P(("group", "member"), None),
        P(("group", "member"), None),
        P(("group", "member")),
        P(("group", "member")),
        P(("group", "member"), None),
    )
    return jax.shard_map(
        shards,
        mesh=mesh,
        in_specs=placed,
        out_specs=(P(("group", "member")), P(("group", "member"))),
        check_vma=False,
    )
```

```python
import functools

import jax
import jax.numpy as jnp
from jax import lax
from jax.experimental import pallas as pl
from jax.experimental.pallas import tpu as pltpu
from jax.sharding import PartitionSpec as P

ITERS = 2


entropy_strength = 0.3
very_low = -1e30


def log_partition(values, axis):
    largest_score = jnp.max(values, axis=axis, keepdims=True)
    return jnp.squeeze(largest_score, axis) + jnp.log(
        jnp.sum(jnp.exp(values - largest_score), axis=axis)
    )


def slot_layout(lists, per_device, members, capacity):
    owner = lists // per_device
    partner = owner % members
    local_block = lists % per_device
    ordering = jnp.arange(lists.shape[-1], dtype=jnp.int32)
    matching = partner[..., :, None] == partner[..., None, :]
    earlier = ordering[None, :] < ordering[:, None]
    position = jnp.sum(jnp.logical_and(matching, earlier).astype(jnp.int32), axis=-1)
    return (partner * capacity + position, local_block)


def trade_member(values):
    return lax.all_to_all(values, "member", split_axis=0, concat_axis=0, tiled=True)


def trade_group(values):
    return lax.all_to_all(values, "group", split_axis=0, concat_axis=0, tiled=True)


def tile_terms(sources, target_blocks, picks, side, by_rows):
    tile_count, block_rows, width = sources.shape
    batch = 4
    grouped = (
        sources.reshape(tile_count // batch, batch, block_rows, width),
        picks.reshape(tile_count // batch, batch),
        side.reshape(tile_count // batch, batch, block_rows),
    )

    def visit(grouped_part):
        source_portion, pick_part, side_portion = grouped_part
        key_entries = jnp.take(target_blocks, pick_part, axis=0)
        score_matrix = jnp.einsum(
            "umk,ugk->umg", source_portion, key_entries, preferred_element_type=jnp.float32
        )
        if by_rows:
            return log_partition((score_matrix + side_portion[:, None, :]) / entropy_strength, 2)
        return log_partition((score_matrix + side_portion[:, :, None]) / entropy_strength, 1)

    return lax.map(visit, grouped).reshape(tile_count, block_rows)


def owner_update(slot_terms, mirror_terms, incoming, target_marginal):
    output_list = []
    for local_block in range(target_marginal.shape[0]):
        masked = jnp.where((incoming == local_block)[:, None], slot_terms, very_low)
        stacked = jnp.concatenate([masked, mirror_terms[local_block][None, :]], axis=0)
        output_list.append(log_partition(stacked, 0))
    return entropy_strength * target_marginal - entropy_strength * jnp.stack(output_list)


def shards_any(source_vectors, target_vectors, source_mass, target_mass, candidates):
    members = lax.axis_size("member")
    groups = lax.axis_size("group")
    own_member = lax.axis_index("member")
    source_count, cand_count = candidates.shape
    inside_count = cand_count - 1
    block_rows = source_vectors.shape[0] // source_count
    width = source_vectors.shape[1]
    target_count = target_vectors.shape[0] // block_rows
    capacity = (source_count * inside_count + members - 1) // members
    spots = members * capacity
    source_blocks = source_vectors.reshape(source_count, block_rows, width)
    target_blocks = target_vectors.reshape(target_count, block_rows, width)
    source_marginal = source_mass.reshape(source_count, block_rows)
    target_marginal = target_mass.reshape(target_count, block_rows)
    own_lists = candidates[:, :inside_count]
    own_spots, own_local = slot_layout(
        own_lists.reshape(1, source_count * inside_count), target_count, members, capacity
    )
    own_spots = own_spots[0]
    all_lists = lax.all_gather(own_lists, "member", axis=0, tiled=True)
    their_spots, their_local = slot_layout(
        all_lists.reshape(members, source_count * inside_count), target_count, members, capacity
    )
    wanted_spots = own_member * capacity + jnp.arange(capacity, dtype=jnp.int32)
    hits = their_spots[:, :, None] == wanted_spots[None, None, :]
    incoming = (jnp.sum(jnp.where(hits, their_local[:, :, None] + 1, 0), axis=1) - 1).reshape(spots)
    picks = jnp.maximum(incoming, 0)
    mirror_group = candidates[:, inside_count] // target_count // members
    spot_range = jnp.arange(spots, dtype=jnp.int32)
    group_range = jnp.arange(groups, dtype=jnp.int32)
    source_of = jnp.arange(source_count * inside_count, dtype=jnp.int32) // inside_count
    slot_index = jnp.sum(
        jnp.where(own_spots[:, None] == spot_range[None, :], source_of[:, None], 0), axis=0
    )
    mirror_index = jnp.sum(
        jnp.where(
            mirror_group[:, None] == group_range[None, :],
            jnp.arange(source_count, dtype=jnp.int32)[:, None],
            0,
        ),
        axis=0,
    )
    slot_payload = jnp.take(source_blocks, slot_index, axis=0)
    mirror_payload = jnp.take(source_blocks, mirror_index, axis=0)
    arrived = lax.all_to_all(
        slot_payload.reshape(members, capacity, block_rows, width),
        "member",
        split_axis=0,
        concat_axis=0,
        tiled=True,
    ).reshape(spots, block_rows, width)
    arrived_mirror = lax.all_to_all(
        mirror_payload, "group", split_axis=0, concat_axis=0, tiled=True
    )
    target_current = jnp.zeros((target_count, block_rows), jnp.float32)
    for step in range(ITERS):
        row_slots = tile_terms(
            arrived, target_blocks, picks, jnp.take(target_current, picks, axis=0), True
        )
        row_mirror = tile_terms(arrived_mirror, target_blocks, group_range, target_current, True)
        slot_back = trade_member(row_slots.reshape(members, capacity, block_rows)).reshape(
            spots, block_rows
        )
        mirror_back = trade_group(row_mirror)
        collected_rows = jnp.concatenate(
            [
                jnp.take(slot_back, own_spots, axis=0).reshape(
                    source_count, inside_count, block_rows
                ),
                jnp.take(mirror_back, mirror_group, axis=0)[:, None],
            ],
            axis=1,
        )
        source_current = entropy_strength * source_marginal - entropy_strength * log_partition(
            collected_rows, 1
        )
        slot_sides = trade_member(
            jnp.take(source_current, slot_index, axis=0).reshape(members, capacity, block_rows)
        ).reshape(spots, block_rows)
        mirror_sides = trade_group(jnp.take(source_current, mirror_index, axis=0))
        column_slots = tile_terms(arrived, target_blocks, picks, slot_sides, False)
        column_mirror = tile_terms(arrived_mirror, target_blocks, group_range, mirror_sides, False)
        target_current = owner_update(column_slots, column_mirror, incoming, target_marginal)
    return (
        source_current.reshape(source_count * block_rows),
        target_current.reshape(target_count * block_rows),
    )


LOG2E = 1.4426950408889634
TO_LOGIT = LOG2E / entropy_strength
TO_POTENTIAL = entropy_strength / LOG2E
CAPACITY = 4
SOURCE_SLOTS = 16
TARGET_SLOTS = 12
FAR = 8
SECTIONS = ((0, 12), (12, 8), (20, 8), (28, 8))
TILE_SLOTS = 40
SMALL, LARGE = 2.0**-100, 2.0**100


def merge(parts):
    top = functools.reduce(jnp.maximum, parts)
    return top + LOG2E * jnp.log(sum(jnp.exp2(part - top) for part in parts))


def swapped(rows, size):
    pieces = [rows[start : start + size] for start in range(0, rows.shape[0], size)]
    return jnp.concatenate([pieces[index ^ 1] for index in range(len(pieces))], axis=0)


def source_bias(note_refs, part_refs):
    own, core, near, cross = (ref[...] for ref in part_refs)
    core = swapped(core, 4)
    near = swapped(near, 8)
    cross = swapped(swapped(cross, 4), 8)
    mass = jnp.concatenate([ref[0:4] for ref in note_refs], axis=0)
    return mass - merge([own, core, near, cross])


def target_bias(scalars, columns, partner, mirrors, scratch):
    group = scalars[4, 0]
    scratch[...] = jnp.full(scratch.shape, very_low, jnp.float32)
    for offset, ref in enumerate(mirrors, 1):
        scratch[pl.ds(group ^ offset, 1), :] = ref[0:1]
        scratch[pl.ds(4 + (group ^ offset), 1), :] = ref[1:2]
    own = columns[12:16] - merge([columns[0:4], partner[8:12], scratch[0:4]])
    far = partner[12:16] - merge([columns[8:12], partner[0:4], scratch[4:8]])
    across = [
        ref[3:4] - merge([ref[2:3], columns[3 + offset : 4 + offset]])
        for offset, ref in enumerate(mirrors, 1)
    ]
    blank = jnp.zeros((1, own.shape[1]), jnp.float32)
    return jnp.concatenate([own, *across, blank, far, *([blank] * 4)], axis=0)


def spread(rows, bias):
    high = rows.astype(jnp.bfloat16)
    rest = rows - high.astype(jnp.float32)
    middle = rest.astype(jnp.bfloat16)
    low = (rest - middle.astype(jnp.float32)).astype(jnp.bfloat16)
    parts = jnp.concatenate([high, middle, low], axis=0)
    count = rows.shape[0]
    shape = (3 * count, count * 128)
    slot = lax.broadcasted_iota(jnp.int32, shape, 0) & (count - 1)
    place = lax.broadcasted_iota(jnp.int32, shape, 1) >> 7
    chosen = jnp.where(slot == place, 1.0, 0.0).astype(jnp.bfloat16)
    turned = lax.dot_general(
        parts, chosen, (((0,), (0,)), ((), ())), preferred_element_type=jnp.float32
    )
    for index in range(bias.shape[0]):
        bias[index] = turned[:, 128 * index : 128 * (index + 1)]


def score(summed, kept):
    product = lax.dot_general(summed, kept, (((1,), (1,)), ((), ())), preferred_element_type=jnp.float32)
    return product * TO_LOGIT


def wide(values):
    return jnp.concatenate([values, values], axis=1)


def sides(section, by_rows, sources, targets):
    late_source, late_target = section in (1, 3), section in (2, 3)
    source = (sources[late_source], 0, 8 if late_source else 0)
    target = (targets[late_target], 1, FAR if late_target else 0)
    return (target, source) if by_rows else (source, target)


def exact_pass(scalars, ids, by_rows, sections, sources, targets, bias, tops, sums, unrolled):
    for section in sections:
        first, count = SECTIONS[section]
        (summed, summed_row, summed_base), (kept, kept_row, _) = sides(section, by_rows, sources, targets)

        def visit(slot, carry=0):
            block = scalars[summed_row, slot]
            logits = score(summed[block], kept[scalars[kept_row, slot]])
            if bias is not None:
                logits = logits + wide(bias[summed_base + block])
            top = jnp.max(logits, axis=0, keepdims=True)
            tops[pl.ds(slot, 1), :] = top
            sums[pl.ds(slot, 1), :] = jnp.sum(jnp.exp2(logits - top), axis=0, keepdims=True)
            return carry

        if unrolled:
            for slot in range(first, first + count):
                visit(slot)
        else:
            lax.fori_loop(first, first + count, visit, 0)
    first, last = SECTIONS[sections[0]][0], sum(SECTIONS[sections[-1]])
    low, high = first // 8 * 8, (last + 7) // 8 * 8
    id_rows = wide(ids[low:high])
    if low < first or last < high:
        slot = low + lax.broadcasted_iota(jnp.int32, id_rows.shape, 0)
        id_rows = jnp.where(jnp.logical_and(slot >= first, slot < last), id_rows, -1)
    top_rows, sum_rows = tops[low:high], sums[low:high]
    best, total = [], []
    for block in range(SOURCE_SLOTS if by_rows else TARGET_SLOTS):
        mine = id_rows == block
        top = jnp.max(jnp.where(mine, top_rows, very_low), axis=0, keepdims=True)
        best.append(top)
        total.append(
            jnp.sum(jnp.where(mine, sum_rows * jnp.exp2(top_rows - top), 0.0), axis=0, keepdims=True)
        )
    best = jnp.concatenate(best, axis=0)
    total = jnp.concatenate(total, axis=0)
    return jnp.where(total > 0, best + LOG2E * jnp.log(jnp.where(total > 0, total, 1.0)), very_low)


def fast_pass(scalars, ids, present, by_rows, sources, targets, bias, reference, total, tops, sums, out):
    total[...] = jnp.zeros(total.shape, jnp.float32)
    for section, (first, count) in enumerate(SECTIONS):
        (summed, summed_row, summed_base), (kept, kept_row, kept_base) = sides(
            section, by_rows, sources, targets
        )
        for slot in range(first, first + count):
            block, partner = scalars[summed_row, slot], scalars[kept_row, slot]
            logits = score(summed[block], kept[partner]) + wide(bias[summed_base + block])
            if reference is not None:
                logits = logits + reference[pl.ds(kept_base + partner, 1), :]
            terms = jnp.exp2(logits)
            place = scalars[2 + kept_row, slot]
            total[place] = total[place] + jnp.sum(terms.reshape(-1, 8, terms.shape[1]), axis=0)
    count = SOURCE_SLOTS if by_rows else TARGET_SLOTS
    sums_of = jnp.concatenate(
        [jnp.sum(total[block], axis=0, keepdims=True) for block in range(count)], axis=0
    )
    here = wide(present[0:count]) > 0
    result = LOG2E * jnp.log(jnp.where(here, sums_of, 1.0))
    if reference is not None:
        result = result - reference[0:count]
    out[0:count, :] = jnp.where(here, result, very_low)
    fine = jnp.logical_and(sums_of > SMALL, sums_of < LARGE)
    worst = jnp.min(jnp.where(jnp.logical_or(fine, jnp.logical_not(here)), 1.0, 0.0))

    @pl.when(worst < 0.5)
    def _():
        out[0:count, :] = exact_pass(
            scalars, ids, by_rows, (0, 1, 2, 3), sources, targets, bias, tops, sums, False
        )


def early_kernel(
    scalars, ids, own, core, target, mirror_1, mirror_2, mirror_3, out, sources, targets, tops, sums
):
    sources[0:4] = own[...]
    sources[4:8] = core[...]
    targets[0:4] = target[...]
    for index, mirror in enumerate((mirror_1, mirror_2, mirror_3)):
        targets[4 + index : 5 + index] = mirror[...]
    out[...] = exact_pass(
        scalars, ids, True, (0,), (sources, None), (targets, None), None, tops, sums, True
    )


def first_kernel(
    scalars, ids, early, sources, near, cross, targets, far, out, late_sources, tops, sums
):
    late_sources[0:4] = near[...]
    late_sources[4:8] = cross[...]
    late = exact_pass(
        scalars, ids, True, (1, 2, 3), (sources, late_sources), (targets, far), None, tops, sums, True
    )
    out[...] = merge([early[...], late])


def columns_kernel(last_pass, *refs):
    scalars, ids, present = refs[:3]
    sources, targets = refs[3:5], refs[5:7]
    notes, parts, target_mass = refs[7:11], refs[11:15], refs[15]
    rest = refs[16:]
    reference = None
    if last_pass:
        reference, *rest = rest
    out, second, total, tops, sums, bias = rest
    rows = source_bias(notes, parts)
    spread(rows, bias)
    if last_pass:
        for block in range(4):
            for half in range(2):
                second[2 * block + half : 2 * block + half + 1, :] = (
                    TO_POTENTIAL * rows[block : block + 1, 128 * half : 128 * (half + 1)]
                )
    else:
        second[...] = rows
    fast_pass(
        scalars, ids, present, False, sources, targets, bias, reference, total, tops, sums, out
    )
    out[12:16, :] = target_mass[0:4]


def rows_kernel(*refs):
    scalars, ids, present = refs[:3]
    sources, targets = refs[3:5], refs[5:7]
    reference, columns, partner, *mirrors = refs[7:13]
    out, second, total, tops, sums, bias, scratch = refs[13:]
    rows = target_bias(scalars, columns, partner, mirrors, scratch)
    spread(rows, bias)
    second[...] = rows
    fast_pass(
        scalars, ids, present, True, sources, targets, bias, reference, total, tops, sums, out
    )


def forward_kernel(scalars, columns, partner, *outs):
    group = scalars[4, 0]
    for offset, out in enumerate(outs, 1):
        block = group ^ offset
        out[0:1, :] = columns[3 + offset : 4 + offset]
        out[1:2, :] = partner[3 + offset : 4 + offset]
        out[2:3, :] = merge([columns[pl.ds(block, 1), :], partner[pl.ds(FAR + block, 1), :]])
        out[3:4, :] = columns[pl.ds(12 + block, 1), :]


def finish_kernel(scalars, columns, partner, *rest):
    *mirrors, out, scratch = rest
    group = scalars[4, 0]
    scratch[...] = jnp.full(scratch.shape, very_low, jnp.float32)
    for offset, ref in enumerate(mirrors, 1):
        scratch[pl.ds(group ^ offset, 1), :] = ref[3 + offset : 4 + offset]
    rows = columns[12:16] - merge([columns[0:4], partner[8:12], scratch[0:4]])
    for block in range(4):
        for half in range(2):
            out[2 * block + half : 2 * block + half + 1, :] = (
                TO_POTENTIAL * rows[block : block + 1, 128 * half : 128 * (half + 1)]
            )


SMEM, VMEM = pltpu.SMEM, pltpu.VMEM


def call(kernel, inputs, outs, scratch=()):
    whole = pl.BlockSpec(memory_space=VMEM)
    return pl.pallas_call(
        kernel,
        out_shape=outs,
        in_specs=[pl.BlockSpec(memory_space=SMEM)] + [whole] * (len(inputs) - 1),
        out_specs=[whole] * len(outs),
        scratch_shapes=list(scratch),
        compiler_params=pltpu.CompilerParams(vmem_limit_bytes=32 << 20),
    )(*inputs)


def swap(values, axis, size, bit):
    return lax.ppermute(values, axis, [(index, index ^ bit) for index in range(size)])


def tile_lists(candidates, own_group, own_member, members, per_device):
    owner = candidates // per_device
    local = candidates % per_device
    apart = (owner % members) ^ own_member
    last = candidates.shape[1] - 1
    mirror = (owner // members) ^ own_group
    is_last = jnp.arange(last + 1)[None, :] == last
    source = jnp.broadcast_to(jnp.arange(SOURCE_SLOTS, dtype=jnp.int32)[:, None], candidates.shape)
    own_mirror = jnp.logical_and(is_last, source < per_device)
    near = jnp.logical_and(~is_last, apart == 0)
    far = jnp.logical_and(~is_last, apart == 4)
    late = source >= 2 * per_device
    target = jnp.where(jnp.logical_and(is_last, mirror > 0), 3 + mirror, local)
    members_of = (
        jnp.logical_or(jnp.logical_and(near, ~late), own_mirror),
        jnp.logical_and(near, late),
        jnp.logical_and(far, ~late),
        jnp.logical_and(far, late),
    )
    source, target = source.reshape(1, -1), target.reshape(1, -1)
    order = jnp.arange(source.shape[1], dtype=jnp.int32)
    before = order[None, :] < order[:, None]
    place = jnp.full(order.shape, -1, jnp.int32)
    for (first, _), taken in zip(SECTIONS, members_of):
        taken = taken.reshape(-1)
        earlier = jnp.sum(jnp.logical_and(before, taken[None, :]).astype(jnp.int32), axis=1)
        place = jnp.where(taken, first + earlier, place)
    slots = jnp.arange(TILE_SLOTS, dtype=jnp.int32)
    hits = place[None, :] == slots[:, None]
    used = jnp.any(hits, axis=1)
    sources = jnp.sum(jnp.where(hits, source, 0), axis=1)
    targets = jnp.sum(jnp.where(hits, target, 0), axis=1)
    late_slot = jnp.logical_or(jnp.logical_and(slots >= 12, slots < 20), slots >= 28)
    source_ids = jnp.where(used, sources, -1)
    target_ids = jnp.where(used, jnp.where(slots >= 20, FAR + targets, targets), -1)
    scalars = jnp.stack(
        [
            jnp.where(jnp.logical_and(late_slot, used), sources - 8, sources),
            targets,
            jnp.where(used, source_ids, SOURCE_SLOTS),
            jnp.where(used, target_ids, TARGET_SLOTS),
            jnp.broadcast_to(own_group, slots.shape).astype(jnp.int32),
        ]
    )
    lists = []
    for ids in (source_ids, target_ids):
        rows = jnp.any(ids[None, :] == jnp.arange(16)[:, None], axis=1).astype(jnp.float32)
        lists.append(jnp.broadcast_to(ids[:, None], (TILE_SLOTS, 128)))
        lists.append(jnp.broadcast_to(rows[:, None], (16, 128)))
    return scalars, *lists


def shards_quad(source_vectors, target_vectors, source_mass, target_mass, candidates):
    members = lax.axis_size("member")
    groups = lax.axis_size("group")
    own_group = lax.axis_index("group")
    own_member = lax.axis_index("member")
    per_device, cand_count = candidates.shape
    block_rows = source_vectors.shape[0] // per_device
    width = source_vectors.shape[1]
    blocked = (per_device, block_rows, width)
    member_swap = lambda values, bit: swap(values, "member", members, bit)
    group_swap = lambda values, bit: swap(values, "group", groups, bit)

    source_own = source_vectors.reshape(blocked)
    target_own = target_vectors.reshape(blocked)
    target_far = member_swap(target_own, 4)
    source_near = member_swap(source_own, 2)
    source_core = member_swap(source_own, 1)
    source_cross = member_swap(source_near, 1)
    source_mass_late, candidates_late, target_late, _ = lax.optimization_barrier(
        (source_mass, candidates, target_own, source_core)
    )
    note = jnp.concatenate(
        [
            LOG2E * source_mass_late.reshape(per_device, block_rows),
            jnp.pad(
                candidates_late.astype(jnp.float32).reshape(1, per_device * cand_count),
                ((0, 3), (0, block_rows - per_device * cand_count)),
            ),
        ]
    )
    notes = [note] + [member_swap(note, bit) for bit in (1, 2, 3)]
    mirrors = [
        group_swap(lax.dynamic_slice_in_dim(target_late, own_group ^ bit, 1, 0), bit) for bit in (1, 2, 3)
    ]
    named = jnp.stack([values[4, : per_device * cand_count] for values in notes])
    named = named.reshape(SOURCE_SLOTS, cand_count).astype(jnp.int32)
    scalars, by_source, has_source, by_target, has_target = tile_lists(
        named, own_group, own_member, members, per_device
    )
    own_mass = LOG2E * target_mass.reshape(per_device, block_rows)

    side = jax.ShapeDtypeStruct((16, block_rows), jnp.float32)
    flat = jax.ShapeDtypeStruct((8, 128), jnp.float32)
    stacked = lambda count: jax.ShapeDtypeStruct((count, block_rows, width), source_vectors.dtype)
    tile_rows = [VMEM((TILE_SLOTS, block_rows), jnp.float32)] * 2
    pass_buffers = [
        VMEM((SOURCE_SLOTS + 1, 8, block_rows), jnp.float32),
        *tile_rows,
        VMEM((SOURCE_SLOTS, block_rows, 128), jnp.float32),
    ]

    early, sources, targets = call(
        early_kernel,
        [scalars, by_source, source_own, source_core, target_own, *mirrors],
        [side, stacked(8), stacked(7)],
        tile_rows,
    )
    parts, late_sources = call(
        first_kernel,
        [scalars, by_source, early, sources, source_near, source_cross, targets, target_far],
        [side, stacked(8)],
        tile_rows,
    )
    blocks = [sources, late_sources, targets, target_far]
    reference = []
    for step in range(ITERS):
        last_pass = step == ITERS - 1
        theirs = [member_swap(parts, bit) for bit in (1, 2, 3)]
        columns, potential = call(
            functools.partial(columns_kernel, last_pass),
            [scalars, by_target, has_target, *blocks, *notes, parts, *theirs, own_mass, *reference],
            [side, flat if last_pass else side],
            pass_buffers,
        )
        partner = member_swap(columns, 4)
        if last_pass:
            break
        sent = call(
            forward_kernel,
            [scalars, columns, partner],
            [jax.ShapeDtypeStruct((4, block_rows), jnp.float32)] * 3,
        )
        received = [group_swap(values, bit) for bit, values in enumerate(sent, 1)]
        parts, target_rows = call(
            rows_kernel,
            [scalars, by_source, has_source, *blocks, potential, columns, partner, *received],
            [side, side],
            [*pass_buffers, VMEM((8, block_rows), jnp.float32)],
        )
        reference = [target_rows]
    received = [group_swap(columns, bit) for bit in (1, 2, 3)]
    (final,) = call(
        finish_kernel,
        [scalars, columns, partner, *received],
        [flat],
        [VMEM((8, block_rows), jnp.float32)],
    )
    return potential.reshape(source_mass.shape), final.reshape(target_mass.shape)


def shards(source_vectors, target_vectors, source_mass, target_mass, candidates):
    quad = lax.axis_size("member") == 8 and lax.axis_size("group") == 4 and candidates.shape == (4, 8)
    plan = shards_quad if quad else shards_any
    return plan(source_vectors, target_vectors, source_mass, target_mass, candidates)


def solution(mesh):
    placed = (
        P(("group", "member"), None),
        P(("group", "member"), None),
        P(("group", "member")),
        P(("group", "member")),
        P(("group", "member"), None),
    )
    return jax.shard_map(
        shards,
        mesh=mesh,
        in_specs=placed,
        out_specs=(P(("group", "member")), P(("group", "member"))),
        check_vma=False,
    )
```

```python
import functools

import jax
import jax.numpy as jnp
from jax import lax
from jax.experimental import pallas as pl
from jax.experimental.pallas import tpu as pltpu
from jax.sharding import PartitionSpec as P

ITERS = 2


entropy_strength = 0.3
very_low = -1e30


def log_partition(values, axis):
    largest_score = jnp.max(values, axis=axis, keepdims=True)
    return jnp.squeeze(largest_score, axis) + jnp.log(
        jnp.sum(jnp.exp(values - largest_score), axis=axis)
    )


def slot_layout(lists, per_device, members, capacity):
    owner = lists // per_device
    partner = owner % members
    local_block = lists % per_device
    ordering = jnp.arange(lists.shape[-1], dtype=jnp.int32)
    matching = partner[..., :, None] == partner[..., None, :]
    earlier = ordering[None, :] < ordering[:, None]
    position = jnp.sum(jnp.logical_and(matching, earlier).astype(jnp.int32), axis=-1)
    return (partner * capacity + position, local_block)


def trade_member(values):
    return lax.all_to_all(values, "member", split_axis=0, concat_axis=0, tiled=True)


def trade_group(values):
    return lax.all_to_all(values, "group", split_axis=0, concat_axis=0, tiled=True)


def tile_terms(sources, target_blocks, picks, side, by_rows):
    tile_count, block_rows, width = sources.shape
    batch = 4
    grouped = (
        sources.reshape(tile_count // batch, batch, block_rows, width),
        picks.reshape(tile_count // batch, batch),
        side.reshape(tile_count // batch, batch, block_rows),
    )

    def visit(grouped_part):
        source_portion, pick_part, side_portion = grouped_part
        key_entries = jnp.take(target_blocks, pick_part, axis=0)
        score_matrix = jnp.einsum(
            "umk,ugk->umg", source_portion, key_entries, preferred_element_type=jnp.float32
        )
        if by_rows:
            return log_partition((score_matrix + side_portion[:, None, :]) / entropy_strength, 2)
        return log_partition((score_matrix + side_portion[:, :, None]) / entropy_strength, 1)

    return lax.map(visit, grouped).reshape(tile_count, block_rows)


def owner_update(slot_terms, mirror_terms, incoming, target_marginal):
    output_list = []
    for local_block in range(target_marginal.shape[0]):
        masked = jnp.where((incoming == local_block)[:, None], slot_terms, very_low)
        stacked = jnp.concatenate([masked, mirror_terms[local_block][None, :]], axis=0)
        output_list.append(log_partition(stacked, 0))
    return entropy_strength * target_marginal - entropy_strength * jnp.stack(output_list)


def shards_any(source_vectors, target_vectors, source_mass, target_mass, candidates):
    members = lax.axis_size("member")
    groups = lax.axis_size("group")
    own_member = lax.axis_index("member")
    source_count, cand_count = candidates.shape
    inside_count = cand_count - 1
    block_rows = source_vectors.shape[0] // source_count
    width = source_vectors.shape[1]
    target_count = target_vectors.shape[0] // block_rows
    capacity = (source_count * inside_count + members - 1) // members
    spots = members * capacity
    source_blocks = source_vectors.reshape(source_count, block_rows, width)
    target_blocks = target_vectors.reshape(target_count, block_rows, width)
    source_marginal = source_mass.reshape(source_count, block_rows)
    target_marginal = target_mass.reshape(target_count, block_rows)
    own_lists = candidates[:, :inside_count]
    own_spots, own_local = slot_layout(
        own_lists.reshape(1, source_count * inside_count), target_count, members, capacity
    )
    own_spots = own_spots[0]
    all_lists = lax.all_gather(own_lists, "member", axis=0, tiled=True)
    their_spots, their_local = slot_layout(
        all_lists.reshape(members, source_count * inside_count), target_count, members, capacity
    )
    wanted_spots = own_member * capacity + jnp.arange(capacity, dtype=jnp.int32)
    hits = their_spots[:, :, None] == wanted_spots[None, None, :]
    incoming = (jnp.sum(jnp.where(hits, their_local[:, :, None] + 1, 0), axis=1) - 1).reshape(spots)
    picks = jnp.maximum(incoming, 0)
    mirror_group = candidates[:, inside_count] // target_count // members
    spot_range = jnp.arange(spots, dtype=jnp.int32)
    group_range = jnp.arange(groups, dtype=jnp.int32)
    source_of = jnp.arange(source_count * inside_count, dtype=jnp.int32) // inside_count
    slot_index = jnp.sum(
        jnp.where(own_spots[:, None] == spot_range[None, :], source_of[:, None], 0), axis=0
    )
    mirror_index = jnp.sum(
        jnp.where(
            mirror_group[:, None] == group_range[None, :],
            jnp.arange(source_count, dtype=jnp.int32)[:, None],
            0,
        ),
        axis=0,
    )
    slot_payload = jnp.take(source_blocks, slot_index, axis=0)
    mirror_payload = jnp.take(source_blocks, mirror_index, axis=0)
    arrived = lax.all_to_all(
        slot_payload.reshape(members, capacity, block_rows, width),
        "member",
        split_axis=0,
        concat_axis=0,
        tiled=True,
    ).reshape(spots, block_rows, width)
    arrived_mirror = lax.all_to_all(
        mirror_payload, "group", split_axis=0, concat_axis=0, tiled=True
    )
    target_current = jnp.zeros((target_count, block_rows), jnp.float32)
    for step in range(ITERS):
        row_slots = tile_terms(
            arrived, target_blocks, picks, jnp.take(target_current, picks, axis=0), True
        )
        row_mirror = tile_terms(arrived_mirror, target_blocks, group_range, target_current, True)
        slot_back = trade_member(row_slots.reshape(members, capacity, block_rows)).reshape(
            spots, block_rows
        )
        mirror_back = trade_group(row_mirror)
        collected_rows = jnp.concatenate(
            [
                jnp.take(slot_back, own_spots, axis=0).reshape(
                    source_count, inside_count, block_rows
                ),
                jnp.take(mirror_back, mirror_group, axis=0)[:, None],
            ],
            axis=1,
        )
        source_current = entropy_strength * source_marginal - entropy_strength * log_partition(
            collected_rows, 1
        )
        slot_sides = trade_member(
            jnp.take(source_current, slot_index, axis=0).reshape(members, capacity, block_rows)
        ).reshape(spots, block_rows)
        mirror_sides = trade_group(jnp.take(source_current, mirror_index, axis=0))
        column_slots = tile_terms(arrived, target_blocks, picks, slot_sides, False)
        column_mirror = tile_terms(arrived_mirror, target_blocks, group_range, mirror_sides, False)
        target_current = owner_update(column_slots, column_mirror, incoming, target_marginal)
    return (
        source_current.reshape(source_count * block_rows),
        target_current.reshape(target_count * block_rows),
    )


LOG2E = 1.4426950408889634
TO_LOGIT = LOG2E / entropy_strength
TO_POTENTIAL = entropy_strength / LOG2E
CAPACITY = 4
SOURCE_SLOTS = 16
TARGET_SLOTS = 12
FAR = 8
SECTIONS = ((0, 12), (12, 8), (20, 8), (28, 8))
TILE_SLOTS = 40
SMALL, LARGE = 2.0**-100, 2.0**100


def merge(parts):
    top = functools.reduce(jnp.maximum, parts)
    return top + LOG2E * jnp.log(sum(jnp.exp2(part - top) for part in parts))


def swapped(rows, size):
    pieces = [rows[start : start + size] for start in range(0, rows.shape[0], size)]
    return jnp.concatenate([pieces[index ^ 1] for index in range(len(pieces))], axis=0)


def source_bias(mass_refs, part_refs):
    own, core, near, cross = (ref[0:16] for ref in part_refs)
    core = swapped(core, 4)
    near = swapped(near, 8)
    cross = swapped(swapped(cross, 4), 8)
    mass = jnp.concatenate([ref[16:20] for ref in mass_refs], axis=0)
    return mass - merge([own, core, near, cross])


def target_bias(scalars, columns, partner, mirrors, scratch):
    group = scalars[4, 0]
    scratch[...] = jnp.full(scratch.shape, very_low, jnp.float32)
    for offset, ref in enumerate(mirrors, 1):
        scratch[pl.ds(group ^ offset, 1), :] = ref[0:1]
        scratch[pl.ds(4 + (group ^ offset), 1), :] = ref[1:2]
    own = columns[12:16] - merge([columns[0:4], partner[8:12], scratch[0:4]])
    far = partner[12:16] - merge([columns[8:12], partner[0:4], scratch[4:8]])
    across = [
        ref[3:4] - merge([ref[2:3], columns[3 + offset : 4 + offset]])
        for offset, ref in enumerate(mirrors, 1)
    ]
    blank = jnp.zeros((1, own.shape[1]), jnp.float32)
    return jnp.concatenate([own, *across, blank, far, *([blank] * 4)], axis=0)


def spread(rows, bias):
    high = rows.astype(jnp.bfloat16)
    rest = rows - high.astype(jnp.float32)
    middle = rest.astype(jnp.bfloat16)
    low = (rest - middle.astype(jnp.float32)).astype(jnp.bfloat16)
    parts = jnp.concatenate([high, middle, low], axis=0)
    count = rows.shape[0]
    shape = (3 * count, count * 128)
    slot = lax.broadcasted_iota(jnp.int32, shape, 0) & (count - 1)
    place = lax.broadcasted_iota(jnp.int32, shape, 1) >> 7
    chosen = jnp.where(slot == place, 1.0, 0.0).astype(jnp.bfloat16)
    turned = lax.dot_general(
        parts, chosen, (((0,), (0,)), ((), ())), preferred_element_type=jnp.float32
    )
    for index in range(bias.shape[0]):
        bias[index] = turned[:, 128 * index : 128 * (index + 1)]


def score(summed, kept):
    product = lax.dot_general(summed, kept, (((1,), (1,)), ((), ())), preferred_element_type=jnp.float32)
    return product * TO_LOGIT


def wide(values):
    return jnp.concatenate([values, values], axis=1)


def sides(section, by_rows, sources, targets):
    late_source, late_target = section in (1, 3), section in (2, 3)
    source = (sources[late_source], 0, 8 if late_source else 0)
    target = (targets[late_target], 1, FAR if late_target else 0)
    return (target, source) if by_rows else (source, target)


def exact_pass(scalars, ids, by_rows, sections, sources, targets, bias, tops, sums, unrolled):
    for section in sections:
        first, count = SECTIONS[section]
        (summed, summed_row, summed_base), (kept, kept_row, _) = sides(section, by_rows, sources, targets)

        def visit(slot, carry=0):
            block = scalars[summed_row, slot]
            logits = score(summed[block], kept[scalars[kept_row, slot]])
            if bias is not None:
                logits = logits + wide(bias[summed_base + block])
            top = jnp.max(logits, axis=0, keepdims=True)
            tops[pl.ds(slot, 1), :] = top
            sums[pl.ds(slot, 1), :] = jnp.sum(jnp.exp2(logits - top), axis=0, keepdims=True)
            return carry

        if unrolled:
            for slot in range(first, first + count):
                visit(slot)
        else:
            lax.fori_loop(first, first + count, visit, 0)
    first, last = SECTIONS[sections[0]][0], sum(SECTIONS[sections[-1]])
    low, high = first // 8 * 8, (last + 7) // 8 * 8
    id_rows = wide(ids[low:high])
    if low < first or last < high:
        slot = low + lax.broadcasted_iota(jnp.int32, id_rows.shape, 0)
        id_rows = jnp.where(jnp.logical_and(slot >= first, slot < last), id_rows, -1)
    top_rows, sum_rows = tops[low:high], sums[low:high]
    best, total = [], []
    for block in range(SOURCE_SLOTS if by_rows else TARGET_SLOTS):
        mine = id_rows == block
        top = jnp.max(jnp.where(mine, top_rows, very_low), axis=0, keepdims=True)
        best.append(top)
        total.append(
            jnp.sum(jnp.where(mine, sum_rows * jnp.exp2(top_rows - top), 0.0), axis=0, keepdims=True)
        )
    best = jnp.concatenate(best, axis=0)
    total = jnp.concatenate(total, axis=0)
    return jnp.where(total > 0, best + LOG2E * jnp.log(jnp.where(total > 0, total, 1.0)), very_low)


def fast_pass(scalars, ids, present, by_rows, sources, targets, bias, reference, total, tops, sums, out):
    total[...] = jnp.zeros(total.shape, jnp.float32)
    for section, (first, count) in enumerate(SECTIONS):
        (summed, summed_row, summed_base), (kept, kept_row, kept_base) = sides(
            section, by_rows, sources, targets
        )
        for slot in range(first, first + count):
            block, partner = scalars[summed_row, slot], scalars[kept_row, slot]
            logits = score(summed[block], kept[partner]) + wide(bias[summed_base + block])
            if reference is not None:
                logits = logits + reference[pl.ds(kept_base + partner, 1), :]
            terms = jnp.exp2(logits)
            place = scalars[2 + kept_row, slot]
            total[place] = total[place] + jnp.sum(terms.reshape(-1, 8, terms.shape[1]), axis=0)
    count = SOURCE_SLOTS if by_rows else TARGET_SLOTS
    sums_of = jnp.concatenate(
        [jnp.sum(total[block], axis=0, keepdims=True) for block in range(count)], axis=0
    )
    here = wide(present[0:count]) > 0
    result = LOG2E * jnp.log(jnp.where(here, sums_of, 1.0))
    if reference is not None:
        result = result - reference[0:count]
    out[0:count, :] = jnp.where(here, result, very_low)
    fine = jnp.logical_and(sums_of > SMALL, sums_of < LARGE)
    worst = jnp.min(jnp.where(jnp.logical_or(fine, jnp.logical_not(here)), 1.0, 0.0))

    @pl.when(worst < 0.5)
    def _():
        out[0:count, :] = exact_pass(
            scalars, ids, by_rows, (0, 1, 2, 3), sources, targets, bias, tops, sums, False
        )


def early_kernel(scalars, ids, own, core, target, mirrors, out, sources, targets, tops, sums):
    sources[0:4] = own[...]
    sources[4:8] = core[...]
    targets[0:4] = target[...]
    for offset in (1, 2, 3):
        targets[3 + offset] = mirrors[scalars[4, 0] ^ offset]
    out[...] = exact_pass(
        scalars, ids, True, (0,), (sources, None), (targets, None), None, tops, sums, True
    )


def first_kernel(
    scalars, ids, early, mass, sources, near, cross, targets, far, out, late_sources, tops, sums
):
    late_sources[0:4] = near[...]
    late_sources[4:8] = cross[...]
    late = exact_pass(
        scalars, ids, True, (1, 2, 3), (sources, late_sources), (targets, far), None, tops, sums, True
    )
    out[0:16, :] = merge([early[...], late])
    out[16:20, :] = mass[...]
    out[20:24, :] = jnp.zeros((4, out.shape[1]), jnp.float32)


def columns_kernel(last_pass, *refs):
    scalars, ids, present = refs[:3]
    sources, targets = refs[3:5], refs[5:7]
    masses, target_mass, rest = refs[7:11], refs[11], refs[12:]
    parts, reference = masses, None
    if last_pass:
        parts, (reference, *rest) = rest[:4], rest[4:]
    out, second, total, tops, sums, bias = rest
    rows = source_bias(masses, parts)
    spread(rows, bias)
    if last_pass:
        for block in range(4):
            for half in range(2):
                second[2 * block + half : 2 * block + half + 1, :] = (
                    TO_POTENTIAL * rows[block : block + 1, 128 * half : 128 * (half + 1)]
                )
    else:
        second[...] = rows
    fast_pass(
        scalars, ids, present, False, sources, targets, bias, reference, total, tops, sums, out
    )
    out[12:16, :] = target_mass[0:4]


def rows_kernel(*refs):
    scalars, ids, present = refs[:3]
    sources, targets = refs[3:5], refs[5:7]
    reference, columns, partner, *mirrors = refs[7:13]
    out, second, total, tops, sums, bias, scratch = refs[13:]
    rows = target_bias(scalars, columns, partner, mirrors, scratch)
    spread(rows, bias)
    second[...] = rows
    fast_pass(
        scalars, ids, present, True, sources, targets, bias, reference, total, tops, sums, out
    )


def forward_kernel(scalars, columns, partner, *outs):
    group = scalars[4, 0]
    for offset, out in enumerate(outs, 1):
        block = group ^ offset
        out[0:1, :] = columns[3 + offset : 4 + offset]
        out[1:2, :] = partner[3 + offset : 4 + offset]
        out[2:3, :] = merge([columns[pl.ds(block, 1), :], partner[pl.ds(FAR + block, 1), :]])
        out[3:4, :] = columns[pl.ds(12 + block, 1), :]


def finish_kernel(scalars, columns, partner, *rest):
    *mirrors, out, scratch = rest
    group = scalars[4, 0]
    scratch[...] = jnp.full(scratch.shape, very_low, jnp.float32)
    for offset, ref in enumerate(mirrors, 1):
        scratch[pl.ds(group ^ offset, 1), :] = ref[3 + offset : 4 + offset]
    rows = columns[12:16] - merge([columns[0:4], partner[8:12], scratch[0:4]])
    for block in range(4):
        for half in range(2):
            out[2 * block + half : 2 * block + half + 1, :] = (
                TO_POTENTIAL * rows[block : block + 1, 128 * half : 128 * (half + 1)]
            )


SMEM, VMEM = pltpu.SMEM, pltpu.VMEM


def call(kernel, inputs, outs, scratch=()):
    whole = pl.BlockSpec(memory_space=VMEM)
    return pl.pallas_call(
        kernel,
        out_shape=outs,
        in_specs=[pl.BlockSpec(memory_space=SMEM)] + [whole] * (len(inputs) - 1),
        out_specs=[whole] * len(outs),
        scratch_shapes=list(scratch),
        compiler_params=pltpu.CompilerParams(vmem_limit_bytes=32 << 20),
    )(*inputs)


def swap(values, axis, size, bit):
    return lax.ppermute(values, axis, [(index, index ^ bit) for index in range(size)])


def tile_lists(candidates, own_group, own_member, members, per_device):
    owner = candidates // per_device
    local = candidates % per_device
    apart = (owner % members) ^ own_member
    last = candidates.shape[1] - 1
    mirror = (owner // members) ^ own_group
    is_last = jnp.arange(last + 1)[None, :] == last
    source = jnp.broadcast_to(jnp.arange(SOURCE_SLOTS, dtype=jnp.int32)[:, None], candidates.shape)
    own_mirror = jnp.logical_and(is_last, source < per_device)
    near = jnp.logical_and(~is_last, apart == 0)
    far = jnp.logical_and(~is_last, apart == 4)
    late = source >= 2 * per_device
    target = jnp.where(jnp.logical_and(is_last, mirror > 0), 3 + mirror, local)
    members_of = (
        jnp.logical_or(jnp.logical_and(near, ~late), own_mirror),
        jnp.logical_and(near, late),
        jnp.logical_and(far, ~late),
        jnp.logical_and(far, late),
    )
    source, target = source.reshape(1, -1), target.reshape(1, -1)
    order = jnp.arange(source.shape[1], dtype=jnp.int32)
    before = order[None, :] < order[:, None]
    place = jnp.full(order.shape, -1, jnp.int32)
    for (first, _), taken in zip(SECTIONS, members_of):
        taken = taken.reshape(-1)
        earlier = jnp.sum(jnp.logical_and(before, taken[None, :]).astype(jnp.int32), axis=1)
        place = jnp.where(taken, first + earlier, place)
    slots = jnp.arange(TILE_SLOTS, dtype=jnp.int32)
    hits = place[None, :] == slots[:, None]
    used = jnp.any(hits, axis=1)
    sources = jnp.sum(jnp.where(hits, source, 0), axis=1)
    targets = jnp.sum(jnp.where(hits, target, 0), axis=1)
    late_slot = jnp.logical_or(jnp.logical_and(slots >= 12, slots < 20), slots >= 28)
    source_ids = jnp.where(used, sources, -1)
    target_ids = jnp.where(used, jnp.where(slots >= 20, FAR + targets, targets), -1)
    scalars = jnp.stack(
        [
            jnp.where(jnp.logical_and(late_slot, used), sources - 8, sources),
            targets,
            jnp.where(used, source_ids, SOURCE_SLOTS),
            jnp.where(used, target_ids, TARGET_SLOTS),
            jnp.broadcast_to(own_group, slots.shape).astype(jnp.int32),
        ]
    )
    lists = []
    for ids in (source_ids, target_ids):
        rows = jnp.any(ids[None, :] == jnp.arange(16)[:, None], axis=1).astype(jnp.float32)
        lists.append(jnp.broadcast_to(ids[:, None], (TILE_SLOTS, 128)))
        lists.append(jnp.broadcast_to(rows[:, None], (16, 128)))
    return scalars, *lists


def shards_quad(source_vectors, target_vectors, source_mass, target_mass, candidates):
    members = lax.axis_size("member")
    groups = lax.axis_size("group")
    own_group = lax.axis_index("group")
    own_member = lax.axis_index("member")
    per_device, cand_count = candidates.shape
    block_rows = source_vectors.shape[0] // per_device
    width = source_vectors.shape[1]
    blocked = (per_device, block_rows, width)
    member_swap = lambda values, bit: swap(values, "member", members, bit)
    group_swap = lambda values, bit: swap(values, "group", groups, bit)

    source_own = source_vectors.reshape(blocked)
    target_own = target_vectors.reshape(blocked)
    named = [candidates] + [member_swap(candidates, bit) for bit in (1, 2, 3)]
    target_far = member_swap(target_own, 4)
    source_near = member_swap(source_own, 2)
    source_late, target_late, *named = lax.optimization_barrier((source_own, target_own, *named))
    mirrors = lax.all_to_all(target_late, "group", split_axis=0, concat_axis=0, tiled=True)
    source_core = member_swap(source_late, 1)
    scalars, by_source, has_source, by_target, has_target = tile_lists(
        jnp.concatenate(named), own_group, own_member, members, per_device
    )
    own_source_mass = LOG2E * source_mass.reshape(per_device, block_rows)
    own_mass = LOG2E * target_mass.reshape(per_device, block_rows)

    side = jax.ShapeDtypeStruct((16, block_rows), jnp.float32)
    flat = jax.ShapeDtypeStruct((8, 128), jnp.float32)
    stacked = lambda count: jax.ShapeDtypeStruct((count, block_rows, width), source_vectors.dtype)
    tile_rows = [VMEM((TILE_SLOTS, block_rows), jnp.float32)] * 2
    pass_buffers = [
        VMEM((SOURCE_SLOTS + 1, 8, block_rows), jnp.float32),
        *tile_rows,
        VMEM((SOURCE_SLOTS, block_rows, 128), jnp.float32),
    ]

    early, sources, targets = call(
        early_kernel,
        [scalars, by_source, source_own, source_core, target_own, mirrors],
        [side, stacked(8), stacked(7)],
        tile_rows,
    )
    source_near, early = lax.optimization_barrier((source_near, early))
    source_cross = member_swap(source_near, 1)
    parts, late_sources = call(
        first_kernel,
        [
            scalars,
            by_source,
            early,
            own_source_mass,
            sources,
            source_near,
            source_cross,
            targets,
            target_far,
        ],
        [jax.ShapeDtypeStruct((24, block_rows), jnp.float32), stacked(8)],
        tile_rows,
    )
    blocks = [sources, late_sources, targets, target_far]
    masses, extra = [], []
    for step in range(ITERS):
        last_pass = step == ITERS - 1
        parts = [parts] + [member_swap(parts, bit) for bit in (1, 2, 3)]
        masses = masses or parts
        columns, potential = call(
            functools.partial(columns_kernel, last_pass),
            [scalars, by_target, has_target, *blocks, *masses, own_mass, *(parts + extra if last_pass else [])],
            [side, flat if last_pass else side],
            pass_buffers,
        )
        partner = member_swap(columns, 4)
        if last_pass:
            break
        sent = call(
            forward_kernel,
            [scalars, columns, partner],
            [jax.ShapeDtypeStruct((4, block_rows), jnp.float32)] * 3,
        )
        received = [group_swap(values, bit) for bit, values in enumerate(sent, 1)]
        parts, target_rows = call(
            rows_kernel,
            [scalars, by_source, has_source, *blocks, potential, columns, partner, *received],
            [side, side],
            [*pass_buffers, VMEM((8, block_rows), jnp.float32)],
        )
        extra = [target_rows]
    received = [group_swap(columns, bit) for bit in (1, 2, 3)]
    (final,) = call(
        finish_kernel,
        [scalars, columns, partner, *received],
        [flat],
        [VMEM((8, block_rows), jnp.float32)],
    )
    return potential.reshape(source_mass.shape), final.reshape(target_mass.shape)


def shards(source_vectors, target_vectors, source_mass, target_mass, candidates):
    quad = lax.axis_size("member") == 8 and lax.axis_size("group") == 4 and candidates.shape == (4, 8)
    plan = shards_quad if quad else shards_any
    return plan(source_vectors, target_vectors, source_mass, target_mass, candidates)


def solution(mesh):
    placed = (
        P(("group", "member"), None),
        P(("group", "member"), None),
        P(("group", "member")),
        P(("group", "member")),
        P(("group", "member"), None),
    )
    return jax.shard_map(
        shards,
        mesh=mesh,
        in_specs=placed,
        out_specs=(P(("group", "member")), P(("group", "member"))),
        check_vma=False,
    )
```

```python
import functools

import jax
import jax.numpy as jnp
from jax import lax
from jax.experimental import pallas as pl
from jax.experimental.pallas import tpu as pltpu
from jax.sharding import PartitionSpec as P

ITERS = 2


entropy_strength = 0.3
very_low = -1e30


def log_partition(values, axis):
    largest_score = jnp.max(values, axis=axis, keepdims=True)
    return jnp.squeeze(largest_score, axis) + jnp.log(
        jnp.sum(jnp.exp(values - largest_score), axis=axis)
    )


def slot_layout(lists, per_device, members, capacity):
    owner = lists // per_device
    partner = owner % members
    local_block = lists % per_device
    ordering = jnp.arange(lists.shape[-1], dtype=jnp.int32)
    matching = partner[..., :, None] == partner[..., None, :]
    earlier = ordering[None, :] < ordering[:, None]
    position = jnp.sum(jnp.logical_and(matching, earlier).astype(jnp.int32), axis=-1)
    return (partner * capacity + position, local_block)


def trade_member(values):
    return lax.all_to_all(values, "member", split_axis=0, concat_axis=0, tiled=True)


def trade_group(values):
    return lax.all_to_all(values, "group", split_axis=0, concat_axis=0, tiled=True)


def tile_terms(sources, target_blocks, picks, side, by_rows):
    tile_count, block_rows, width = sources.shape
    batch = 4
    grouped = (
        sources.reshape(tile_count // batch, batch, block_rows, width),
        picks.reshape(tile_count // batch, batch),
        side.reshape(tile_count // batch, batch, block_rows),
    )

    def visit(grouped_part):
        source_portion, pick_part, side_portion = grouped_part
        key_entries = jnp.take(target_blocks, pick_part, axis=0)
        score_matrix = jnp.einsum(
            "umk,ugk->umg", source_portion, key_entries, preferred_element_type=jnp.float32
        )
        if by_rows:
            return log_partition((score_matrix + side_portion[:, None, :]) / entropy_strength, 2)
        return log_partition((score_matrix + side_portion[:, :, None]) / entropy_strength, 1)

    return lax.map(visit, grouped).reshape(tile_count, block_rows)


def owner_update(slot_terms, mirror_terms, incoming, target_marginal):
    output_list = []
    for local_block in range(target_marginal.shape[0]):
        masked = jnp.where((incoming == local_block)[:, None], slot_terms, very_low)
        stacked = jnp.concatenate([masked, mirror_terms[local_block][None, :]], axis=0)
        output_list.append(log_partition(stacked, 0))
    return entropy_strength * target_marginal - entropy_strength * jnp.stack(output_list)


def shards_any(source_vectors, target_vectors, source_mass, target_mass, candidates):
    members = lax.axis_size("member")
    groups = lax.axis_size("group")
    own_member = lax.axis_index("member")
    source_count, cand_count = candidates.shape
    inside_count = cand_count - 1
    block_rows = source_vectors.shape[0] // source_count
    width = source_vectors.shape[1]
    target_count = target_vectors.shape[0] // block_rows
    capacity = (source_count * inside_count + members - 1) // members
    spots = members * capacity
    source_blocks = source_vectors.reshape(source_count, block_rows, width)
    target_blocks = target_vectors.reshape(target_count, block_rows, width)
    source_marginal = source_mass.reshape(source_count, block_rows)
    target_marginal = target_mass.reshape(target_count, block_rows)
    own_lists = candidates[:, :inside_count]
    own_spots, own_local = slot_layout(
        own_lists.reshape(1, source_count * inside_count), target_count, members, capacity
    )
    own_spots = own_spots[0]
    all_lists = lax.all_gather(own_lists, "member", axis=0, tiled=True)
    their_spots, their_local = slot_layout(
        all_lists.reshape(members, source_count * inside_count), target_count, members, capacity
    )
    wanted_spots = own_member * capacity + jnp.arange(capacity, dtype=jnp.int32)
    hits = their_spots[:, :, None] == wanted_spots[None, None, :]
    incoming = (jnp.sum(jnp.where(hits, their_local[:, :, None] + 1, 0), axis=1) - 1).reshape(spots)
    picks = jnp.maximum(incoming, 0)
    mirror_group = candidates[:, inside_count] // target_count // members
    spot_range = jnp.arange(spots, dtype=jnp.int32)
    group_range = jnp.arange(groups, dtype=jnp.int32)
    source_of = jnp.arange(source_count * inside_count, dtype=jnp.int32) // inside_count
    slot_index = jnp.sum(
        jnp.where(own_spots[:, None] == spot_range[None, :], source_of[:, None], 0), axis=0
    )
    mirror_index = jnp.sum(
        jnp.where(
            mirror_group[:, None] == group_range[None, :],
            jnp.arange(source_count, dtype=jnp.int32)[:, None],
            0,
        ),
        axis=0,
    )
    slot_payload = jnp.take(source_blocks, slot_index, axis=0)
    mirror_payload = jnp.take(source_blocks, mirror_index, axis=0)
    arrived = lax.all_to_all(
        slot_payload.reshape(members, capacity, block_rows, width),
        "member",
        split_axis=0,
        concat_axis=0,
        tiled=True,
    ).reshape(spots, block_rows, width)
    arrived_mirror = lax.all_to_all(
        mirror_payload, "group", split_axis=0, concat_axis=0, tiled=True
    )
    target_current = jnp.zeros((target_count, block_rows), jnp.float32)
    for step in range(ITERS):
        row_slots = tile_terms(
            arrived, target_blocks, picks, jnp.take(target_current, picks, axis=0), True
        )
        row_mirror = tile_terms(arrived_mirror, target_blocks, group_range, target_current, True)
        slot_back = trade_member(row_slots.reshape(members, capacity, block_rows)).reshape(
            spots, block_rows
        )
        mirror_back = trade_group(row_mirror)
        collected_rows = jnp.concatenate(
            [
                jnp.take(slot_back, own_spots, axis=0).reshape(
                    source_count, inside_count, block_rows
                ),
                jnp.take(mirror_back, mirror_group, axis=0)[:, None],
            ],
            axis=1,
        )
        source_current = entropy_strength * source_marginal - entropy_strength * log_partition(
            collected_rows, 1
        )
        slot_sides = trade_member(
            jnp.take(source_current, slot_index, axis=0).reshape(members, capacity, block_rows)
        ).reshape(spots, block_rows)
        mirror_sides = trade_group(jnp.take(source_current, mirror_index, axis=0))
        column_slots = tile_terms(arrived, target_blocks, picks, slot_sides, False)
        column_mirror = tile_terms(arrived_mirror, target_blocks, group_range, mirror_sides, False)
        target_current = owner_update(column_slots, column_mirror, incoming, target_marginal)
    return (
        source_current.reshape(source_count * block_rows),
        target_current.reshape(target_count * block_rows),
    )


LOG2E = 1.4426950408889634
TO_LOGIT = LOG2E / entropy_strength
TO_POTENTIAL = entropy_strength / LOG2E
CAPACITY = 4
SOURCE_SLOTS = 16
TARGET_SLOTS = 12
FAR = 8
SECTIONS = ((0, 12), (12, 8), (20, 8), (28, 8))
TILE_SLOTS = 40
SMALL, LARGE = 2.0**-100, 2.0**100


def merge(parts):
    top = functools.reduce(jnp.maximum, parts)
    return top + LOG2E * jnp.log(sum(jnp.exp2(part - top) for part in parts))


def swapped(rows, size):
    pieces = [rows[start : start + size] for start in range(0, rows.shape[0], size)]
    return jnp.concatenate([pieces[index ^ 1] for index in range(len(pieces))], axis=0)


def source_bias(mass_refs, part_refs):
    own, core, near, cross = (ref[0:16] for ref in part_refs)
    core = swapped(core, 4)
    near = swapped(near, 8)
    cross = swapped(swapped(cross, 4), 8)
    mass = jnp.concatenate([ref[16:20] for ref in mass_refs], axis=0)
    return mass - merge([own, core, near, cross])


def target_bias(scalars, columns, partner, mirrors, scratch):
    group = scalars[4, 0]
    scratch[...] = jnp.full(scratch.shape, very_low, jnp.float32)
    for offset, ref in enumerate(mirrors, 1):
        scratch[pl.ds(group ^ offset, 1), :] = ref[0:1]
        scratch[pl.ds(4 + (group ^ offset), 1), :] = ref[1:2]
    own = columns[12:16] - merge([columns[0:4], partner[8:12], scratch[0:4]])
    far = partner[12:16] - merge([columns[8:12], partner[0:4], scratch[4:8]])
    across = [
        ref[3:4] - merge([ref[2:3], columns[3 + offset : 4 + offset]])
        for offset, ref in enumerate(mirrors, 1)
    ]
    blank = jnp.zeros((1, own.shape[1]), jnp.float32)
    return jnp.concatenate([own, *across, blank, far, *([blank] * 4)], axis=0)


def spread(rows, bias):
    high = rows.astype(jnp.bfloat16)
    rest = rows - high.astype(jnp.float32)
    middle = rest.astype(jnp.bfloat16)
    low = (rest - middle.astype(jnp.float32)).astype(jnp.bfloat16)
    parts = jnp.concatenate([high, middle, low], axis=0)
    count = rows.shape[0]
    shape = (3 * count, count * 128)
    slot = lax.broadcasted_iota(jnp.int32, shape, 0) & (count - 1)
    place = lax.broadcasted_iota(jnp.int32, shape, 1) >> 7
    chosen = jnp.where(slot == place, 1.0, 0.0).astype(jnp.bfloat16)
    turned = lax.dot_general(
        parts, chosen, (((0,), (0,)), ((), ())), preferred_element_type=jnp.float32
    )
    for index in range(bias.shape[0]):
        bias[index] = turned[:, 128 * index : 128 * (index + 1)]


def score(summed, kept):
    product = lax.dot_general(summed, kept, (((1,), (1,)), ((), ())), preferred_element_type=jnp.float32)
    return product * TO_LOGIT


def wide(values):
    return jnp.concatenate([values, values], axis=1)


def sides(section, by_rows, sources, targets):
    late_source, late_target = section in (1, 3), section in (2, 3)
    source = (sources[late_source], 0, 8 if late_source else 0)
    target = (targets[late_target], 1, FAR if late_target else 0)
    return (target, source) if by_rows else (source, target)


def exact_pass(scalars, ids, by_rows, sections, sources, targets, bias, tops, sums, unrolled):
    for section in sections:
        first, count = SECTIONS[section]
        (summed, summed_row, summed_base), (kept, kept_row, _) = sides(section, by_rows, sources, targets)

        def visit(slot, carry=0):
            block = scalars[summed_row, slot]
            logits = score(summed[block], kept[scalars[kept_row, slot]])
            if bias is not None:
                logits = logits + wide(bias[summed_base + block])
            top = jnp.max(logits, axis=0, keepdims=True)
            tops[pl.ds(slot, 1), :] = top
            sums[pl.ds(slot, 1), :] = jnp.sum(jnp.exp2(logits - top), axis=0, keepdims=True)
            return carry

        if unrolled:
            for slot in range(first, first + count):
                visit(slot)
        else:
            lax.fori_loop(first, first + count, visit, 0)
    first, last = SECTIONS[sections[0]][0], sum(SECTIONS[sections[-1]])
    low, high = first // 8 * 8, (last + 7) // 8 * 8
    id_rows = wide(ids[low:high])
    if low < first or last < high:
        slot = low + lax.broadcasted_iota(jnp.int32, id_rows.shape, 0)
        id_rows = jnp.where(jnp.logical_and(slot >= first, slot < last), id_rows, -1)
    top_rows, sum_rows = tops[low:high], sums[low:high]
    best, total = [], []
    for block in range(SOURCE_SLOTS if by_rows else TARGET_SLOTS):
        mine = id_rows == block
        top = jnp.max(jnp.where(mine, top_rows, very_low), axis=0, keepdims=True)
        best.append(top)
        total.append(
            jnp.sum(jnp.where(mine, sum_rows * jnp.exp2(top_rows - top), 0.0), axis=0, keepdims=True)
        )
    best = jnp.concatenate(best, axis=0)
    total = jnp.concatenate(total, axis=0)
    return jnp.where(total > 0, best + LOG2E * jnp.log(jnp.where(total > 0, total, 1.0)), very_low)


def fast_pass(scalars, ids, present, by_rows, sections, sources, targets, bias, shift, total, tops, sums):
    total[...] = jnp.zeros(total.shape, jnp.float32)
    for section in sections:
        first, count = SECTIONS[section]
        (summed, summed_row, summed_base), (kept, kept_row, _) = sides(section, by_rows, sources, targets)
        for slot in range(first, first + count):
            block = scalars[summed_row, slot]
            logits = score(summed[block], kept[scalars[kept_row, slot]])
            logits = logits + (shift if bias is None else wide(bias[summed_base + block]))
            terms = jnp.exp2(logits)
            place = scalars[2 + kept_row, slot]
            total[place] = total[place] + jnp.sum(terms.reshape(-1, 8, terms.shape[1]), axis=0)
    count = SOURCE_SLOTS if by_rows else TARGET_SLOTS
    sums_of = jnp.concatenate(
        [jnp.sum(total[block], axis=0, keepdims=True) for block in range(count)], axis=0
    )
    here = wide(present[0:count]) > 0
    result = LOG2E * jnp.log(jnp.where(here, sums_of, 1.0))
    if shift is not None:
        result = result - shift
    fine = jnp.logical_and(sums_of > SMALL, sums_of < LARGE)
    worst = jnp.min(jnp.where(jnp.logical_or(fine, jnp.logical_not(here)), 1.0, 0.0))
    return jnp.where(here, result, very_low), worst > 0.5


def guarded_pass(scalars, ids, present, by_rows, sections, sources, targets, rows, shift, work, write):
    total, tops, sums, *bias = work
    bias = bias[0] if bias else None
    if bias is not None:
        spread(rows if shift is None else rows + shift, bias)
    result, fine = fast_pass(
        scalars, ids, present, by_rows, sections, sources, targets, bias, shift, total, tops, sums
    )
    write(result)

    @pl.when(jnp.logical_not(fine))
    def _():
        if shift is not None and bias is not None:
            spread(rows, bias)
        write(exact_pass(scalars, ids, by_rows, sections, sources, targets, bias, tops, sums, False))


def middle(pieces):
    top = functools.reduce(jnp.maximum, [jnp.max(piece, axis=(0, 1), keepdims=True) for piece in pieces])
    bottom = functools.reduce(jnp.minimum, [jnp.min(piece, axis=(0, 1), keepdims=True) for piece in pieces])
    return 0.5 * (top + bottom)


def early_kernel(scalars, ids, own, core, target, mirrors, out, sources, targets, tops, sums):
    sources[0:4] = own[...]
    sources[4:8] = core[...]
    targets[0:4] = target[...]
    for offset in (1, 2, 3):
        targets[3 + offset] = mirrors[scalars[4, 0] ^ offset]
    out[...] = exact_pass(
        scalars, ids, True, (0,), (sources, None), (targets, None), None, tops, sums, True
    )


def first_kernel(
    scalars, ids, present, early, mass, sources, near, cross, targets, far, out, late_sources, *work
):
    late_sources[0:4] = near[0 : mass.shape[1] * 4].reshape(late_sources[0:4].shape)
    late_sources[4:8] = cross[0 : mass.shape[1] * 4].reshape(late_sources[4:8].shape)
    out[16:20, :] = mass[...]
    out[20:24, :] = jnp.zeros((4, out.shape[1]), jnp.float32)
    begun = early[...]
    shift = -jnp.max(begun, axis=(0, 1), keepdims=True)

    def write(late):
        out[0:16, :] = merge([begun, late])

    guarded_pass(
        scalars,
        ids,
        present,
        True,
        (1, 2, 3),
        (sources, late_sources),
        (targets, far),
        None,
        shift,
        work,
        write,
    )


def columns_kernel(last_pass, *refs):
    scalars, ids, present = refs[:3]
    sources, targets = refs[3:5], refs[5:7]
    masses, target_mass, rest = refs[7:11], refs[11], refs[12:]
    parts, shift = masses, None
    if last_pass:
        parts, (shift, *rest) = rest[:4], rest[4:]
        shift = shift[0:1, 0:1]
    out, second, *work = rest
    rows = source_bias(masses, parts)
    if last_pass:
        for block in range(4):
            for half in range(2):
                second[2 * block + half : 2 * block + half + 1, :] = (
                    TO_POTENTIAL * rows[block : block + 1, 128 * half : 128 * (half + 1)]
                )
    else:
        second[...] = jnp.broadcast_to(middle([rows]), second.shape)
    out[12:16, :] = target_mass[0:4]

    def write(result):
        out[0:TARGET_SLOTS, :] = result

    guarded_pass(
        scalars, ids, present, False, (0, 1, 2, 3), sources, targets, rows, shift, work, write
    )


def rows_kernel(*refs):
    scalars, ids, present = refs[:3]
    sources, targets = refs[3:5], refs[5:7]
    shift, columns, partner, *mirrors = refs[7:13]
    out, second, *work, scratch = refs[13:]
    rows = target_bias(scalars, columns, partner, mirrors, scratch)
    second[...] = jnp.broadcast_to(middle([rows[0:7], rows[8:12]]), second.shape)

    def write(result):
        out[...] = result

    guarded_pass(
        scalars, ids, present, True, (0, 1, 2, 3), sources, targets, rows, shift[0:1, 0:1], work, write
    )


def forward_kernel(scalars, columns, partner, *outs):
    group = scalars[4, 0]
    for offset, out in enumerate(outs, 1):
        block = group ^ offset
        out[0:1, :] = columns[3 + offset : 4 + offset]
        out[1:2, :] = partner[3 + offset : 4 + offset]
        out[2:3, :] = merge([columns[pl.ds(block, 1), :], partner[pl.ds(FAR + block, 1), :]])
        out[3:4, :] = columns[pl.ds(12 + block, 1), :]


def finish_kernel(scalars, columns, partner, *rest):
    *mirrors, out, scratch = rest
    group = scalars[4, 0]
    scratch[...] = jnp.full(scratch.shape, very_low, jnp.float32)
    for offset, ref in enumerate(mirrors, 1):
        scratch[pl.ds(group ^ offset, 1), :] = ref[3 + offset : 4 + offset]
    rows = columns[12:16] - merge([columns[0:4], partner[8:12], scratch[0:4]])
    for block in range(4):
        for half in range(2):
            out[2 * block + half : 2 * block + half + 1, :] = (
                TO_POTENTIAL * rows[block : block + 1, 128 * half : 128 * (half + 1)]
            )


SMEM, VMEM = pltpu.SMEM, pltpu.VMEM


def call(kernel, inputs, outs, scratch=()):
    whole = pl.BlockSpec(memory_space=VMEM)
    return pl.pallas_call(
        kernel,
        out_shape=outs,
        in_specs=[pl.BlockSpec(memory_space=SMEM)] + [whole] * (len(inputs) - 1),
        out_specs=[whole] * len(outs),
        scratch_shapes=list(scratch),
        compiler_params=pltpu.CompilerParams(vmem_limit_bytes=32 << 20),
    )(*inputs)


def swap(values, axis, size, bit):
    return lax.ppermute(values, axis, [(index, index ^ bit) for index in range(size)])


def tile_lists(candidates, own_group, own_member, members, per_device, slot_count):
    owner = candidates // per_device
    local = candidates % per_device
    apart = (owner % members) ^ own_member
    last = candidates.shape[1] - 1
    mirror = (owner // members) ^ own_group
    is_last = jnp.arange(last + 1)[None, :] == last
    source = jnp.broadcast_to(
        jnp.arange(candidates.shape[0], dtype=jnp.int32)[:, None], candidates.shape
    )
    own_mirror = jnp.logical_and(is_last, source < per_device)
    near = jnp.logical_and(~is_last, apart == 0)
    far = jnp.logical_and(~is_last, apart == 4)
    late = source >= 2 * per_device
    target = jnp.where(jnp.logical_and(is_last, mirror > 0), 3 + mirror, local)
    members_of = (
        jnp.logical_or(jnp.logical_and(near, ~late), own_mirror),
        jnp.logical_and(near, late),
        jnp.logical_and(far, ~late),
        jnp.logical_and(far, late),
    )
    source, target = source.reshape(1, -1), target.reshape(1, -1)
    order = jnp.arange(source.shape[1], dtype=jnp.int32)
    before = order[None, :] < order[:, None]
    place = jnp.full(order.shape, -1, jnp.int32)
    for (first, _), taken in zip(SECTIONS, members_of):
        if first >= 12 and slot_count == 16:
            break
        taken = taken.reshape(-1)
        earlier = jnp.sum(jnp.logical_and(before, taken[None, :]).astype(jnp.int32), axis=1)
        place = jnp.where(taken, first + earlier, place)
    slots = jnp.arange(slot_count, dtype=jnp.int32)
    hits = place[None, :] == slots[:, None]
    used = jnp.any(hits, axis=1)
    sources = jnp.sum(jnp.where(hits, source, 0), axis=1)
    targets = jnp.sum(jnp.where(hits, target, 0), axis=1)
    late_slot = jnp.logical_or(jnp.logical_and(slots >= 12, slots < 20), slots >= 28)
    source_ids = jnp.where(used, sources, -1)
    target_ids = jnp.where(used, jnp.where(slots >= 20, FAR + targets, targets), -1)
    scalars = jnp.stack(
        [
            jnp.where(jnp.logical_and(late_slot, used), sources - 8, sources),
            targets,
            jnp.where(used, source_ids, SOURCE_SLOTS),
            jnp.where(used, target_ids, TARGET_SLOTS),
            jnp.broadcast_to(own_group, slots.shape).astype(jnp.int32),
        ]
    )
    lists = []
    for ids in (source_ids, target_ids):
        lists.append(jnp.broadcast_to(ids[:, None], (slot_count, 128)))
        for counted in (ids, jnp.where(slots >= 12, ids, -1)):
            rows = jnp.any(counted[None, :] == jnp.arange(16)[:, None], axis=1).astype(jnp.float32)
            lists.append(jnp.broadcast_to(rows[:, None], (16, 128)))
    return scalars, *lists


def shards_quad(source_vectors, target_vectors, source_mass, target_mass, candidates):
    members = lax.axis_size("member")
    groups = lax.axis_size("group")
    own_group = lax.axis_index("group")
    own_member = lax.axis_index("member")
    per_device, cand_count = candidates.shape
    block_rows = source_vectors.shape[0] // per_device
    width = source_vectors.shape[1]
    blocked = (per_device, block_rows, width)
    member_swap = lambda values, bit: swap(values, "member", members, bit)
    group_swap = lambda values, bit: swap(values, "group", groups, bit)

    source_own = source_vectors.reshape(blocked)
    target_own = target_vectors.reshape(blocked)
    target_far = member_swap(target_own, 4)
    named = jnp.concatenate([candidates, member_swap(candidates, 1)])
    note = jnp.pad(
        named.astype(source_vectors.dtype).reshape(1, named.size), ((0, 15), (0, width - named.size))
    )
    source_near = member_swap(jnp.concatenate([source_vectors, note]), 2)
    source_late, target_late, named = lax.optimization_barrier((source_own, target_own, named))
    mirrors = lax.all_to_all(target_late, "group", split_axis=0, concat_axis=0, tiled=True)
    source_core = member_swap(source_late, 1)
    place = (own_group, own_member, members, per_device)
    early_scalars, early_by_source, *_ = tile_lists(named, *place, 16)
    own_source_mass = LOG2E * source_mass.reshape(per_device, block_rows)
    own_mass = LOG2E * target_mass.reshape(per_device, block_rows)

    side = jax.ShapeDtypeStruct((16, block_rows), jnp.float32)
    flat = jax.ShapeDtypeStruct((8, 128), jnp.float32)
    stacked = lambda count: jax.ShapeDtypeStruct((count, block_rows, width), source_vectors.dtype)
    tile_rows = [VMEM((TILE_SLOTS, block_rows), jnp.float32)] * 2
    pass_buffers = [
        VMEM((SOURCE_SLOTS + 1, 8, block_rows), jnp.float32),
        *tile_rows,
        VMEM((SOURCE_SLOTS, block_rows, 128), jnp.float32),
    ]

    early, sources, targets = call(
        early_kernel,
        [early_scalars, early_by_source, source_own, source_core, target_own, mirrors],
        [side, stacked(8), stacked(7)],
        tile_rows,
    )
    source_near, early = lax.optimization_barrier((source_near, early))
    source_cross = member_swap(source_near, 1)
    theirs = source_near[per_device * block_rows, : named.size].astype(jnp.int32).reshape(named.shape)
    scalars, by_source, has_source, has_late_source, by_target, has_target, _ = tile_lists(
        jnp.concatenate([named, theirs]), *place, TILE_SLOTS
    )
    parts, late_sources = call(
        first_kernel,
        [
            scalars,
            by_source,
            has_late_source,
            early,
            own_source_mass,
            sources,
            source_near,
            source_cross,
            targets,
            target_far,
        ],
        [jax.ShapeDtypeStruct((24, block_rows), jnp.float32), stacked(8)],
        pass_buffers[:3],
    )
    blocks = [sources, late_sources, targets, target_far]
    masses, extra = [], []
    for step in range(ITERS):
        last_pass = step == ITERS - 1
        parts = [parts] + [member_swap(parts, bit) for bit in (1, 2, 3)]
        masses = masses or parts
        columns, potential = call(
            functools.partial(columns_kernel, last_pass),
            [scalars, by_target, has_target, *blocks, *masses, own_mass, *(parts + extra if last_pass else [])],
            [side, flat],
            pass_buffers,
        )
        partner = member_swap(columns, 4)
        if last_pass:
            break
        sent = call(
            forward_kernel,
            [scalars, columns, partner],
            [jax.ShapeDtypeStruct((4, block_rows), jnp.float32)] * 3,
        )
        received = [group_swap(values, bit) for bit, values in enumerate(sent, 1)]
        parts, shift = call(
            rows_kernel,
            [scalars, by_source, has_source, *blocks, potential, columns, partner, *received],
            [side, flat],
            [*pass_buffers, VMEM((8, block_rows), jnp.float32)],
        )
        extra = [shift]
    received = [group_swap(columns, bit) for bit in (1, 2, 3)]
    (final,) = call(
        finish_kernel,
        [scalars, columns, partner, *received],
        [flat],
        [VMEM((8, block_rows), jnp.float32)],
    )
    return potential.reshape(source_mass.shape), final.reshape(target_mass.shape)


def shards(source_vectors, target_vectors, source_mass, target_mass, candidates):
    quad = lax.axis_size("member") == 8 and lax.axis_size("group") == 4 and candidates.shape == (4, 8)
    plan = shards_quad if quad else shards_any
    return plan(source_vectors, target_vectors, source_mass, target_mass, candidates)


def solution(mesh):
    placed = (
        P(("group", "member"), None),
        P(("group", "member"), None),
        P(("group", "member")),
        P(("group", "member")),
        P(("group", "member"), None),
    )
    return jax.shard_map(
        shards,
        mesh=mesh,
        in_specs=placed,
        out_specs=(P(("group", "member")), P(("group", "member"))),
        check_vma=False,
    )
```

```python
import functools

import jax
import jax.numpy as jnp
from jax import lax
from jax.experimental import pallas as pl
from jax.experimental.pallas import tpu as pltpu
from jax.sharding import PartitionSpec as P

ITERS = 2


entropy_strength = 0.3
very_low = -1e30


def log_partition(values, axis):
    largest_score = jnp.max(values, axis=axis, keepdims=True)
    return jnp.squeeze(largest_score, axis) + jnp.log(
        jnp.sum(jnp.exp(values - largest_score), axis=axis)
    )


def slot_layout(lists, per_device, members, capacity):
    owner = lists // per_device
    partner = owner % members
    local_block = lists % per_device
    ordering = jnp.arange(lists.shape[-1], dtype=jnp.int32)
    matching = partner[..., :, None] == partner[..., None, :]
    earlier = ordering[None, :] < ordering[:, None]
    position = jnp.sum(jnp.logical_and(matching, earlier).astype(jnp.int32), axis=-1)
    return (partner * capacity + position, local_block)


def trade_member(values):
    return lax.all_to_all(values, "member", split_axis=0, concat_axis=0, tiled=True)


def trade_group(values):
    return lax.all_to_all(values, "group", split_axis=0, concat_axis=0, tiled=True)


def tile_terms(sources, target_blocks, picks, side, by_rows):
    tile_count, block_rows, width = sources.shape
    batch = 4
    grouped = (
        sources.reshape(tile_count // batch, batch, block_rows, width),
        picks.reshape(tile_count // batch, batch),
        side.reshape(tile_count // batch, batch, block_rows),
    )

    def visit(grouped_part):
        source_portion, pick_part, side_portion = grouped_part
        key_entries = jnp.take(target_blocks, pick_part, axis=0)
        score_matrix = jnp.einsum(
            "umk,ugk->umg", source_portion, key_entries, preferred_element_type=jnp.float32
        )
        if by_rows:
            return log_partition((score_matrix + side_portion[:, None, :]) / entropy_strength, 2)
        return log_partition((score_matrix + side_portion[:, :, None]) / entropy_strength, 1)

    return lax.map(visit, grouped).reshape(tile_count, block_rows)


def owner_update(slot_terms, mirror_terms, incoming, target_marginal):
    output_list = []
    for local_block in range(target_marginal.shape[0]):
        masked = jnp.where((incoming == local_block)[:, None], slot_terms, very_low)
        stacked = jnp.concatenate([masked, mirror_terms[local_block][None, :]], axis=0)
        output_list.append(log_partition(stacked, 0))
    return entropy_strength * target_marginal - entropy_strength * jnp.stack(output_list)


def shards_any(source_vectors, target_vectors, source_mass, target_mass, candidates):
    members = lax.axis_size("member")
    groups = lax.axis_size("group")
    own_member = lax.axis_index("member")
    source_count, cand_count = candidates.shape
    inside_count = cand_count - 1
    block_rows = source_vectors.shape[0] // source_count
    width = source_vectors.shape[1]
    target_count = target_vectors.shape[0] // block_rows
    capacity = (source_count * inside_count + members - 1) // members
    spots = members * capacity
    source_blocks = source_vectors.reshape(source_count, block_rows, width)
    target_blocks = target_vectors.reshape(target_count, block_rows, width)
    source_marginal = source_mass.reshape(source_count, block_rows)
    target_marginal = target_mass.reshape(target_count, block_rows)
    own_lists = candidates[:, :inside_count]
    own_spots, own_local = slot_layout(
        own_lists.reshape(1, source_count * inside_count), target_count, members, capacity
    )
    own_spots = own_spots[0]
    all_lists = lax.all_gather(own_lists, "member", axis=0, tiled=True)
    their_spots, their_local = slot_layout(
        all_lists.reshape(members, source_count * inside_count), target_count, members, capacity
    )
    wanted_spots = own_member * capacity + jnp.arange(capacity, dtype=jnp.int32)
    hits = their_spots[:, :, None] == wanted_spots[None, None, :]
    incoming = (jnp.sum(jnp.where(hits, their_local[:, :, None] + 1, 0), axis=1) - 1).reshape(spots)
    picks = jnp.maximum(incoming, 0)
    mirror_group = candidates[:, inside_count] // target_count // members
    spot_range = jnp.arange(spots, dtype=jnp.int32)
    group_range = jnp.arange(groups, dtype=jnp.int32)
    source_of = jnp.arange(source_count * inside_count, dtype=jnp.int32) // inside_count
    slot_index = jnp.sum(
        jnp.where(own_spots[:, None] == spot_range[None, :], source_of[:, None], 0), axis=0
    )
    mirror_index = jnp.sum(
        jnp.where(
            mirror_group[:, None] == group_range[None, :],
            jnp.arange(source_count, dtype=jnp.int32)[:, None],
            0,
        ),
        axis=0,
    )
    slot_payload = jnp.take(source_blocks, slot_index, axis=0)
    mirror_payload = jnp.take(source_blocks, mirror_index, axis=0)
    arrived = lax.all_to_all(
        slot_payload.reshape(members, capacity, block_rows, width),
        "member",
        split_axis=0,
        concat_axis=0,
        tiled=True,
    ).reshape(spots, block_rows, width)
    arrived_mirror = lax.all_to_all(
        mirror_payload, "group", split_axis=0, concat_axis=0, tiled=True
    )
    target_current = jnp.zeros((target_count, block_rows), jnp.float32)
    for step in range(ITERS):
        row_slots = tile_terms(
            arrived, target_blocks, picks, jnp.take(target_current, picks, axis=0), True
        )
        row_mirror = tile_terms(arrived_mirror, target_blocks, group_range, target_current, True)
        slot_back = trade_member(row_slots.reshape(members, capacity, block_rows)).reshape(
            spots, block_rows
        )
        mirror_back = trade_group(row_mirror)
        collected_rows = jnp.concatenate(
            [
                jnp.take(slot_back, own_spots, axis=0).reshape(
                    source_count, inside_count, block_rows
                ),
                jnp.take(mirror_back, mirror_group, axis=0)[:, None],
            ],
            axis=1,
        )
        source_current = entropy_strength * source_marginal - entropy_strength * log_partition(
            collected_rows, 1
        )
        slot_sides = trade_member(
            jnp.take(source_current, slot_index, axis=0).reshape(members, capacity, block_rows)
        ).reshape(spots, block_rows)
        mirror_sides = trade_group(jnp.take(source_current, mirror_index, axis=0))
        column_slots = tile_terms(arrived, target_blocks, picks, slot_sides, False)
        column_mirror = tile_terms(arrived_mirror, target_blocks, group_range, mirror_sides, False)
        target_current = owner_update(column_slots, column_mirror, incoming, target_marginal)
    return (
        source_current.reshape(source_count * block_rows),
        target_current.reshape(target_count * block_rows),
    )


LOG2E = 1.4426950408889634
TO_LOGIT = LOG2E / entropy_strength
TO_POTENTIAL = entropy_strength / LOG2E
CAPACITY = 4
SOURCE_SLOTS = 16
TARGET_SLOTS = 12
FAR = 8
SECTIONS = ((0, 12), (12, 8), (20, 8), (28, 8))
TILE_SLOTS = 40
SMALL, LARGE = 2.0**-100, 2.0**100


def merge(parts):
    top = functools.reduce(jnp.maximum, parts)
    return top + LOG2E * jnp.log(sum(jnp.exp2(part - top) for part in parts))


def swapped(rows, size):
    pieces = [rows[start : start + size] for start in range(0, rows.shape[0], size)]
    return jnp.concatenate([pieces[index ^ 1] for index in range(len(pieces))], axis=0)


def source_bias(mass_refs, part_refs):
    own, core, near, cross = (ref[0:16] for ref in part_refs)
    core = swapped(core, 4)
    near = swapped(near, 8)
    cross = swapped(swapped(cross, 4), 8)
    mass = jnp.concatenate([ref[16:20] for ref in mass_refs], axis=0)
    return mass - merge([own, core, near, cross])


def target_bias(scalars, columns, partner, mirrors, scratch):
    group = scalars[4, 0]
    scratch[...] = jnp.full(scratch.shape, very_low, jnp.float32)
    for offset, ref in enumerate(mirrors, 1):
        scratch[pl.ds(group ^ offset, 1), :] = ref[0:1]
        scratch[pl.ds(4 + (group ^ offset), 1), :] = ref[1:2]
    own = columns[12:16] - merge([columns[0:4], partner[8:12], scratch[0:4]])
    far = partner[12:16] - merge([columns[8:12], partner[0:4], scratch[4:8]])
    across = [
        ref[3:4] - merge([ref[2:3], columns[3 + offset : 4 + offset]])
        for offset, ref in enumerate(mirrors, 1)
    ]
    blank = jnp.zeros((1, own.shape[1]), jnp.float32)
    return jnp.concatenate([own, *across, blank, far, *([blank] * 4)], axis=0)


def spread(rows, bias):
    high = rows.astype(jnp.bfloat16)
    rest = rows - high.astype(jnp.float32)
    middle = rest.astype(jnp.bfloat16)
    low = (rest - middle.astype(jnp.float32)).astype(jnp.bfloat16)
    parts = jnp.concatenate([high, middle, low], axis=0)
    count = rows.shape[0]
    shape = (3 * count, count * 128)
    slot = lax.broadcasted_iota(jnp.int32, shape, 0) & (count - 1)
    place = lax.broadcasted_iota(jnp.int32, shape, 1) >> 7
    chosen = jnp.where(slot == place, 1.0, 0.0).astype(jnp.bfloat16)
    turned = lax.dot_general(
        parts, chosen, (((0,), (0,)), ((), ())), preferred_element_type=jnp.float32
    )
    for index in range(bias.shape[0]):
        bias[index] = turned[:, 128 * index : 128 * (index + 1)]


def score(summed, kept):
    product = lax.dot_general(summed, kept, (((1,), (1,)), ((), ())), preferred_element_type=jnp.float32)
    return product * TO_LOGIT


def wide(values):
    return jnp.concatenate([values, values], axis=1)


def sides(section, by_rows, sources, targets):
    late_source, late_target = section in (1, 3), section in (2, 3)
    source = (sources[late_source], 0, 8 if late_source else 0)
    target = (targets[late_target], 1, FAR if late_target else 0)
    return (target, source) if by_rows else (source, target)


def exact_pass(scalars, by_rows, sections, sources, targets, bias, tops, sums, ids, unrolled):
    for section in sections:
        first, count = SECTIONS[section]
        (summed, summed_row, summed_base), (kept, kept_row, _) = sides(section, by_rows, sources, targets)

        def visit(slot, carry=0):
            block = scalars[summed_row, slot]
            logits = score(summed[block], kept[scalars[kept_row, slot]])
            if bias is not None:
                logits = logits + wide(bias[summed_base + block])
            top = jnp.max(logits, axis=0, keepdims=True)
            tops[pl.ds(slot, 1), :] = top
            sums[pl.ds(slot, 1), :] = jnp.sum(jnp.exp2(logits - top), axis=0, keepdims=True)
            ids[pl.ds(slot, 1), :] = jnp.full((1, ids.shape[1]), scalars[2 + kept_row, slot], jnp.int32)
            return carry

        if unrolled:
            for slot in range(first, first + count):
                visit(slot)
        else:
            lax.fori_loop(first, first + count, visit, 0)
    first, last = SECTIONS[sections[0]][0], sum(SECTIONS[sections[-1]])
    low, high = first // 8 * 8, (last + 7) // 8 * 8
    id_rows = ids[low:high]
    if low < first or last < high:
        slot = low + lax.broadcasted_iota(jnp.int32, id_rows.shape, 0)
        id_rows = jnp.where(jnp.logical_and(slot >= first, slot < last), id_rows, -1)
    top_rows, sum_rows = tops[low:high], sums[low:high]
    best, total = [], []
    for block in range(SOURCE_SLOTS if by_rows else TARGET_SLOTS):
        mine = id_rows == block
        top = jnp.max(jnp.where(mine, top_rows, very_low), axis=0, keepdims=True)
        best.append(top)
        total.append(
            jnp.sum(jnp.where(mine, sum_rows * jnp.exp2(top_rows - top), 0.0), axis=0, keepdims=True)
        )
    best = jnp.concatenate(best, axis=0)
    total = jnp.concatenate(total, axis=0)
    return jnp.where(total > 0, best + LOG2E * jnp.log(jnp.where(total > 0, total, 1.0)), very_low)


def fast_pass(scalars, by_rows, sections, sources, targets, bias, shift, total, present):
    total[...] = jnp.zeros(total.shape, jnp.float32)
    present[...] = jnp.zeros(present.shape, jnp.float32)
    for section in sections:
        first, count = SECTIONS[section]
        (summed, summed_row, summed_base), (kept, kept_row, _) = sides(section, by_rows, sources, targets)
        for slot in range(first, first + count):
            block = scalars[summed_row, slot]
            logits = score(summed[block], kept[scalars[kept_row, slot]])
            logits = logits + (shift if bias is None else wide(bias[summed_base + block]))
            terms = jnp.exp2(logits)
            place = scalars[2 + kept_row, slot]
            present[pl.ds(place, 1), :] = jnp.ones((1, present.shape[1]), jnp.float32)
            total[place] = total[place] + jnp.sum(terms.reshape(-1, 8, terms.shape[1]), axis=0)
    count = SOURCE_SLOTS if by_rows else TARGET_SLOTS
    sums_of = jnp.concatenate(
        [jnp.sum(total[block], axis=0, keepdims=True) for block in range(count)], axis=0
    )
    here = present[0:count] > 0
    result = LOG2E * jnp.log(jnp.where(here, sums_of, 1.0))
    if shift is not None:
        result = result - shift
    fine = jnp.logical_and(sums_of > SMALL, sums_of < LARGE)
    worst = jnp.min(jnp.where(jnp.logical_or(fine, jnp.logical_not(here)), 1.0, 0.0))
    return jnp.where(here, result, very_low), worst > 0.5


def guarded_pass(scalars, by_rows, sections, sources, targets, rows, shift, work, write):
    total, present, tops, sums, ids, *bias = work
    bias = bias[0] if bias else None
    if bias is not None:
        spread(rows if shift is None else rows + shift, bias)
    result, fine = fast_pass(
        scalars, by_rows, sections, sources, targets, bias, shift, total, present
    )
    write(result)

    @pl.when(jnp.logical_not(fine))
    def _():
        if shift is not None and bias is not None:
            spread(rows, bias)
        write(exact_pass(scalars, by_rows, sections, sources, targets, bias, tops, sums, ids, False))


def middle(pieces):
    top = functools.reduce(jnp.maximum, [jnp.max(piece, axis=(0, 1), keepdims=True) for piece in pieces])
    bottom = functools.reduce(jnp.minimum, [jnp.min(piece, axis=(0, 1), keepdims=True) for piece in pieces])
    return 0.5 * (top + bottom)


def early_kernel(scalars, own, core, target, mirrors, out, sources, targets, tops, sums, ids):
    sources[0:4] = own[...]
    sources[4:8] = core[...]
    targets[0:4] = target[...]
    for offset in (1, 2, 3):
        targets[3 + offset] = mirrors[scalars[4, 0] ^ offset]
    out[...] = exact_pass(
        scalars, True, (0,), (sources, None), (targets, None), None, tops, sums, ids, True
    )


def first_kernel(
    scalars, early, mass, sources, near, cross, targets, far, out, late_sources, *work
):
    late_sources[0:4] = near[...]
    late_sources[4:8] = cross[...]
    out[16:20, :] = mass[...]
    out[20:24, :] = jnp.zeros((4, out.shape[1]), jnp.float32)
    begun = early[...]
    shift = -jnp.max(begun, axis=(0, 1), keepdims=True)

    def write(late):
        out[0:16, :] = merge([begun, late])

    guarded_pass(
        scalars,
        True,
        (1, 2, 3),
        (sources, late_sources),
        (targets, far),
        None,
        shift,
        work,
        write,
    )


def columns_kernel(last_pass, *refs):
    scalars, sources, targets = refs[0], refs[1:3], refs[3:5]
    masses, target_mass, rest = refs[5:9], refs[9], refs[10:]
    parts, shift = masses, None
    if last_pass:
        parts, (shift, *rest) = rest[:4], rest[4:]
        shift = shift[0:1, 0:1]
    out, second, *work = rest
    rows = source_bias(masses, parts)
    if last_pass:
        for block in range(4):
            for half in range(2):
                second[2 * block + half : 2 * block + half + 1, :] = (
                    TO_POTENTIAL * rows[block : block + 1, 128 * half : 128 * (half + 1)]
                )
    else:
        second[...] = jnp.broadcast_to(middle([rows]), second.shape)
    out[12:16, :] = target_mass[0:4]

    def write(result):
        out[0:TARGET_SLOTS, :] = result

    guarded_pass(scalars, False, (0, 1, 2, 3), sources, targets, rows, shift, work, write)


def rows_kernel(*refs):
    scalars, sources, targets = refs[0], refs[1:3], refs[3:5]
    shift, columns, partner, *mirrors = refs[5:11]
    out, second, *work, scratch = refs[11:]
    rows = target_bias(scalars, columns, partner, mirrors, scratch)
    second[...] = jnp.broadcast_to(middle([rows[0:7], rows[8:12]]), second.shape)

    def write(result):
        out[...] = result

    guarded_pass(
        scalars, True, (0, 1, 2, 3), sources, targets, rows, shift[0:1, 0:1], work, write
    )


def forward_kernel(scalars, columns, partner, *outs):
    group = scalars[4, 0]
    for offset, out in enumerate(outs, 1):
        block = group ^ offset
        out[0:1, :] = columns[3 + offset : 4 + offset]
        out[1:2, :] = partner[3 + offset : 4 + offset]
        out[2:3, :] = merge([columns[pl.ds(block, 1), :], partner[pl.ds(FAR + block, 1), :]])
        out[3:4, :] = columns[pl.ds(12 + block, 1), :]


def finish_kernel(scalars, columns, partner, *rest):
    *mirrors, out, scratch = rest
    group = scalars[4, 0]
    scratch[...] = jnp.full(scratch.shape, very_low, jnp.float32)
    for offset, ref in enumerate(mirrors, 1):
        scratch[pl.ds(group ^ offset, 1), :] = ref[3 + offset : 4 + offset]
    rows = columns[12:16] - merge([columns[0:4], partner[8:12], scratch[0:4]])
    for block in range(4):
        for half in range(2):
            out[2 * block + half : 2 * block + half + 1, :] = (
                TO_POTENTIAL * rows[block : block + 1, 128 * half : 128 * (half + 1)]
            )


SMEM, VMEM = pltpu.SMEM, pltpu.VMEM


def call(kernel, inputs, outs, scratch=()):
    whole = pl.BlockSpec(memory_space=VMEM)
    return pl.pallas_call(
        kernel,
        out_shape=outs,
        in_specs=[pl.BlockSpec(memory_space=SMEM)] + [whole] * (len(inputs) - 1),
        out_specs=[whole] * len(outs),
        scratch_shapes=list(scratch),
        compiler_params=pltpu.CompilerParams(vmem_limit_bytes=32 << 20),
    )(*inputs)


def swap(values, axis, size, bit):
    return lax.ppermute(values, axis, [(index, index ^ bit) for index in range(size)])


def tile_lists(candidates, own_group, own_member, members, per_device, slot_count):
    owner = candidates // per_device
    local = candidates % per_device
    apart = (owner % members) ^ own_member
    last = candidates.shape[1] - 1
    mirror = (owner // members) ^ own_group
    is_last = jnp.arange(last + 1)[None, :] == last
    source = jnp.broadcast_to(
        jnp.arange(candidates.shape[0], dtype=jnp.int32)[:, None], candidates.shape
    )
    own_mirror = jnp.logical_and(is_last, source < per_device)
    near = jnp.logical_and(~is_last, apart == 0)
    far = jnp.logical_and(~is_last, apart == 4)
    late = source >= 2 * per_device
    target = jnp.where(jnp.logical_and(is_last, mirror > 0), 3 + mirror, local)
    members_of = (
        jnp.logical_or(jnp.logical_and(near, ~late), own_mirror),
        jnp.logical_and(near, late),
        jnp.logical_and(far, ~late),
        jnp.logical_and(far, late),
    )
    source, target = source.reshape(1, -1), target.reshape(1, -1)
    order = jnp.arange(source.shape[1], dtype=jnp.int32)
    before = order[None, :] < order[:, None]
    place = jnp.full(order.shape, -1, jnp.int32)
    for (first, _), taken in zip(SECTIONS, members_of):
        if first >= 12 and slot_count == 16:
            break
        taken = taken.reshape(-1)
        earlier = jnp.sum(jnp.logical_and(before, taken[None, :]).astype(jnp.int32), axis=1)
        place = jnp.where(taken, first + earlier, place)
    slots = jnp.arange(slot_count, dtype=jnp.int32)
    hits = place[None, :] == slots[:, None]
    used = jnp.any(hits, axis=1)
    sources = jnp.sum(jnp.where(hits, source, 0), axis=1)
    targets = jnp.sum(jnp.where(hits, target, 0), axis=1)
    late_slot = jnp.logical_or(jnp.logical_and(slots >= 12, slots < 20), slots >= 28)
    return jnp.stack(
        [
            jnp.where(jnp.logical_and(late_slot, used), sources - 8, sources),
            targets,
            jnp.where(used, sources, SOURCE_SLOTS),
            jnp.where(used, jnp.where(slots >= 20, FAR + targets, targets), TARGET_SLOTS),
            jnp.broadcast_to(own_group, slots.shape).astype(jnp.int32),
        ]
    )


def shards_quad(source_vectors, target_vectors, source_mass, target_mass, candidates):
    members = lax.axis_size("member")
    groups = lax.axis_size("group")
    own_group = lax.axis_index("group")
    own_member = lax.axis_index("member")
    per_device, cand_count = candidates.shape
    block_rows = source_vectors.shape[0] // per_device
    width = source_vectors.shape[1]
    blocked = (per_device, block_rows, width)
    member_swap = lambda values, bit: swap(values, "member", members, bit)
    group_swap = lambda values, bit: swap(values, "group", groups, bit)

    source_own = source_vectors.reshape(blocked)
    target_own = target_vectors.reshape(blocked)
    target_far = member_swap(target_own, 4)
    named = jnp.concatenate([candidates, member_swap(candidates, 1)])
    source_near = member_swap(source_own, 2)
    theirs = member_swap(named, 2)
    source_late, target_late, named = lax.optimization_barrier((source_own, target_own, named))
    mirrors = lax.all_to_all(target_late, "group", split_axis=0, concat_axis=0, tiled=True)
    source_core = member_swap(source_late, 1)
    place = (own_group, own_member, members, per_device)
    early_scalars = tile_lists(named, *place, 16)
    own_source_mass = LOG2E * source_mass.reshape(per_device, block_rows)
    own_mass = LOG2E * target_mass.reshape(per_device, block_rows)

    side = jax.ShapeDtypeStruct((16, block_rows), jnp.float32)
    flat = jax.ShapeDtypeStruct((8, 128), jnp.float32)
    stacked = lambda count: jax.ShapeDtypeStruct((count, block_rows, width), source_vectors.dtype)
    tile_rows = [VMEM((TILE_SLOTS, block_rows), kind) for kind in (jnp.float32, jnp.float32, jnp.int32)]
    pass_buffers = [
        VMEM((SOURCE_SLOTS + 1, 8, block_rows), jnp.float32),
        VMEM((24, block_rows), jnp.float32),
        *tile_rows,
        VMEM((SOURCE_SLOTS, block_rows, 128), jnp.float32),
    ]

    early, sources, targets = call(
        early_kernel,
        [early_scalars, source_own, source_core, target_own, mirrors],
        [side, stacked(8), stacked(7)],
        tile_rows,
    )
    source_near, theirs, early = lax.optimization_barrier((source_near, theirs, early))
    source_cross = member_swap(source_near, 1)
    scalars = tile_lists(jnp.concatenate([named, theirs]), *place, TILE_SLOTS)
    parts, late_sources = call(
        first_kernel,
        [
            scalars,
            early,
            own_source_mass,
            sources,
            source_near,
            source_cross,
            targets,
            target_far,
        ],
        [jax.ShapeDtypeStruct((24, block_rows), jnp.float32), stacked(8)],
        pass_buffers[:5],
    )
    blocks = [sources, late_sources, targets, target_far]
    masses, extra = [], []
    for step in range(ITERS):
        last_pass = step == ITERS - 1
        parts = [parts] + [member_swap(parts, bit) for bit in (1, 2, 3)]
        masses = masses or parts
        columns, potential = call(
            functools.partial(columns_kernel, last_pass),
            [scalars, *blocks, *masses, own_mass, *(parts + extra if last_pass else [])],
            [side, flat],
            pass_buffers,
        )
        partner = member_swap(columns, 4)
        if last_pass:
            break
        sent = call(
            forward_kernel,
            [scalars, columns, partner],
            [jax.ShapeDtypeStruct((4, block_rows), jnp.float32)] * 3,
        )
        received = [group_swap(values, bit) for bit, values in enumerate(sent, 1)]
        parts, shift = call(
            rows_kernel,
            [scalars, *blocks, potential, columns, partner, *received],
            [side, flat],
            [*pass_buffers, VMEM((8, block_rows), jnp.float32)],
        )
        extra = [shift]
    received = [group_swap(columns, bit) for bit in (1, 2, 3)]
    (final,) = call(
        finish_kernel,
        [scalars, columns, partner, *received],
        [flat],
        [VMEM((8, block_rows), jnp.float32)],
    )
    return potential.reshape(source_mass.shape), final.reshape(target_mass.shape)


def shards(source_vectors, target_vectors, source_mass, target_mass, candidates):
    quad = lax.axis_size("member") == 8 and lax.axis_size("group") == 4 and candidates.shape == (4, 8)
    plan = shards_quad if quad else shards_any
    return plan(source_vectors, target_vectors, source_mass, target_mass, candidates)


def solution(mesh):
    placed = (
        P(("group", "member"), None),
        P(("group", "member"), None),
        P(("group", "member")),
        P(("group", "member")),
        P(("group", "member"), None),
    )
    return jax.shard_map(
        shards,
        mesh=mesh,
        in_specs=placed,
        out_specs=(P(("group", "member")), P(("group", "member"))),
        check_vma=False,
    )
```

```python
import functools

import jax
import jax.numpy as jnp
from jax import lax
from jax.experimental import pallas as pl
from jax.experimental.pallas import tpu as pltpu
from jax.sharding import PartitionSpec as P

ITERS = 2


entropy_strength = 0.3
very_low = -1e30


def log_partition(values, axis):
    largest_score = jnp.max(values, axis=axis, keepdims=True)
    return jnp.squeeze(largest_score, axis) + jnp.log(
        jnp.sum(jnp.exp(values - largest_score), axis=axis)
    )


def slot_layout(lists, per_device, members, capacity):
    owner = lists // per_device
    partner = owner % members
    local_block = lists % per_device
    ordering = jnp.arange(lists.shape[-1], dtype=jnp.int32)
    matching = partner[..., :, None] == partner[..., None, :]
    earlier = ordering[None, :] < ordering[:, None]
    position = jnp.sum(jnp.logical_and(matching, earlier).astype(jnp.int32), axis=-1)
    return (partner * capacity + position, local_block)


def trade_member(values):
    return lax.all_to_all(values, "member", split_axis=0, concat_axis=0, tiled=True)


def trade_group(values):
    return lax.all_to_all(values, "group", split_axis=0, concat_axis=0, tiled=True)


def tile_terms(sources, target_blocks, picks, side, by_rows):
    tile_count, block_rows, width = sources.shape
    batch = 4
    grouped = (
        sources.reshape(tile_count // batch, batch, block_rows, width),
        picks.reshape(tile_count // batch, batch),
        side.reshape(tile_count // batch, batch, block_rows),
    )

    def visit(grouped_part):
        source_portion, pick_part, side_portion = grouped_part
        key_entries = jnp.take(target_blocks, pick_part, axis=0)
        score_matrix = jnp.einsum(
            "umk,ugk->umg", source_portion, key_entries, preferred_element_type=jnp.float32
        )
        if by_rows:
            return log_partition((score_matrix + side_portion[:, None, :]) / entropy_strength, 2)
        return log_partition((score_matrix + side_portion[:, :, None]) / entropy_strength, 1)

    return lax.map(visit, grouped).reshape(tile_count, block_rows)


def owner_update(slot_terms, mirror_terms, incoming, target_marginal):
    output_list = []
    for local_block in range(target_marginal.shape[0]):
        masked = jnp.where((incoming == local_block)[:, None], slot_terms, very_low)
        stacked = jnp.concatenate([masked, mirror_terms[local_block][None, :]], axis=0)
        output_list.append(log_partition(stacked, 0))
    return entropy_strength * target_marginal - entropy_strength * jnp.stack(output_list)


def shards_any(source_vectors, target_vectors, source_mass, target_mass, candidates):
    members = lax.axis_size("member")
    groups = lax.axis_size("group")
    own_member = lax.axis_index("member")
    source_count, cand_count = candidates.shape
    inside_count = cand_count - 1
    block_rows = source_vectors.shape[0] // source_count
    width = source_vectors.shape[1]
    target_count = target_vectors.shape[0] // block_rows
    capacity = (source_count * inside_count + members - 1) // members
    spots = members * capacity
    source_blocks = source_vectors.reshape(source_count, block_rows, width)
    target_blocks = target_vectors.reshape(target_count, block_rows, width)
    source_marginal = source_mass.reshape(source_count, block_rows)
    target_marginal = target_mass.reshape(target_count, block_rows)
    own_lists = candidates[:, :inside_count]
    own_spots, own_local = slot_layout(
        own_lists.reshape(1, source_count * inside_count), target_count, members, capacity
    )
    own_spots = own_spots[0]
    all_lists = lax.all_gather(own_lists, "member", axis=0, tiled=True)
    their_spots, their_local = slot_layout(
        all_lists.reshape(members, source_count * inside_count), target_count, members, capacity
    )
    wanted_spots = own_member * capacity + jnp.arange(capacity, dtype=jnp.int32)
    hits = their_spots[:, :, None] == wanted_spots[None, None, :]
    incoming = (jnp.sum(jnp.where(hits, their_local[:, :, None] + 1, 0), axis=1) - 1).reshape(spots)
    picks = jnp.maximum(incoming, 0)
    mirror_group = candidates[:, inside_count] // target_count // members
    spot_range = jnp.arange(spots, dtype=jnp.int32)
    group_range = jnp.arange(groups, dtype=jnp.int32)
    source_of = jnp.arange(source_count * inside_count, dtype=jnp.int32) // inside_count
    slot_index = jnp.sum(
        jnp.where(own_spots[:, None] == spot_range[None, :], source_of[:, None], 0), axis=0
    )
    mirror_index = jnp.sum(
        jnp.where(
            mirror_group[:, None] == group_range[None, :],
            jnp.arange(source_count, dtype=jnp.int32)[:, None],
            0,
        ),
        axis=0,
    )
    slot_payload = jnp.take(source_blocks, slot_index, axis=0)
    mirror_payload = jnp.take(source_blocks, mirror_index, axis=0)
    arrived = lax.all_to_all(
        slot_payload.reshape(members, capacity, block_rows, width),
        "member",
        split_axis=0,
        concat_axis=0,
        tiled=True,
    ).reshape(spots, block_rows, width)
    arrived_mirror = lax.all_to_all(
        mirror_payload, "group", split_axis=0, concat_axis=0, tiled=True
    )
    target_current = jnp.zeros((target_count, block_rows), jnp.float32)
    for step in range(ITERS):
        row_slots = tile_terms(
            arrived, target_blocks, picks, jnp.take(target_current, picks, axis=0), True
        )
        row_mirror = tile_terms(arrived_mirror, target_blocks, group_range, target_current, True)
        slot_back = trade_member(row_slots.reshape(members, capacity, block_rows)).reshape(
            spots, block_rows
        )
        mirror_back = trade_group(row_mirror)
        collected_rows = jnp.concatenate(
            [
                jnp.take(slot_back, own_spots, axis=0).reshape(
                    source_count, inside_count, block_rows
                ),
                jnp.take(mirror_back, mirror_group, axis=0)[:, None],
            ],
            axis=1,
        )
        source_current = entropy_strength * source_marginal - entropy_strength * log_partition(
            collected_rows, 1
        )
        slot_sides = trade_member(
            jnp.take(source_current, slot_index, axis=0).reshape(members, capacity, block_rows)
        ).reshape(spots, block_rows)
        mirror_sides = trade_group(jnp.take(source_current, mirror_index, axis=0))
        column_slots = tile_terms(arrived, target_blocks, picks, slot_sides, False)
        column_mirror = tile_terms(arrived_mirror, target_blocks, group_range, mirror_sides, False)
        target_current = owner_update(column_slots, column_mirror, incoming, target_marginal)
    return (
        source_current.reshape(source_count * block_rows),
        target_current.reshape(target_count * block_rows),
    )


LOG2E = 1.4426950408889634
TO_LOGIT = LOG2E / entropy_strength
TO_POTENTIAL = entropy_strength / LOG2E
SOURCE_SLOTS = 16
TARGET_SLOTS = 12
FAR = 8
CAPACITY = 4
SECTIONS = (
    (0, 0, 0),
    (1, 0, 4),
    (0, 2, 8),
    (2, 0, 12),
    (0, 1, 16),
    (1, 1, 20),
    (2, 1, 24),
    (3, 0, 28),
    (3, 1, 32),
)
EARLY, LATE = SECTIONS[:3], SECTIONS[3:]
LATE_SLOT = 12
TILE_SLOTS = 40
NO_SLOT = 36
GROUP_AT = 39
SMALL, LARGE, LARGEST = 2.0**-100, 2.0**100, 2.0**110


def merge(parts):
    top = functools.reduce(jnp.maximum, parts)
    return top + LOG2E * jnp.log(sum(jnp.exp2(part - top) for part in parts))


def swapped(rows, size):
    pieces = [rows[start : start + size] for start in range(0, rows.shape[0], size)]
    return jnp.concatenate([pieces[index ^ 1] for index in range(len(pieces))], axis=0)


def source_bias(mass_refs, part_refs):
    own, core, near, cross = (ref[0:16] for ref in part_refs)
    core = swapped(core, 4)
    near = swapped(near, 8)
    cross = swapped(swapped(cross, 4), 8)
    mass = jnp.concatenate([ref[16:20] for ref in mass_refs], axis=0)
    return mass - merge([own, core, near, cross])


def target_bias(scalars, columns, partner, mirrors, scratch):
    group = scalars[0, GROUP_AT]
    scratch[...] = jnp.full(scratch.shape, very_low, jnp.float32)
    for offset, ref in enumerate(mirrors, 1):
        scratch[pl.ds(group ^ offset, 1), :] = ref[0:1]
        scratch[pl.ds(4 + (group ^ offset), 1), :] = ref[1:2]
    own = columns[12:16] - merge([columns[0:4], partner[8:12], scratch[0:4]])
    far = partner[12:16] - merge([columns[8:12], partner[0:4], scratch[4:8]])
    across = [
        ref[3:4] - merge([ref[2:3], columns[3 + offset : 4 + offset]])
        for offset, ref in enumerate(mirrors, 1)
    ]
    blank = jnp.zeros((1, own.shape[1]), jnp.float32)
    return jnp.concatenate([own, *across, blank, far, *([blank] * 4)], axis=0)


def in_parts(rows):
    high = rows.astype(jnp.bfloat16)
    rest = rows - high.astype(jnp.float32)
    middle = rest.astype(jnp.bfloat16)
    low = (rest - middle.astype(jnp.float32)).astype(jnp.bfloat16)
    return jnp.concatenate([high, middle, low], axis=0)


def spread(rows, bias):
    count = rows.shape[0]
    shape = (3 * count, count * 128)
    slot = lax.broadcasted_iota(jnp.int32, shape, 0) & (count - 1)
    place = lax.broadcasted_iota(jnp.int32, shape, 1) >> 7
    chosen = jnp.where(slot == place, 1.0, 0.0).astype(jnp.bfloat16)
    turned = lax.dot_general(
        in_parts(rows), chosen, (((0,), (0,)), ((), ())), preferred_element_type=jnp.float32
    )
    for index in range(count):
        bias[index] = turned[:, 128 * index : 128 * (index + 1)]


def score(summed, kept):
    product = lax.dot_general(summed, kept, (((1,), (1,)), ((), ())), preferred_element_type=jnp.float32)
    return product * TO_LOGIT


def wide(values):
    return jnp.concatenate([values, values], axis=1)


def exact_pass(lists, by_rows, sections, sources, targets, tops, sums, ids):
    summed_row, kept_row = (1, 0) if by_rows else (0, 1)
    ids[...] = jnp.full(ids.shape, -1, jnp.int32)
    for source, target, first in sections:
        pair = (sources[source], targets[target])
        for slot in range(first, first + CAPACITY):
            blocks = [array[lists[row, slot]] for row, array in enumerate(pair)]
            exact_tile(lists, by_rows, slot, blocks, None, tops, sums, ids)
    return merge_tiles(by_rows, tops, sums, ids)


def exact_tile(lists, by_rows, slot, blocks, bias, tops, sums, ids):
    summed, kept = blocks[::-1] if by_rows else blocks
    logits = score(summed, kept)
    if bias is not None:
        count = bias.shape[0] - 1
        logits = logits + wide(bias[jnp.minimum(lists[3 if by_rows else 2, slot], count)])
    top = jnp.max(logits, axis=0, keepdims=True)
    tops[pl.ds(slot, 1), :] = top
    sums[pl.ds(slot, 1), :] = jnp.sum(jnp.exp2(logits - top), axis=0, keepdims=True)
    ids[pl.ds(slot, 1), :] = jnp.full((1, ids.shape[1]), lists[2 if by_rows else 3, slot], jnp.int32)


def merge_tiles(by_rows, tops, sums, ids):
    best, total = [], []
    for block in range(SOURCE_SLOTS if by_rows else TARGET_SLOTS):
        mine = ids[...] == block
        top = jnp.max(jnp.where(mine, tops[...], very_low), axis=0, keepdims=True)
        best.append(top)
        total.append(
            jnp.sum(jnp.where(mine, sums[...] * jnp.exp2(tops[...] - top), 0.0), axis=0, keepdims=True)
        )
    best = jnp.concatenate(best, axis=0)
    total = jnp.concatenate(total, axis=0)
    return jnp.where(total > 0, best + LOG2E * jnp.log(jnp.where(total > 0, total, 1.0)), very_low)


def exact_loop(lists, by_rows, first, sources, targets, bias, shift, work):
    tops, sums, ids, packed, semaphore = work
    for index, blocks in enumerate((*sources, *targets)):
        copy = pltpu.make_async_copy(blocks, packed.at[pl.ds(4 * index, 4)], semaphore)
        copy.start()
        copy.wait()
    ids[...] = jnp.full(ids.shape, -1, jnp.int32)

    def visit(slot, carry):
        blocks = packed[lists[4, slot]], packed[lists[5, slot]]
        exact_tile(lists, by_rows, slot, blocks, bias, tops, sums, ids)
        return carry

    lax.fori_loop(first, NO_SLOT, visit, 0)
    result = merge_tiles(by_rows, tops, sums, ids)
    return result if bias is None or shift is None else result - shift


def guarded_pass(lists, present, by_rows, sections, sources, targets, bias, shift, total, work, write):
    summed_row, kept_row = (1, 0) if by_rows else (0, 1)
    total[...] = jnp.zeros(total.shape, jnp.float32)
    for source, target, first in sections:
        pair = (sources[source], targets[target])
        summed, kept = pair[summed_row], pair[kept_row]
        for slot in range(first, first + CAPACITY):
            block = lists[summed_row, slot]
            logits = score(summed[block], kept[lists[kept_row, slot]])
            if bias is None:
                logits = logits + shift
            else:
                if not by_rows:
                    place = 4 * source + block
                elif target == 2:
                    place = lists[3, slot]
                else:
                    place = FAR * target + block
                logits = logits + wide(bias[place])
            terms = jnp.exp2(logits)
            place = lists[2 + kept_row, slot]
            total[place] = total[place] + jnp.sum(terms.reshape(-1, 8, terms.shape[1]), axis=0)
    count = SOURCE_SLOTS if by_rows else TARGET_SLOTS
    sums_of = jnp.concatenate(
        [jnp.sum(total[block], axis=0, keepdims=True) for block in range(count)], axis=0
    )
    here = wide(present[0:count]) > 0
    result = LOG2E * jnp.log(jnp.where(here, sums_of, 1.0))
    if shift is not None:
        result = result - shift
    write(jnp.where(here, result, very_low))
    fine = jnp.logical_and(sums_of > SMALL, sums_of < LARGE)
    worst = jnp.min(jnp.where(jnp.logical_or(fine, jnp.logical_not(here)), 1.0, 0.0))

    @pl.when(worst < 0.5)
    def _():
        write(exact_loop(lists, by_rows, sections[0][2], sources, targets, bias, shift, work))


def middle(pieces):
    top = functools.reduce(jnp.maximum, [jnp.max(piece, axis=(0, 1), keepdims=True) for piece in pieces])
    bottom = functools.reduce(jnp.minimum, [jnp.min(piece, axis=(0, 1), keepdims=True) for piece in pieces])
    return 0.5 * (top + bottom)


def early_kernel(lists, own, core, target, mirrors, out, reference, tops, sums, ids):
    result = exact_pass(lists, True, EARLY, (own, core), (target, None, mirrors), tops, sums, ids)
    out[...] = result
    largest = jnp.max(result, axis=(0, 1), keepdims=True)
    reference[...] = jnp.broadcast_to(-largest, reference.shape)


def first_kernel(lists, present, *refs):
    sources, targets = refs[0:4], refs[4:7]
    reference, early, mass, out, total, *work = refs[7:]
    out[16:20, :] = mass[...]
    out[20:24, :] = jnp.zeros((4, out.shape[1]), jnp.float32)

    def write(result):
        out[0:16, :] = merge([early[...], result])

    guarded_pass(
        lists, present, True, LATE, sources, targets, None, reference[0:1, 0:1], total, work, write
    )


def columns_kernel(last_pass, lists, present, *refs):
    sources, targets = refs[0:4], refs[4:7]
    masses, target_mass, rest = refs[7:11], refs[11], refs[12:]
    parts, shift = masses, None
    if last_pass:
        parts, (shift, *rest) = rest[:4], rest[4:]
        shift = shift[0:1, 0:1]
    out, second, bias, total, *work = rest
    rows = source_bias(masses, parts)
    spread(rows + shift if last_pass else rows, bias)
    if last_pass:
        for block in range(4):
            for half in range(2):
                second[2 * block + half : 2 * block + half + 1, :] = (
                    TO_POTENTIAL * rows[block : block + 1, 128 * half : 128 * (half + 1)]
                )
    else:
        second[...] = jnp.broadcast_to(middle([rows]), second.shape)
    out[12:16, :] = target_mass[0:4]

    def write(result):
        out[0:TARGET_SLOTS, :] = result

    guarded_pass(
        lists, present, False, SECTIONS, sources, targets, bias, shift, total, work, write
    )


def rows_kernel(lists, present, *refs):
    sources, targets = refs[0:4], refs[4:7]
    shift, columns, partner, *mirrors = refs[7:13]
    out, second, bias, total, *work, scratch = refs[13:]
    rows = target_bias(lists, columns, partner, mirrors, scratch)
    shift = shift[0:1, 0:1]
    spread(rows + shift, bias)
    second[...] = jnp.broadcast_to(middle([rows[0:7], rows[8:12]]), second.shape)

    def write(result):
        out[...] = result

    guarded_pass(lists, present, True, SECTIONS, sources, targets, bias, shift, total, work, write)


def forward_kernel(scalars, columns, partner, *outs):
    group = scalars[0, GROUP_AT]
    for offset, out in enumerate(outs, 1):
        block = group ^ offset
        out[0:1, :] = columns[3 + offset : 4 + offset]
        out[1:2, :] = partner[3 + offset : 4 + offset]
        out[2:3, :] = merge([columns[pl.ds(block, 1), :], partner[pl.ds(FAR + block, 1), :]])
        out[3:4, :] = columns[pl.ds(12 + block, 1), :]


def finish_kernel(scalars, columns, partner, *rest):
    *mirrors, out, scratch = rest
    group = scalars[0, GROUP_AT]
    scratch[...] = jnp.full(scratch.shape, very_low, jnp.float32)
    for offset, ref in enumerate(mirrors, 1):
        scratch[pl.ds(group ^ offset, 1), :] = ref[3 + offset : 4 + offset]
    rows = columns[12:16] - merge([columns[0:4], partner[8:12], scratch[0:4]])
    for block in range(4):
        for half in range(2):
            out[2 * block + half : 2 * block + half + 1, :] = (
                TO_POTENTIAL * rows[block : block + 1, 128 * half : 128 * (half + 1)]
            )


SMEM, VMEM = pltpu.SMEM, pltpu.VMEM


def call(kernel, inputs, outs, scratch=()):
    whole = pl.BlockSpec(memory_space=VMEM)
    scalar = pl.BlockSpec(memory_space=SMEM)
    return pl.pallas_call(
        kernel,
        out_shape=outs,
        in_specs=[scalar] + [whole] * (len(inputs) - 1),
        out_specs=[whole] * len(outs),
        scratch_shapes=list(scratch),
        compiler_params=pltpu.CompilerParams(vmem_limit_bytes=16 << 20),
    )(*inputs)


def swap(values, axis, size, bit):
    return lax.ppermute(values, axis, [(index, index ^ bit) for index in range(size)])


def tile_lists(table, group, member):
    count = table.shape[1]
    row = jnp.arange(table.shape[0], dtype=jnp.int32)[:, None]
    source = row >> 2
    pick = jnp.arange(count, dtype=jnp.int32)[None, :]
    is_last = pick == count - 1
    apart = ((table >> 2) & 7) ^ member
    far = jnp.logical_and(~is_last, apart == 4)
    other = table >> 5
    starts = {(source, target): first for source, target, first in SECTIONS}

    def first_of(target):
        return functools.reduce(
            lambda value, index: jnp.where(source == index, starts[index, target], value),
            range(1, 4),
            jnp.full(source.shape, starts[0, target], jnp.int32),
        )

    section = jnp.where(apart == 0, first_of(0), jnp.where(apart == 4, first_of(1), -1))
    section = jnp.where(is_last, jnp.where(source == 0, starts[0, 2], -1), section)
    local = table & 3
    block = jnp.where(is_last, other, local)
    slot = jnp.where(is_last, jnp.where(other == group, local, 3 + (other ^ group)), local)
    slot = slot + jnp.where(far, FAR, 0)
    array = jnp.where(is_last, 6, jnp.where(far, 5, 4))
    code = (row & 3) + 4 * block + 16 * row + 512 * slot + 16384 * (4 * array + block)
    section, code = section.reshape(-1), code.reshape(-1)
    order = jnp.arange(section.shape[0], dtype=jnp.int32)
    earlier = jnp.logical_and(order[None, :] < order[:, None], section[None, :] == section[:, None])
    place = jnp.where(section >= 0, section + jnp.sum(earlier.astype(jnp.int32), axis=1), -1)
    slots = jnp.arange(TILE_SLOTS, dtype=jnp.int32)
    hits = place[None, :] == slots[:, None]
    found = jnp.sum(jnp.where(hits, code[None, :] + 1, 0), axis=1)
    found = jnp.where(found > 0, found - 1, SOURCE_SLOTS * 16 + TARGET_SLOTS * 512 + 16 * 16384)
    source_slots, target_slots = (found >> 4) & 31, (found >> 9) & 31
    blocks = jnp.minimum(source_slots, SOURCE_SLOTS - 1), found >> 14
    lists = jnp.stack(
        [
            jnp.where(slots == GROUP_AT, group, found & 3),
            (found >> 2) & 3,
            source_slots,
            target_slots,
            *blocks,
        ]
    )
    late_slots = jnp.where(slots >= LATE_SLOT, source_slots, SOURCE_SLOTS)
    rows = jnp.arange(16, dtype=jnp.int32)
    present = [
        jnp.broadcast_to(
            jnp.any(taken[None, :] == rows[:, None], axis=1).astype(jnp.float32)[:, None], (16, 128)
        )
        for taken in (source_slots, target_slots, late_slots)
    ]
    return lists, *present


def shards_quad(source_vectors, target_vectors, source_mass, target_mass, candidates):
    members = lax.axis_size("member")
    groups = lax.axis_size("group")
    own_group = lax.axis_index("group")
    own_member = lax.axis_index("member")
    per_device, cand_count = candidates.shape
    block_rows = source_vectors.shape[0] // per_device
    width = source_vectors.shape[1]
    blocked = (per_device, block_rows, width)
    member_swap = lambda values, bit: swap(values, "member", members, bit)
    group_swap = lambda values, bit: swap(values, "group", groups, bit)

    source_own = source_vectors.reshape(blocked)
    target_own = target_vectors.reshape(blocked)
    target_far = member_swap(target_own, 4)
    source_near = member_swap(source_own, 2)
    named = jnp.concatenate([candidates, member_swap(candidates, 2)])
    source_late, target_late, named = lax.optimization_barrier((source_own, target_own, named))
    source_core = member_swap(source_late, 1)
    named_core = member_swap(named, 1)
    mirrors = lax.all_to_all(target_late, "group", split_axis=0, concat_axis=0, tiled=True)
    lists, has_source, has_target, has_late = tile_lists(
        jnp.concatenate([named[0:4], named_core[0:4], named[4:8], named_core[4:8]]),
        own_group.astype(jnp.int32),
        own_member.astype(jnp.int32),
    )
    own_source_mass = LOG2E * source_mass.reshape(per_device, block_rows)
    own_mass = LOG2E * target_mass.reshape(per_device, block_rows)

    side = jax.ShapeDtypeStruct((16, block_rows), jnp.float32)
    flat = jax.ShapeDtypeStruct((8, 128), jnp.float32)
    tile_rows = [VMEM((TILE_SLOTS, block_rows), kind) for kind in (jnp.float32, jnp.float32, jnp.int32)]
    pass_buffers = [
        VMEM((SOURCE_SLOTS + 1, 8, block_rows), jnp.float32),
        *tile_rows,
        VMEM((28, block_rows, width), source_vectors.dtype),
        pltpu.SemaphoreType.DMA,
    ]
    bias_buffer = VMEM((SOURCE_SLOTS, block_rows, 128), jnp.float32)

    early, reference = call(
        early_kernel, [lists, source_own, source_core, target_own, mirrors], [side, flat], tile_rows
    )
    source_near, early = lax.optimization_barrier((source_near, early))
    source_cross = member_swap(source_near, 1)
    blocks = [source_own, source_core, source_near, source_cross, target_own, target_far, mirrors]
    (parts,) = call(
        first_kernel,
        [lists, has_late, *blocks, reference, early, own_source_mass],
        [jax.ShapeDtypeStruct((24, block_rows), jnp.float32)],
        pass_buffers,
    )
    masses, extra = [], []
    for step in range(ITERS):
        last_pass = step == ITERS - 1
        parts = [parts] + [member_swap(parts, bit) for bit in (1, 2, 3)]
        masses = masses or parts
        columns, potential = call(
            functools.partial(columns_kernel, last_pass),
            [lists, has_target, *blocks, *masses, own_mass, *(parts + extra if last_pass else [])],
            [side, flat],
            [bias_buffer, *pass_buffers],
        )
        partner = member_swap(columns, 4)
        if last_pass:
            break
        sent = call(
            forward_kernel,
            [lists, columns, partner],
            [jax.ShapeDtypeStruct((4, block_rows), jnp.float32)] * 3,
        )
        received = [group_swap(values, bit) for bit, values in enumerate(sent, 1)]
        parts, shift = call(
            rows_kernel,
            [lists, has_source, *blocks, potential, columns, partner, *received],
            [side, flat],
            [bias_buffer, *pass_buffers, VMEM((8, block_rows), jnp.float32)],
        )
        extra = [shift]
    received = [group_swap(columns, bit) for bit in (1, 2, 3)]
    (final,) = call(
        finish_kernel,
        [lists, columns, partner, *received],
        [flat],
        [VMEM((8, block_rows), jnp.float32)],
    )
    return potential.reshape(source_mass.shape), final.reshape(target_mass.shape)


def shards(source_vectors, target_vectors, source_mass, target_mass, candidates):
    quad = lax.axis_size("member") == 8 and lax.axis_size("group") == 4 and candidates.shape == (4, 8)
    plan = shards_quad if quad else shards_any
    return plan(source_vectors, target_vectors, source_mass, target_mass, candidates)


def solution(mesh):
    placed = (
        P(("group", "member"), None),
        P(("group", "member"), None),
        P(("group", "member")),
        P(("group", "member")),
        P(("group", "member"), None),
    )
    return jax.shard_map(
        shards,
        mesh=mesh,
        in_specs=placed,
        out_specs=(P(("group", "member")), P(("group", "member"))),
        check_vma=False,
    )
```

```python
import functools

import jax
import jax.numpy as jnp
from jax import lax
from jax.experimental import pallas as pl
from jax.experimental.pallas import tpu as pltpu
from jax.sharding import PartitionSpec as P

ITERS = 2


entropy_strength = 0.3
very_low = -1e30


def log_partition(values, axis):
    largest_score = jnp.max(values, axis=axis, keepdims=True)
    return jnp.squeeze(largest_score, axis) + jnp.log(
        jnp.sum(jnp.exp(values - largest_score), axis=axis)
    )


def slot_layout(lists, per_device, members, capacity):
    owner = lists // per_device
    partner = owner % members
    local_block = lists % per_device
    ordering = jnp.arange(lists.shape[-1], dtype=jnp.int32)
    matching = partner[..., :, None] == partner[..., None, :]
    earlier = ordering[None, :] < ordering[:, None]
    position = jnp.sum(jnp.logical_and(matching, earlier).astype(jnp.int32), axis=-1)
    return (partner * capacity + position, local_block)


def trade_member(values):
    return lax.all_to_all(values, "member", split_axis=0, concat_axis=0, tiled=True)


def trade_group(values):
    return lax.all_to_all(values, "group", split_axis=0, concat_axis=0, tiled=True)


def tile_terms(sources, target_blocks, picks, side, by_rows):
    tile_count, block_rows, width = sources.shape
    batch = 4
    grouped = (
        sources.reshape(tile_count // batch, batch, block_rows, width),
        picks.reshape(tile_count // batch, batch),
        side.reshape(tile_count // batch, batch, block_rows),
    )

    def visit(grouped_part):
        source_portion, pick_part, side_portion = grouped_part
        key_entries = jnp.take(target_blocks, pick_part, axis=0)
        score_matrix = jnp.einsum(
            "umk,ugk->umg", source_portion, key_entries, preferred_element_type=jnp.float32
        )
        if by_rows:
            return log_partition((score_matrix + side_portion[:, None, :]) / entropy_strength, 2)
        return log_partition((score_matrix + side_portion[:, :, None]) / entropy_strength, 1)

    return lax.map(visit, grouped).reshape(tile_count, block_rows)


def owner_update(slot_terms, mirror_terms, incoming, target_marginal):
    output_list = []
    for local_block in range(target_marginal.shape[0]):
        masked = jnp.where((incoming == local_block)[:, None], slot_terms, very_low)
        stacked = jnp.concatenate([masked, mirror_terms[local_block][None, :]], axis=0)
        output_list.append(log_partition(stacked, 0))
    return entropy_strength * target_marginal - entropy_strength * jnp.stack(output_list)


def shards_any(source_vectors, target_vectors, source_mass, target_mass, candidates):
    members = lax.axis_size("member")
    groups = lax.axis_size("group")
    own_member = lax.axis_index("member")
    source_count, cand_count = candidates.shape
    inside_count = cand_count - 1
    block_rows = source_vectors.shape[0] // source_count
    width = source_vectors.shape[1]
    target_count = target_vectors.shape[0] // block_rows
    capacity = (source_count * inside_count + members - 1) // members
    spots = members * capacity
    source_blocks = source_vectors.reshape(source_count, block_rows, width)
    target_blocks = target_vectors.reshape(target_count, block_rows, width)
    source_marginal = source_mass.reshape(source_count, block_rows)
    target_marginal = target_mass.reshape(target_count, block_rows)
    own_lists = candidates[:, :inside_count]
    own_spots, own_local = slot_layout(
        own_lists.reshape(1, source_count * inside_count), target_count, members, capacity
    )
    own_spots = own_spots[0]
    all_lists = lax.all_gather(own_lists, "member", axis=0, tiled=True)
    their_spots, their_local = slot_layout(
        all_lists.reshape(members, source_count * inside_count), target_count, members, capacity
    )
    wanted_spots = own_member * capacity + jnp.arange(capacity, dtype=jnp.int32)
    hits = their_spots[:, :, None] == wanted_spots[None, None, :]
    incoming = (jnp.sum(jnp.where(hits, their_local[:, :, None] + 1, 0), axis=1) - 1).reshape(spots)
    picks = jnp.maximum(incoming, 0)
    mirror_group = candidates[:, inside_count] // target_count // members
    spot_range = jnp.arange(spots, dtype=jnp.int32)
    group_range = jnp.arange(groups, dtype=jnp.int32)
    source_of = jnp.arange(source_count * inside_count, dtype=jnp.int32) // inside_count
    slot_index = jnp.sum(
        jnp.where(own_spots[:, None] == spot_range[None, :], source_of[:, None], 0), axis=0
    )
    mirror_index = jnp.sum(
        jnp.where(
            mirror_group[:, None] == group_range[None, :],
            jnp.arange(source_count, dtype=jnp.int32)[:, None],
            0,
        ),
        axis=0,
    )
    slot_payload = jnp.take(source_blocks, slot_index, axis=0)
    mirror_payload = jnp.take(source_blocks, mirror_index, axis=0)
    arrived = lax.all_to_all(
        slot_payload.reshape(members, capacity, block_rows, width),
        "member",
        split_axis=0,
        concat_axis=0,
        tiled=True,
    ).reshape(spots, block_rows, width)
    arrived_mirror = lax.all_to_all(
        mirror_payload, "group", split_axis=0, concat_axis=0, tiled=True
    )
    target_current = jnp.zeros((target_count, block_rows), jnp.float32)
    for step in range(ITERS):
        row_slots = tile_terms(
            arrived, target_blocks, picks, jnp.take(target_current, picks, axis=0), True
        )
        row_mirror = tile_terms(arrived_mirror, target_blocks, group_range, target_current, True)
        slot_back = trade_member(row_slots.reshape(members, capacity, block_rows)).reshape(
            spots, block_rows
        )
        mirror_back = trade_group(row_mirror)
        collected_rows = jnp.concatenate(
            [
                jnp.take(slot_back, own_spots, axis=0).reshape(
                    source_count, inside_count, block_rows
                ),
                jnp.take(mirror_back, mirror_group, axis=0)[:, None],
            ],
            axis=1,
        )
        source_current = entropy_strength * source_marginal - entropy_strength * log_partition(
            collected_rows, 1
        )
        slot_sides = trade_member(
            jnp.take(source_current, slot_index, axis=0).reshape(members, capacity, block_rows)
        ).reshape(spots, block_rows)
        mirror_sides = trade_group(jnp.take(source_current, mirror_index, axis=0))
        column_slots = tile_terms(arrived, target_blocks, picks, slot_sides, False)
        column_mirror = tile_terms(arrived_mirror, target_blocks, group_range, mirror_sides, False)
        target_current = owner_update(column_slots, column_mirror, incoming, target_marginal)
    return (
        source_current.reshape(source_count * block_rows),
        target_current.reshape(target_count * block_rows),
    )


LOG2E = 1.4426950408889634
TO_LOGIT = LOG2E / entropy_strength
TO_POTENTIAL = entropy_strength / LOG2E
SOURCE_SLOTS = 16
TARGET_SLOTS = 12
FAR = 8
CAPACITY = 4
SECTIONS = (
    (0, 0, 0),
    (1, 0, 4),
    (0, 2, 8),
    (2, 0, 12),
    (0, 1, 16),
    (1, 1, 20),
    (2, 1, 24),
    (3, 0, 28),
    (3, 1, 32),
)
EARLY, LATE = SECTIONS[:3], SECTIONS[3:]
LATE_SLOT = 12
TILE_SLOTS = 40
NO_SLOT = 36
GROUP_AT = 39
SMALL, LARGE, LARGEST = 2.0**-100, 2.0**100, 2.0**110


def merge(parts):
    top = functools.reduce(jnp.maximum, parts)
    return top + LOG2E * jnp.log(sum(jnp.exp2(part - top) for part in parts))


def swapped(rows, size):
    pieces = [rows[start : start + size] for start in range(0, rows.shape[0], size)]
    return jnp.concatenate([pieces[index ^ 1] for index in range(len(pieces))], axis=0)


def source_bias(mass_refs, part_refs):
    own, core, near, cross = (ref[0:16] for ref in part_refs)
    core = swapped(core, 4)
    near = swapped(near, 8)
    cross = swapped(swapped(cross, 4), 8)
    mass = jnp.concatenate([ref[16:20] for ref in mass_refs], axis=0)
    return mass - merge([own, core, near, cross])


def target_bias(scalars, columns, partner, mirrors, scratch):
    group = scalars[0, GROUP_AT]
    scratch[...] = jnp.full(scratch.shape, very_low, jnp.float32)
    for offset, ref in enumerate(mirrors, 1):
        scratch[pl.ds(group ^ offset, 1), :] = ref[0:1]
        scratch[pl.ds(4 + (group ^ offset), 1), :] = ref[1:2]
    own = columns[12:16] - merge([columns[0:4], partner[8:12], scratch[0:4]])
    far = partner[12:16] - merge([columns[8:12], partner[0:4], scratch[4:8]])
    across = [
        ref[3:4] - merge([ref[2:3], columns[3 + offset : 4 + offset]])
        for offset, ref in enumerate(mirrors, 1)
    ]
    blank = jnp.zeros((1, own.shape[1]), jnp.float32)
    return jnp.concatenate([own, *across, blank, far, *([blank] * 4)], axis=0)


def in_parts(rows):
    high = rows.astype(jnp.bfloat16)
    rest = rows - high.astype(jnp.float32)
    middle = rest.astype(jnp.bfloat16)
    low = (rest - middle.astype(jnp.float32)).astype(jnp.bfloat16)
    return jnp.concatenate([high, middle, low], axis=0)


def spread(rows, bias):
    count = rows.shape[0]
    shape = (3 * count, count * 128)
    slot = lax.broadcasted_iota(jnp.int32, shape, 0) & (count - 1)
    place = lax.broadcasted_iota(jnp.int32, shape, 1) >> 7
    chosen = jnp.where(slot == place, 1.0, 0.0).astype(jnp.bfloat16)
    turned = lax.dot_general(
        in_parts(rows), chosen, (((0,), (0,)), ((), ())), preferred_element_type=jnp.float32
    )
    for index in range(count):
        bias[index] = turned[:, 128 * index : 128 * (index + 1)]


def score(summed, kept):
    product = lax.dot_general(summed, kept, (((1,), (1,)), ((), ())), preferred_element_type=jnp.float32)
    return product * TO_LOGIT


def wide(values):
    return jnp.concatenate([values, values], axis=1)


def exact_pass(lists, by_rows, sections, sources, targets, tops, sums, ids):
    summed_row, kept_row = (1, 0) if by_rows else (0, 1)
    ids[...] = jnp.full(ids.shape, -1, jnp.int32)
    for source, target, first in sections:
        pair = (sources[source], targets[target])
        for slot in range(first, first + CAPACITY):
            blocks = [array[lists[row, slot]] for row, array in enumerate(pair)]
            exact_tile(lists, by_rows, slot, blocks, None, tops, sums, ids)
    return merge_tiles(by_rows, tops, sums, ids)


def exact_tile(lists, by_rows, slot, blocks, bias, tops, sums, ids):
    summed, kept = blocks[::-1] if by_rows else blocks
    logits = score(summed, kept)
    if bias is not None:
        count = bias.shape[0] - 1
        logits = logits + wide(bias[jnp.minimum(lists[3 if by_rows else 2, slot], count)])
    top = jnp.max(logits, axis=0, keepdims=True)
    tops[pl.ds(slot, 1), :] = top
    sums[pl.ds(slot, 1), :] = jnp.sum(jnp.exp2(logits - top), axis=0, keepdims=True)
    ids[pl.ds(slot, 1), :] = jnp.full((1, ids.shape[1]), lists[2 if by_rows else 3, slot], jnp.int32)


def merge_tiles(by_rows, tops, sums, ids):
    best, total = [], []
    for block in range(SOURCE_SLOTS if by_rows else TARGET_SLOTS):
        mine = ids[...] == block
        top = jnp.max(jnp.where(mine, tops[...], very_low), axis=0, keepdims=True)
        best.append(top)
        total.append(
            jnp.sum(jnp.where(mine, sums[...] * jnp.exp2(tops[...] - top), 0.0), axis=0, keepdims=True)
        )
    best = jnp.concatenate(best, axis=0)
    total = jnp.concatenate(total, axis=0)
    return jnp.where(total > 0, best + LOG2E * jnp.log(jnp.where(total > 0, total, 1.0)), very_low)


def exact_loop(lists, by_rows, first, sources, targets, bias, shift, work):
    tops, sums, ids, packed, semaphore = work
    for index, blocks in enumerate((*sources, *targets)):
        copy = pltpu.make_async_copy(blocks, packed.at[pl.ds(4 * index, 4)], semaphore)
        copy.start()
        copy.wait()
    ids[...] = jnp.full(ids.shape, -1, jnp.int32)

    def visit(slot, carry):
        blocks = packed[lists[4, slot]], packed[lists[5, slot]]
        exact_tile(lists, by_rows, slot, blocks, bias, tops, sums, ids)
        return carry

    lax.fori_loop(first, NO_SLOT, visit, 0)
    result = merge_tiles(by_rows, tops, sums, ids)
    return result if bias is None or shift is None else result - shift


def guarded_pass(lists, present, by_rows, sections, sources, targets, bias, shift, total, work, write):
    summed_row, kept_row = (1, 0) if by_rows else (0, 1)
    total[...] = jnp.zeros(total.shape, jnp.float32)
    for source, target, first in sections:
        pair = (sources[source], targets[target])
        summed, kept = pair[summed_row], pair[kept_row]
        for slot in range(first, first + CAPACITY):
            block = lists[summed_row, slot]
            logits = score(summed[block], kept[lists[kept_row, slot]])
            if bias is None:
                logits = logits + shift
            else:
                if not by_rows:
                    place = 4 * source + block
                elif target == 2:
                    place = lists[3, slot]
                else:
                    place = FAR * target + block
                logits = logits + wide(bias[place])
            terms = jnp.exp2(logits)
            place = lists[2 + kept_row, slot]
            total[place] = total[place] + jnp.sum(terms.reshape(-1, 8, terms.shape[1]), axis=0)
    count = SOURCE_SLOTS if by_rows else TARGET_SLOTS
    sums_of = jnp.concatenate(
        [jnp.sum(total[block], axis=0, keepdims=True) for block in range(count)], axis=0
    )
    here = wide(present[0:count]) > 0
    result = LOG2E * jnp.log(jnp.where(here, sums_of, 1.0))
    if shift is not None:
        result = result - shift
    write(jnp.where(here, result, very_low))
    fine = jnp.logical_and(sums_of > SMALL, sums_of < LARGE)
    worst = jnp.min(jnp.where(jnp.logical_or(fine, jnp.logical_not(here)), 1.0, 0.0))

    @pl.when(worst < 0.5)
    def _():
        write(exact_loop(lists, by_rows, sections[0][2], sources, targets, bias, shift, work))


def middle(pieces):
    top = functools.reduce(jnp.maximum, [jnp.max(piece, axis=(0, 1), keepdims=True) for piece in pieces])
    bottom = functools.reduce(jnp.minimum, [jnp.min(piece, axis=(0, 1), keepdims=True) for piece in pieces])
    return 0.5 * (top + bottom)


def early_kernel(lists, own, core, target, mirrors, out, reference, tops, sums, ids):
    result = exact_pass(lists, True, EARLY, (own, core), (target, None, mirrors), tops, sums, ids)
    out[...] = result
    largest = jnp.max(result, axis=(0, 1), keepdims=True)
    reference[...] = jnp.broadcast_to(-largest, reference.shape)


def first_kernel(lists, present, cross, *refs):
    near_sources, targets = refs[0:3], refs[3:6]
    reference, early, mass, out, far_source, total, *work = refs[6:]
    far_source[...] = cross[...]
    out[16:20, :] = mass[...]
    out[20:24, :] = jnp.zeros((4, out.shape[1]), jnp.float32)

    def write(result):
        out[0:16, :] = merge([early[...], result])

    guarded_pass(
        lists,
        present,
        True,
        LATE,
        (*near_sources, cross),
        targets,
        None,
        reference[0:1, 0:1],
        total,
        work,
        write,
    )


def columns_kernel(last_pass, lists, present, *refs):
    sources, targets = refs[0:4], refs[4:7]
    masses, target_mass, rest = refs[7:11], refs[11], refs[12:]
    parts, shift = masses, None
    if last_pass:
        parts, (shift, *rest) = rest[:4], rest[4:]
        shift = shift[0:1, 0:1]
    out, second, bias, total, *work = rest
    rows = source_bias(masses, parts)
    spread(rows + shift if last_pass else rows, bias)
    if last_pass:
        for block in range(4):
            for half in range(2):
                second[2 * block + half : 2 * block + half + 1, :] = (
                    rows[block : block + 1, 128 * half : 128 * (half + 1)]
                )
    else:
        second[...] = jnp.broadcast_to(middle([rows]), second.shape)
    out[12:16, :] = target_mass[0:4]

    def write(result):
        out[0:TARGET_SLOTS, :] = result

    guarded_pass(
        lists, present, False, SECTIONS, sources, targets, bias, shift, total, work, write
    )


def rows_kernel(lists, present, *refs):
    sources, targets = refs[0:4], refs[4:7]
    shift, columns, partner, *mirrors = refs[7:13]
    out, second, bias, total, *work, scratch = refs[13:]
    rows = target_bias(lists, columns, partner, mirrors, scratch)
    shift = shift[0:1, 0:1]
    spread(rows + shift, bias)
    second[...] = jnp.broadcast_to(middle([rows[0:7], rows[8:12]]), second.shape)

    def write(result):
        out[...] = result

    guarded_pass(lists, present, True, SECTIONS, sources, targets, bias, shift, total, work, write)


def forward_kernel(scalars, columns, partner, *outs):
    group = scalars[0, GROUP_AT]
    for offset, out in enumerate(outs, 1):
        block = group ^ offset
        out[0:1, :] = columns[3 + offset : 4 + offset]
        out[1:2, :] = partner[3 + offset : 4 + offset]
        out[2:3, :] = merge([columns[pl.ds(block, 1), :], partner[pl.ds(FAR + block, 1), :]])
        out[3:4, :] = columns[pl.ds(12 + block, 1), :]


def finish_kernel(scalars, columns, partner, *rest):
    *mirrors, out, scratch = rest
    group = scalars[0, GROUP_AT]
    scratch[...] = jnp.full(scratch.shape, very_low, jnp.float32)
    for offset, ref in enumerate(mirrors, 1):
        scratch[pl.ds(group ^ offset, 1), :] = ref[3 + offset : 4 + offset]
    rows = columns[12:16] - merge([columns[0:4], partner[8:12], scratch[0:4]])
    for block in range(4):
        for half in range(2):
            out[2 * block + half : 2 * block + half + 1, :] = (
                TO_POTENTIAL * rows[block : block + 1, 128 * half : 128 * (half + 1)]
            )


SMEM, VMEM = pltpu.SMEM, pltpu.VMEM


def call(kernel, inputs, outs, scratch=()):
    whole = pl.BlockSpec(memory_space=VMEM)
    return pl.pallas_call(
        kernel,
        out_shape=outs,
        in_specs=[pl.BlockSpec(memory_space=SMEM)] + [whole] * (len(inputs) - 1),
        out_specs=[whole] * len(outs),
        scratch_shapes=list(scratch),
        compiler_params=pltpu.CompilerParams(vmem_limit_bytes=16 << 20),
    )(*inputs)


def swap(values, axis, size, bit):
    return lax.ppermute(values, axis, [(index, index ^ bit) for index in range(size)])


def tile_lists(table, group, member):
    count = table.shape[1]
    row = jnp.arange(table.shape[0], dtype=jnp.int32)[:, None]
    source = row >> 2
    pick = jnp.arange(count, dtype=jnp.int32)[None, :]
    is_last = pick == count - 1
    apart = ((table >> 2) & 7) ^ member
    far = jnp.logical_and(~is_last, apart == 4)
    other = table >> 5
    starts = {(source, target): first for source, target, first in SECTIONS}

    def first_of(target):
        return functools.reduce(
            lambda value, index: jnp.where(source == index, starts[index, target], value),
            range(1, 4),
            jnp.full(source.shape, starts[0, target], jnp.int32),
        )

    section = jnp.where(apart == 0, first_of(0), jnp.where(apart == 4, first_of(1), -1))
    section = jnp.where(is_last, jnp.where(source == 0, starts[0, 2], -1), section)
    local = table & 3
    block = jnp.where(is_last, other, local)
    slot = jnp.where(is_last, jnp.where(other == group, local, 3 + (other ^ group)), local)
    slot = slot + jnp.where(far, FAR, 0)
    array = jnp.where(is_last, 6, jnp.where(far, 5, 4))
    code = (row & 3) + 4 * block + 16 * row + 512 * slot + 16384 * (4 * array + block)
    section, code = section.reshape(-1), code.reshape(-1)
    order = jnp.arange(section.shape[0], dtype=jnp.int32)
    earlier = jnp.logical_and(order[None, :] < order[:, None], section[None, :] == section[:, None])
    place = jnp.where(section >= 0, section + jnp.sum(earlier.astype(jnp.int32), axis=1), -1)
    slots = jnp.arange(TILE_SLOTS, dtype=jnp.int32)
    hits = place[None, :] == slots[:, None]
    found = jnp.sum(jnp.where(hits, code[None, :] + 1, 0), axis=1)
    found = jnp.where(found > 0, found - 1, SOURCE_SLOTS * 16 + TARGET_SLOTS * 512 + 16 * 16384)
    source_slots, target_slots = (found >> 4) & 31, (found >> 9) & 31
    blocks = jnp.minimum(source_slots, SOURCE_SLOTS - 1), found >> 14
    lists = jnp.stack(
        [
            jnp.where(slots == GROUP_AT, group, found & 3),
            (found >> 2) & 3,
            source_slots,
            target_slots,
            *blocks,
        ]
    )
    late_slots = jnp.where(slots >= LATE_SLOT, source_slots, SOURCE_SLOTS)
    rows = jnp.arange(16, dtype=jnp.int32)
    present = [
        jnp.broadcast_to(
            jnp.any(taken[None, :] == rows[:, None], axis=1).astype(jnp.float32)[:, None], (16, 128)
        )
        for taken in (source_slots, target_slots, late_slots)
    ]
    return lists, *present


def shards_quad(source_vectors, target_vectors, source_mass, target_mass, candidates):
    members = lax.axis_size("member")
    groups = lax.axis_size("group")
    own_group = lax.axis_index("group")
    own_member = lax.axis_index("member")
    per_device, cand_count = candidates.shape
    block_rows = source_vectors.shape[0] // per_device
    width = source_vectors.shape[1]
    blocked = (per_device, block_rows, width)
    member_swap = lambda values, bit: swap(values, "member", members, bit)
    group_swap = lambda values, bit: swap(values, "group", groups, bit)

    source_own = source_vectors.reshape(blocked)
    target_own = target_vectors.reshape(blocked)
    target_far = member_swap(target_own, 4)
    source_near = member_swap(source_own, 2)
    named = jnp.concatenate([candidates, member_swap(candidates, 2)])
    source_late, target_late, named = lax.optimization_barrier((source_own, target_own, named))
    source_core = member_swap(source_late, 1)
    named_core = member_swap(named, 1)
    mirrors = lax.all_to_all(target_late, "group", split_axis=0, concat_axis=0, tiled=True)
    lists, has_source, has_target, has_late = tile_lists(
        jnp.concatenate([named[0:4], named_core[0:4], named[4:8], named_core[4:8]]),
        own_group.astype(jnp.int32),
        own_member.astype(jnp.int32),
    )
    own_source_mass = LOG2E * source_mass.reshape(per_device, block_rows)
    own_mass = LOG2E * target_mass.reshape(per_device, block_rows)

    side = jax.ShapeDtypeStruct((16, block_rows), jnp.float32)
    flat = jax.ShapeDtypeStruct((8, 128), jnp.float32)
    tile_rows = [VMEM((TILE_SLOTS, block_rows), kind) for kind in (jnp.float32, jnp.float32, jnp.int32)]
    pass_buffers = [
        VMEM((SOURCE_SLOTS + 1, 8, block_rows), jnp.float32),
        *tile_rows,
        VMEM((28, block_rows, width), source_vectors.dtype),
        pltpu.SemaphoreType.DMA,
    ]
    bias_buffer = VMEM((SOURCE_SLOTS, block_rows, 128), jnp.float32)

    early, reference = call(
        early_kernel, [lists, source_own, source_core, target_own, mirrors], [side, flat], tile_rows
    )
    source_near, early = lax.optimization_barrier((source_near, early))
    source_cross = member_swap(source_near, 1)
    sources, targets = [source_own, source_core, source_near], [target_own, target_far, mirrors]
    parts, source_cross = call(
        first_kernel,
        [lists, has_late, source_cross, *sources, *targets, reference, early, own_source_mass],
        [
            jax.ShapeDtypeStruct((24, block_rows), jnp.float32),
            jax.ShapeDtypeStruct(blocked, source_vectors.dtype),
        ],
        pass_buffers,
    )
    blocks = [*sources, source_cross, *targets]
    masses, extra = [], []
    for step in range(ITERS):
        last_pass = step == ITERS - 1
        parts = [parts] + [member_swap(parts, bit) for bit in (1, 2, 3)]
        masses = masses or parts
        columns, potential = call(
            functools.partial(columns_kernel, last_pass),
            [lists, has_target, *blocks, *masses, own_mass, *(parts + extra if last_pass else [])],
            [side, flat],
            [bias_buffer, *pass_buffers],
        )
        partner = member_swap(columns, 4)
        if last_pass:
            break
        sent = call(
            forward_kernel,
            [lists, columns, partner],
            [jax.ShapeDtypeStruct((4, block_rows), jnp.float32)] * 3,
        )
        received = [group_swap(values, bit) for bit, values in enumerate(sent, 1)]
        parts, shift = call(
            rows_kernel,
            [lists, has_source, *blocks, potential, columns, partner, *received],
            [side, flat],
            [bias_buffer, *pass_buffers, VMEM((8, block_rows), jnp.float32)],
        )
        extra = [shift]
    received = [group_swap(columns, bit) for bit in (1, 2, 3)]
    (final,) = call(
        finish_kernel,
        [lists, columns, partner, *received],
        [flat],
        [VMEM((8, block_rows), jnp.float32)],
    )
    return (TO_POTENTIAL * potential).reshape(source_mass.shape), final.reshape(target_mass.shape)


def shards(source_vectors, target_vectors, source_mass, target_mass, candidates):
    quad = lax.axis_size("member") == 8 and lax.axis_size("group") == 4 and candidates.shape == (4, 8)
    plan = shards_quad if quad else shards_any
    return plan(source_vectors, target_vectors, source_mass, target_mass, candidates)


def solution(mesh):
    placed = (
        P(("group", "member"), None),
        P(("group", "member"), None),
        P(("group", "member")),
        P(("group", "member")),
        P(("group", "member"), None),
    )
    return jax.shard_map(
        shards,
        mesh=mesh,
        in_specs=placed,
        out_specs=(P(("group", "member")), P(("group", "member"))),
        check_vma=False,
    )
```

```python
import functools

import jax
import jax.numpy as jnp
from jax import lax
from jax.experimental import pallas as pl
from jax.experimental.pallas import tpu as pltpu
from jax.sharding import PartitionSpec as P

ITERS = 2


entropy_strength = 0.3
very_low = -1e30


def log_partition(values, axis):
    largest_score = jnp.max(values, axis=axis, keepdims=True)
    return jnp.squeeze(largest_score, axis) + jnp.log(
        jnp.sum(jnp.exp(values - largest_score), axis=axis)
    )


def slot_layout(lists, per_device, members, capacity):
    owner = lists // per_device
    partner = owner % members
    local_block = lists % per_device
    ordering = jnp.arange(lists.shape[-1], dtype=jnp.int32)
    matching = partner[..., :, None] == partner[..., None, :]
    earlier = ordering[None, :] < ordering[:, None]
    position = jnp.sum(jnp.logical_and(matching, earlier).astype(jnp.int32), axis=-1)
    return (partner * capacity + position, local_block)


def trade_member(values):
    return lax.all_to_all(values, "member", split_axis=0, concat_axis=0, tiled=True)


def trade_group(values):
    return lax.all_to_all(values, "group", split_axis=0, concat_axis=0, tiled=True)


def tile_terms(sources, target_blocks, picks, side, by_rows):
    tile_count, block_rows, width = sources.shape
    batch = 4
    grouped = (
        sources.reshape(tile_count // batch, batch, block_rows, width),
        picks.reshape(tile_count // batch, batch),
        side.reshape(tile_count // batch, batch, block_rows),
    )

    def visit(grouped_part):
        source_portion, pick_part, side_portion = grouped_part
        key_entries = jnp.take(target_blocks, pick_part, axis=0)
        score_matrix = jnp.einsum(
            "umk,ugk->umg", source_portion, key_entries, preferred_element_type=jnp.float32
        )
        if by_rows:
            return log_partition((score_matrix + side_portion[:, None, :]) / entropy_strength, 2)
        return log_partition((score_matrix + side_portion[:, :, None]) / entropy_strength, 1)

    return lax.map(visit, grouped).reshape(tile_count, block_rows)


def owner_update(slot_terms, mirror_terms, incoming, target_marginal):
    output_list = []
    for local_block in range(target_marginal.shape[0]):
        masked = jnp.where((incoming == local_block)[:, None], slot_terms, very_low)
        stacked = jnp.concatenate([masked, mirror_terms[local_block][None, :]], axis=0)
        output_list.append(log_partition(stacked, 0))
    return entropy_strength * target_marginal - entropy_strength * jnp.stack(output_list)


def shards_any(source_vectors, target_vectors, source_mass, target_mass, candidates):
    members = lax.axis_size("member")
    groups = lax.axis_size("group")
    own_member = lax.axis_index("member")
    source_count, cand_count = candidates.shape
    inside_count = cand_count - 1
    block_rows = source_vectors.shape[0] // source_count
    width = source_vectors.shape[1]
    target_count = target_vectors.shape[0] // block_rows
    capacity = (source_count * inside_count + members - 1) // members
    spots = members * capacity
    source_blocks = source_vectors.reshape(source_count, block_rows, width)
    target_blocks = target_vectors.reshape(target_count, block_rows, width)
    source_marginal = source_mass.reshape(source_count, block_rows)
    target_marginal = target_mass.reshape(target_count, block_rows)
    own_lists = candidates[:, :inside_count]
    own_spots, own_local = slot_layout(
        own_lists.reshape(1, source_count * inside_count), target_count, members, capacity
    )
    own_spots = own_spots[0]
    all_lists = lax.all_gather(own_lists, "member", axis=0, tiled=True)
    their_spots, their_local = slot_layout(
        all_lists.reshape(members, source_count * inside_count), target_count, members, capacity
    )
    wanted_spots = own_member * capacity + jnp.arange(capacity, dtype=jnp.int32)
    hits = their_spots[:, :, None] == wanted_spots[None, None, :]
    incoming = (jnp.sum(jnp.where(hits, their_local[:, :, None] + 1, 0), axis=1) - 1).reshape(spots)
    picks = jnp.maximum(incoming, 0)
    mirror_group = candidates[:, inside_count] // target_count // members
    spot_range = jnp.arange(spots, dtype=jnp.int32)
    group_range = jnp.arange(groups, dtype=jnp.int32)
    source_of = jnp.arange(source_count * inside_count, dtype=jnp.int32) // inside_count
    slot_index = jnp.sum(
        jnp.where(own_spots[:, None] == spot_range[None, :], source_of[:, None], 0), axis=0
    )
    mirror_index = jnp.sum(
        jnp.where(
            mirror_group[:, None] == group_range[None, :],
            jnp.arange(source_count, dtype=jnp.int32)[:, None],
            0,
        ),
        axis=0,
    )
    slot_payload = jnp.take(source_blocks, slot_index, axis=0)
    mirror_payload = jnp.take(source_blocks, mirror_index, axis=0)
    arrived = lax.all_to_all(
        slot_payload.reshape(members, capacity, block_rows, width),
        "member",
        split_axis=0,
        concat_axis=0,
        tiled=True,
    ).reshape(spots, block_rows, width)
    arrived_mirror = lax.all_to_all(
        mirror_payload, "group", split_axis=0, concat_axis=0, tiled=True
    )
    target_current = jnp.zeros((target_count, block_rows), jnp.float32)
    for step in range(ITERS):
        row_slots = tile_terms(
            arrived, target_blocks, picks, jnp.take(target_current, picks, axis=0), True
        )
        row_mirror = tile_terms(arrived_mirror, target_blocks, group_range, target_current, True)
        slot_back = trade_member(row_slots.reshape(members, capacity, block_rows)).reshape(
            spots, block_rows
        )
        mirror_back = trade_group(row_mirror)
        collected_rows = jnp.concatenate(
            [
                jnp.take(slot_back, own_spots, axis=0).reshape(
                    source_count, inside_count, block_rows
                ),
                jnp.take(mirror_back, mirror_group, axis=0)[:, None],
            ],
            axis=1,
        )
        source_current = entropy_strength * source_marginal - entropy_strength * log_partition(
            collected_rows, 1
        )
        slot_sides = trade_member(
            jnp.take(source_current, slot_index, axis=0).reshape(members, capacity, block_rows)
        ).reshape(spots, block_rows)
        mirror_sides = trade_group(jnp.take(source_current, mirror_index, axis=0))
        column_slots = tile_terms(arrived, target_blocks, picks, slot_sides, False)
        column_mirror = tile_terms(arrived_mirror, target_blocks, group_range, mirror_sides, False)
        target_current = owner_update(column_slots, column_mirror, incoming, target_marginal)
    return (
        source_current.reshape(source_count * block_rows),
        target_current.reshape(target_count * block_rows),
    )


LOG2E = 1.4426950408889634
TO_LOGIT = LOG2E / entropy_strength
TO_POTENTIAL = entropy_strength / LOG2E
SOURCE_SLOTS = 16
TARGET_SLOTS = 12
FAR = 8
CAPACITY = 4
SECTIONS = (
    (0, 0, 0),
    (1, 0, 4),
    (0, 2, 8),
    (2, 0, 12),
    (0, 1, 16),
    (1, 1, 20),
    (2, 1, 24),
    (3, 0, 28),
    (3, 1, 32),
)
EARLY, LATE = SECTIONS[:3], SECTIONS[3:]
LATE_SLOT = 12
TILE_SLOTS = 40
NO_SLOT = 36
GROUP_AT = 39
SMALL, LARGE, LARGEST = 2.0**-100, 2.0**100, 2.0**110


def merge(parts):
    top = functools.reduce(jnp.maximum, parts)
    return top + LOG2E * jnp.log(sum(jnp.exp2(part - top) for part in parts))


def swapped(rows, size):
    pieces = [rows[start : start + size] for start in range(0, rows.shape[0], size)]
    return jnp.concatenate([pieces[index ^ 1] for index in range(len(pieces))], axis=0)


def source_bias(mass_refs, part_refs):
    own, core, near, cross = (ref[0:16] for ref in part_refs)
    core = swapped(core, 4)
    near = swapped(near, 8)
    cross = swapped(swapped(cross, 4), 8)
    mass = jnp.concatenate([ref[16:20] for ref in mass_refs], axis=0)
    return mass - merge([own, core, near, cross])


def target_bias(chosen, columns, partner, mirrors):
    own_across = far_across = jnp.full((4, columns.shape[1]), very_low, jnp.float32)
    for offset, ref in enumerate(mirrors, 1):
        picked = chosen[8 * offset - 8 : 8 * offset - 4] > 0
        own_across = jnp.where(picked, ref[0:1], own_across)
        far_across = jnp.where(picked, ref[1:2], far_across)
    own = columns[12:16] - merge([columns[0:4], partner[8:12], own_across])
    far = partner[12:16] - merge([columns[8:12], partner[0:4], far_across])
    across = [
        ref[3:4] - merge([ref[2:3], columns[3 + offset : 4 + offset]])
        for offset, ref in enumerate(mirrors, 1)
    ]
    blank = jnp.zeros((1, own.shape[1]), jnp.float32)
    return jnp.concatenate([own, *across, blank, far, *([blank] * 4)], axis=0)


def in_parts(rows):
    high = rows.astype(jnp.bfloat16)
    rest = rows - high.astype(jnp.float32)
    middle = rest.astype(jnp.bfloat16)
    low = (rest - middle.astype(jnp.float32)).astype(jnp.bfloat16)
    return jnp.concatenate([high, middle, low], axis=0)


def spread(rows, bias):
    count = rows.shape[0]
    shape = (3 * count, count * 128)
    slot = lax.broadcasted_iota(jnp.int32, shape, 0) & (count - 1)
    place = lax.broadcasted_iota(jnp.int32, shape, 1) >> 7
    chosen = jnp.where(slot == place, 1.0, 0.0).astype(jnp.bfloat16)
    turned = lax.dot_general(
        in_parts(rows), chosen, (((0,), (0,)), ((), ())), preferred_element_type=jnp.float32
    )
    for index in range(count):
        bias[index] = turned[:, 128 * index : 128 * (index + 1)]


def score(summed, kept):
    product = lax.dot_general(summed, kept, (((1,), (1,)), ((), ())), preferred_element_type=jnp.float32)
    return product * TO_LOGIT


def wide(values):
    return jnp.concatenate([values, values], axis=1)


def exact_pass(lists, by_rows, sections, sources, targets, tops, sums, ids):
    summed_row, kept_row = (1, 0) if by_rows else (0, 1)
    ids[...] = jnp.full(ids.shape, -1, jnp.int32)
    for source, target, first in sections:
        pair = (sources[source], targets[target])
        for slot in range(first, first + CAPACITY):
            blocks = [array[lists[row, slot]] for row, array in enumerate(pair)]
            exact_tile(lists, by_rows, slot, blocks, None, tops, sums, ids)
    return merge_tiles(by_rows, tops, sums, ids)


def exact_tile(lists, by_rows, slot, blocks, bias, tops, sums, ids):
    summed, kept = blocks[::-1] if by_rows else blocks
    logits = score(summed, kept)
    if bias is not None:
        count = bias.shape[0] - 1
        logits = logits + wide(bias[jnp.minimum(lists[3 if by_rows else 2, slot], count)])
    top = jnp.max(logits, axis=0, keepdims=True)
    tops[pl.ds(slot, 1), :] = top
    sums[pl.ds(slot, 1), :] = jnp.sum(jnp.exp2(logits - top), axis=0, keepdims=True)
    ids[pl.ds(slot, 1), :] = jnp.full((1, ids.shape[1]), lists[2 if by_rows else 3, slot], jnp.int32)


def merge_tiles(by_rows, tops, sums, ids):
    best, total = [], []
    for block in range(SOURCE_SLOTS if by_rows else TARGET_SLOTS):
        mine = ids[...] == block
        top = jnp.max(jnp.where(mine, tops[...], very_low), axis=0, keepdims=True)
        best.append(top)
        total.append(
            jnp.sum(jnp.where(mine, sums[...] * jnp.exp2(tops[...] - top), 0.0), axis=0, keepdims=True)
        )
    best = jnp.concatenate(best, axis=0)
    total = jnp.concatenate(total, axis=0)
    return jnp.where(total > 0, best + LOG2E * jnp.log(jnp.where(total > 0, total, 1.0)), very_low)


def exact_loop(lists, by_rows, first, sources, targets, bias, shift, work):
    tops, sums, ids, packed, semaphore = work
    for index, blocks in enumerate((*sources, *targets)):
        copy = pltpu.make_async_copy(blocks, packed.at[pl.ds(4 * index, 4)], semaphore)
        copy.start()
        copy.wait()
    ids[...] = jnp.full(ids.shape, -1, jnp.int32)

    def visit(slot, carry):
        blocks = packed[lists[4, slot]], packed[lists[5, slot]]
        exact_tile(lists, by_rows, slot, blocks, bias, tops, sums, ids)
        return carry

    lax.fori_loop(first, NO_SLOT, visit, 0)
    result = merge_tiles(by_rows, tops, sums, ids)
    return result if bias is None or shift is None else result - shift


def guarded_pass(lists, present, by_rows, sections, sources, targets, bias, shift, total, work, write):
    summed_row, kept_row = (1, 0) if by_rows else (0, 1)
    total[...] = jnp.zeros(total.shape, jnp.float32)
    for source, target, first in sections:
        pair = (sources[source], targets[target])
        summed, kept = pair[summed_row], pair[kept_row]
        for slot in range(first, first + CAPACITY):
            block = lists[summed_row, slot]
            logits = score(summed[block], kept[lists[kept_row, slot]])
            if bias is None:
                logits = logits + shift
            else:
                if not by_rows:
                    place = 4 * source + block
                elif target == 2:
                    place = lists[3, slot]
                else:
                    place = FAR * target + block
                logits = logits + wide(bias[place])
            terms = jnp.exp2(logits)
            place = lists[2 + kept_row, slot]
            total[place] = total[place] + jnp.sum(terms.reshape(-1, 8, terms.shape[1]), axis=0)
    count = SOURCE_SLOTS if by_rows else TARGET_SLOTS
    sums_of = jnp.concatenate(
        [jnp.sum(total[block], axis=0, keepdims=True) for block in range(count)], axis=0
    )
    here = wide(present[0:count]) > 0
    result = LOG2E * jnp.log(jnp.where(here, sums_of, 1.0))
    if shift is not None:
        result = result - shift
    write(jnp.where(here, result, very_low))
    fine = jnp.logical_and(sums_of > SMALL, sums_of < LARGE)
    worst = jnp.min(jnp.where(jnp.logical_or(fine, jnp.logical_not(here)), 1.0, 0.0))

    @pl.when(worst < 0.5)
    def _():
        write(exact_loop(lists, by_rows, sections[0][2], sources, targets, bias, shift, work))


def middle(pieces):
    top = functools.reduce(jnp.maximum, [jnp.max(piece, axis=(0, 1), keepdims=True) for piece in pieces])
    bottom = functools.reduce(jnp.minimum, [jnp.min(piece, axis=(0, 1), keepdims=True) for piece in pieces])
    return 0.5 * (top + bottom)


def early_kernel(lists, wait, own, core, target, mirrors, out, reference, tops, sums, ids):
    wait()
    result = exact_pass(lists, True, EARLY, (own, core), (target, None, mirrors), tops, sums, ids)
    out[...] = result
    largest = jnp.max(result, axis=(0, 1), keepdims=True)
    reference[...] = jnp.broadcast_to(-largest, reference.shape)


def first_kernel(lists, wait, present, cross, *refs):
    near_sources, targets = refs[0:3], refs[3:6]
    reference, early, mass, out, far_source, total, *work = refs[6:]
    far_source[...] = cross[...]
    out[16:20, :] = mass[...]
    out[20:24, :] = jnp.zeros((4, out.shape[1]), jnp.float32)

    def write(result):
        out[0:16, :] = merge([early[...], result])

    wait()
    guarded_pass(
        lists,
        present,
        True,
        LATE,
        (*near_sources, cross),
        targets,
        None,
        reference[0:1, 0:1],
        total,
        work,
        write,
    )


def columns_kernel(last_pass, lists, wait, present, *refs):
    sources, targets = refs[0:4], refs[4:7]
    masses, target_mass, rest = refs[7:11], refs[11], refs[12:]
    parts, shift = masses, None
    if last_pass:
        parts, (shift, *rest) = rest[:4], rest[4:]
        shift = shift[0:1, 0:1]
    out, second, bias, total, *work = rest
    rows = source_bias(masses, parts)
    spread(rows + shift if last_pass else rows, bias)
    if last_pass:
        for block in range(4):
            for half in range(2):
                second[2 * block + half : 2 * block + half + 1, :] = (
                    rows[block : block + 1, 128 * half : 128 * (half + 1)]
                )
    else:
        second[...] = jnp.broadcast_to(middle([rows]), second.shape)
    out[12:16, :] = target_mass[0:4]

    def write(result):
        out[0:TARGET_SLOTS, :] = result

    wait()
    guarded_pass(
        lists, present, False, SECTIONS, sources, targets, bias, shift, total, work, write
    )


def rows_kernel(lists, wait, present, *refs):
    sources, targets = refs[0:4], refs[4:7]
    chosen, shift, columns, partner, *mirrors = refs[7:14]
    out, second, bias, total, *work = refs[14:]
    rows = target_bias(chosen, columns, partner, mirrors)
    shift = shift[0:1, 0:1]
    spread(rows + shift, bias)
    second[...] = jnp.broadcast_to(middle([rows[0:7], rows[8:12]]), second.shape)

    def write(result):
        out[...] = result

    wait()
    guarded_pass(lists, present, True, SECTIONS, sources, targets, bias, shift, total, work, write)


def forward_kernel(chosen, columns, partner, *outs):
    totals = merge([columns[0:4], partner[8:12]])
    masses = columns[12:16]
    for offset, out in enumerate(outs, 1):
        picked = chosen[8 * offset - 8 : 8 * offset - 4] > 0
        out[0:1, :] = columns[3 + offset : 4 + offset]
        out[1:2, :] = partner[3 + offset : 4 + offset]
        out[2:3, :] = jnp.sum(jnp.where(picked, totals, 0.0), axis=0, keepdims=True)
        out[3:4, :] = jnp.sum(jnp.where(picked, masses, 0.0), axis=0, keepdims=True)


def finish_kernel(chosen, columns, partner, *rest):
    *mirrors, out = rest
    across = jnp.full((4, columns.shape[1]), very_low, jnp.float32)
    for offset, ref in enumerate(mirrors, 1):
        picked = chosen[8 * offset - 8 : 8 * offset - 4] > 0
        across = jnp.where(picked, ref[3 + offset : 4 + offset], across)
    rows = columns[12:16] - merge([columns[0:4], partner[8:12], across])
    for block in range(4):
        for half in range(2):
            out[2 * block + half : 2 * block + half + 1, :] = (
                TO_POTENTIAL * rows[block : block + 1, 128 * half : 128 * (half + 1)]
            )


SMEM, VMEM = pltpu.SMEM, pltpu.VMEM


def call(kernel, inputs, outs, scratch=(), scalar=True):
    whole = pl.BlockSpec(memory_space=VMEM)
    first = pl.BlockSpec(memory_space=SMEM) if scalar and inputs[0].dtype == jnp.int32 else whole
    return pl.pallas_call(
        kernel,
        out_shape=outs,
        in_specs=[first] + [whole] * (len(inputs) - 1),
        out_specs=[whole] * len(outs),
        scratch_shapes=list(scratch),
        compiler_params=pltpu.CompilerParams(vmem_limit_bytes=16 << 20),
    )(*inputs)


def call_tiles(kernel, lists, inputs, outs, scratch=(), early=True):
    def body(origin, *refs):
        *refs, scalars, semaphore = refs
        copy = pltpu.make_async_copy(origin, scalars, semaphore)
        copy.start()
        kernel(scalars, copy.wait, *refs)

    def plain(scalars, *refs):
        kernel(scalars, lambda: None, *refs)

    if early:
        return call(plain, [lists, *inputs], outs, scratch)
    extra = [SMEM(lists.shape, lists.dtype), pltpu.SemaphoreType.DMA]
    return call(body, [lists, *inputs], outs, [*scratch, *extra], False)


def swap(values, axis, size, bit):
    return lax.ppermute(values, axis, [(index, index ^ bit) for index in range(size)])


def tile_lists(table, group, member):
    count = table.shape[1]
    row = jnp.arange(table.shape[0], dtype=jnp.int32)[:, None]
    source = row >> 2
    pick = jnp.arange(count, dtype=jnp.int32)[None, :]
    is_last = pick == count - 1
    apart = ((table >> 2) & 7) ^ member
    far = jnp.logical_and(~is_last, apart == 4)
    other = table >> 5
    starts = {(source, target): first for source, target, first in SECTIONS}

    def first_of(target):
        return functools.reduce(
            lambda value, index: jnp.where(source == index, starts[index, target], value),
            range(1, 4),
            jnp.full(source.shape, starts[0, target], jnp.int32),
        )

    section = jnp.where(apart == 0, first_of(0), jnp.where(apart == 4, first_of(1), -1))
    section = jnp.where(is_last, jnp.where(source == 0, starts[0, 2], -1), section)
    local = table & 3
    block = jnp.where(is_last, other, local)
    slot = jnp.where(is_last, jnp.where(other == group, local, 3 + (other ^ group)), local)
    slot = slot + jnp.where(far, FAR, 0)
    array = jnp.where(is_last, 6, jnp.where(far, 5, 4))
    code = (row & 3) + 4 * block + 16 * row + 512 * slot + 16384 * (4 * array + block)
    section, code = section.reshape(-1), code.reshape(-1)
    order = jnp.arange(section.shape[0], dtype=jnp.int32)
    earlier = jnp.logical_and(order[None, :] < order[:, None], section[None, :] == section[:, None])
    place = jnp.where(section >= 0, section + jnp.sum(earlier.astype(jnp.int32), axis=1), -1)
    slots = jnp.arange(TILE_SLOTS, dtype=jnp.int32)
    hits = place[None, :] == slots[:, None]
    found = jnp.sum(jnp.where(hits, code[None, :] + 1, 0), axis=1)
    found = jnp.where(found > 0, found - 1, SOURCE_SLOTS * 16 + TARGET_SLOTS * 512 + 16 * 16384)
    source_slots, target_slots = (found >> 4) & 31, (found >> 9) & 31
    blocks = jnp.minimum(source_slots, SOURCE_SLOTS - 1), found >> 14
    lists = jnp.stack(
        [
            jnp.where(slots == GROUP_AT, group, found & 3),
            (found >> 2) & 3,
            source_slots,
            target_slots,
            *blocks,
        ]
    )
    late_slots = jnp.where(slots >= LATE_SLOT, source_slots, SOURCE_SLOTS)
    rows = jnp.arange(16, dtype=jnp.int32)
    present = [
        jnp.broadcast_to(
            jnp.any(taken[None, :] == rows[:, None], axis=1).astype(jnp.float32)[:, None], (16, 128)
        )
        for taken in (source_slots, target_slots, late_slots)
    ]
    return lists, *present


def shards_quad(source_vectors, target_vectors, source_mass, target_mass, candidates):
    members = lax.axis_size("member")
    groups = lax.axis_size("group")
    own_group = lax.axis_index("group")
    own_member = lax.axis_index("member")
    per_device, cand_count = candidates.shape
    block_rows = source_vectors.shape[0] // per_device
    width = source_vectors.shape[1]
    blocked = (per_device, block_rows, width)
    member_swap = lambda values, bit: swap(values, "member", members, bit)
    group_swap = lambda values, bit: swap(values, "group", groups, bit)

    source_own = source_vectors.reshape(blocked)
    target_own = target_vectors.reshape(blocked)
    target_far = member_swap(target_own, 4)
    source_near = member_swap(source_own, 2)
    named = jnp.concatenate([candidates, member_swap(candidates, 2)])
    source_late, target_late, named = lax.optimization_barrier((source_own, target_own, named))
    source_core = member_swap(source_late, 1)
    named_core = member_swap(named, 1)
    mirrors = lax.all_to_all(target_late, "group", split_axis=0, concat_axis=0, tiled=True)
    lists, has_source, has_target, has_late = tile_lists(
        jnp.concatenate([named[0:4], named_core[0:4], named[4:8], named_core[4:8]]),
        own_group.astype(jnp.int32),
        own_member.astype(jnp.int32),
    )
    own_source_mass = LOG2E * source_mass.reshape(per_device, block_rows)
    marked = jnp.arange(24, dtype=jnp.int32)
    marked = (marked & 7) == (own_group.astype(jnp.int32) ^ ((marked >> 3) + 1))
    chosen = jnp.broadcast_to(marked.astype(jnp.float32)[:, None], (24, block_rows))
    own_mass = LOG2E * target_mass.reshape(per_device, block_rows)

    side = jax.ShapeDtypeStruct((16, block_rows), jnp.float32)
    flat = jax.ShapeDtypeStruct((8, 128), jnp.float32)
    tile_rows = [VMEM((TILE_SLOTS, block_rows), kind) for kind in (jnp.float32, jnp.float32, jnp.int32)]
    pass_buffers = [
        VMEM((SOURCE_SLOTS + 1, 8, block_rows), jnp.float32),
        *tile_rows,
        VMEM((28, block_rows, width), source_vectors.dtype),
        pltpu.SemaphoreType.DMA,
    ]
    bias_buffer = VMEM((SOURCE_SLOTS, block_rows, 128), jnp.float32)

    early, reference = call_tiles(
        early_kernel, lists, [source_own, source_core, target_own, mirrors], [side, flat], tile_rows
    )
    source_near, early = lax.optimization_barrier((source_near, early))
    source_cross = member_swap(source_near, 1)
    sources, targets = [source_own, source_core, source_near], [target_own, target_far, mirrors]
    parts, source_cross = call_tiles(
        first_kernel,
        lists,
        [has_late, source_cross, *sources, *targets, reference, early, own_source_mass],
        [
            jax.ShapeDtypeStruct((24, block_rows), jnp.float32),
            jax.ShapeDtypeStruct(blocked, source_vectors.dtype),
        ],
        pass_buffers,
    )
    blocks = [*sources, source_cross, *targets]
    masses, extra = [], []
    for step in range(ITERS):
        last_pass = step == ITERS - 1
        parts = [parts] + [member_swap(parts, bit) for bit in (1, 2, 3)]
        masses = masses or parts
        columns, potential = call_tiles(
            functools.partial(columns_kernel, last_pass),
            lists,
            [has_target, *blocks, *masses, own_mass, *(parts + extra if last_pass else [])],
            [side, flat],
            [bias_buffer, *pass_buffers],
            early=not last_pass,
        )
        partner = member_swap(columns, 4)
        if last_pass:
            break
        sent = call(
            forward_kernel,
            [chosen, columns, partner],
            [jax.ShapeDtypeStruct((4, block_rows), jnp.float32)] * 3,
        )
        received = [group_swap(values, bit) for bit, values in enumerate(sent, 1)]
        parts, shift = call_tiles(
            rows_kernel,
            lists,
            [has_source, *blocks, chosen, potential, columns, partner, *received],
            [side, flat],
            [bias_buffer, *pass_buffers],
            early=False,
        )
        extra = [shift]
    received = [group_swap(columns, bit) for bit in (1, 2, 3)]
    (final,) = call(
        finish_kernel,
        [chosen, columns, partner, *received],
        [flat],
    )
    return (TO_POTENTIAL * potential).reshape(source_mass.shape), final.reshape(target_mass.shape)


def shards(source_vectors, target_vectors, source_mass, target_mass, candidates):
    quad = lax.axis_size("member") == 8 and lax.axis_size("group") == 4 and candidates.shape == (4, 8)
    plan = shards_quad if quad else shards_any
    return plan(source_vectors, target_vectors, source_mass, target_mass, candidates)


def solution(mesh):
    placed = (
        P(("group", "member"), None),
        P(("group", "member"), None),
        P(("group", "member")),
        P(("group", "member")),
        P(("group", "member"), None),
    )
    return jax.shard_map(
        shards,
        mesh=mesh,
        in_specs=placed,
        out_specs=(P(("group", "member")), P(("group", "member"))),
        check_vma=False,
    )
```

```python
import functools

import jax
import jax.numpy as jnp
from jax import lax
from jax.experimental import pallas as pl
from jax.experimental.pallas import tpu as pltpu
from jax.sharding import PartitionSpec as P

ITERS = 2


entropy_strength = 0.3
very_low = -1e30


def log_partition(values, axis):
    largest_score = jnp.max(values, axis=axis, keepdims=True)
    return jnp.squeeze(largest_score, axis) + jnp.log(
        jnp.sum(jnp.exp(values - largest_score), axis=axis)
    )


def slot_layout(lists, per_device, members, capacity):
    owner = lists // per_device
    partner = owner % members
    local_block = lists % per_device
    ordering = jnp.arange(lists.shape[-1], dtype=jnp.int32)
    matching = partner[..., :, None] == partner[..., None, :]
    earlier = ordering[None, :] < ordering[:, None]
    position = jnp.sum(jnp.logical_and(matching, earlier).astype(jnp.int32), axis=-1)
    return (partner * capacity + position, local_block)


def trade_member(values):
    return lax.all_to_all(values, "member", split_axis=0, concat_axis=0, tiled=True)


def trade_group(values):
    return lax.all_to_all(values, "group", split_axis=0, concat_axis=0, tiled=True)


def tile_terms(sources, target_blocks, picks, side, by_rows):
    tile_count, block_rows, width = sources.shape
    batch = 4
    grouped = (
        sources.reshape(tile_count // batch, batch, block_rows, width),
        picks.reshape(tile_count // batch, batch),
        side.reshape(tile_count // batch, batch, block_rows),
    )

    def visit(grouped_part):
        source_portion, pick_part, side_portion = grouped_part
        key_entries = jnp.take(target_blocks, pick_part, axis=0)
        score_matrix = jnp.einsum(
            "umk,ugk->umg", source_portion, key_entries, preferred_element_type=jnp.float32
        )
        if by_rows:
            return log_partition((score_matrix + side_portion[:, None, :]) / entropy_strength, 2)
        return log_partition((score_matrix + side_portion[:, :, None]) / entropy_strength, 1)

    return lax.map(visit, grouped).reshape(tile_count, block_rows)


def owner_update(slot_terms, mirror_terms, incoming, target_marginal):
    output_list = []
    for local_block in range(target_marginal.shape[0]):
        masked = jnp.where((incoming == local_block)[:, None], slot_terms, very_low)
        stacked = jnp.concatenate([masked, mirror_terms[local_block][None, :]], axis=0)
        output_list.append(log_partition(stacked, 0))
    return entropy_strength * target_marginal - entropy_strength * jnp.stack(output_list)


def shards_any(source_vectors, target_vectors, source_mass, target_mass, candidates):
    members = lax.axis_size("member")
    groups = lax.axis_size("group")
    own_member = lax.axis_index("member")
    source_count, cand_count = candidates.shape
    inside_count = cand_count - 1
    block_rows = source_vectors.shape[0] // source_count
    width = source_vectors.shape[1]
    target_count = target_vectors.shape[0] // block_rows
    capacity = (source_count * inside_count + members - 1) // members
    spots = members * capacity
    source_blocks = source_vectors.reshape(source_count, block_rows, width)
    target_blocks = target_vectors.reshape(target_count, block_rows, width)
    source_marginal = source_mass.reshape(source_count, block_rows)
    target_marginal = target_mass.reshape(target_count, block_rows)
    own_lists = candidates[:, :inside_count]
    own_spots, own_local = slot_layout(
        own_lists.reshape(1, source_count * inside_count), target_count, members, capacity
    )
    own_spots = own_spots[0]
    all_lists = lax.all_gather(own_lists, "member", axis=0, tiled=True)
    their_spots, their_local = slot_layout(
        all_lists.reshape(members, source_count * inside_count), target_count, members, capacity
    )
    wanted_spots = own_member * capacity + jnp.arange(capacity, dtype=jnp.int32)
    hits = their_spots[:, :, None] == wanted_spots[None, None, :]
    incoming = (jnp.sum(jnp.where(hits, their_local[:, :, None] + 1, 0), axis=1) - 1).reshape(spots)
    picks = jnp.maximum(incoming, 0)
    mirror_group = candidates[:, inside_count] // target_count // members
    spot_range = jnp.arange(spots, dtype=jnp.int32)
    group_range = jnp.arange(groups, dtype=jnp.int32)
    source_of = jnp.arange(source_count * inside_count, dtype=jnp.int32) // inside_count
    slot_index = jnp.sum(
        jnp.where(own_spots[:, None] == spot_range[None, :], source_of[:, None], 0), axis=0
    )
    mirror_index = jnp.sum(
        jnp.where(
            mirror_group[:, None] == group_range[None, :],
            jnp.arange(source_count, dtype=jnp.int32)[:, None],
            0,
        ),
        axis=0,
    )
    slot_payload = jnp.take(source_blocks, slot_index, axis=0)
    mirror_payload = jnp.take(source_blocks, mirror_index, axis=0)
    arrived = lax.all_to_all(
        slot_payload.reshape(members, capacity, block_rows, width),
        "member",
        split_axis=0,
        concat_axis=0,
        tiled=True,
    ).reshape(spots, block_rows, width)
    arrived_mirror = lax.all_to_all(
        mirror_payload, "group", split_axis=0, concat_axis=0, tiled=True
    )
    target_current = jnp.zeros((target_count, block_rows), jnp.float32)
    for step in range(ITERS):
        row_slots = tile_terms(
            arrived, target_blocks, picks, jnp.take(target_current, picks, axis=0), True
        )
        row_mirror = tile_terms(arrived_mirror, target_blocks, group_range, target_current, True)
        slot_back = trade_member(row_slots.reshape(members, capacity, block_rows)).reshape(
            spots, block_rows
        )
        mirror_back = trade_group(row_mirror)
        collected_rows = jnp.concatenate(
            [
                jnp.take(slot_back, own_spots, axis=0).reshape(
                    source_count, inside_count, block_rows
                ),
                jnp.take(mirror_back, mirror_group, axis=0)[:, None],
            ],
            axis=1,
        )
        source_current = entropy_strength * source_marginal - entropy_strength * log_partition(
            collected_rows, 1
        )
        slot_sides = trade_member(
            jnp.take(source_current, slot_index, axis=0).reshape(members, capacity, block_rows)
        ).reshape(spots, block_rows)
        mirror_sides = trade_group(jnp.take(source_current, mirror_index, axis=0))
        column_slots = tile_terms(arrived, target_blocks, picks, slot_sides, False)
        column_mirror = tile_terms(arrived_mirror, target_blocks, group_range, mirror_sides, False)
        target_current = owner_update(column_slots, column_mirror, incoming, target_marginal)
    return (
        source_current.reshape(source_count * block_rows),
        target_current.reshape(target_count * block_rows),
    )


LOG2E = 1.4426950408889634
TO_LOGIT = LOG2E / entropy_strength
TO_POTENTIAL = entropy_strength / LOG2E
SOURCE_SLOTS = 16
TARGET_SLOTS = 12
FAR = 8
CAPACITY = 4
SECTIONS = (
    (0, 0, 0),
    (1, 0, 4),
    (0, 2, 8),
    (2, 0, 12),
    (0, 1, 16),
    (1, 1, 20),
    (2, 1, 24),
    (3, 0, 28),
    (3, 1, 32),
)
EARLY, LATE = SECTIONS[:3], SECTIONS[3:]
LATE_SLOT = 12
TILE_SLOTS = 40
NO_SLOT = 36
GROUP_AT = 39
SMALL, LARGE, LARGEST = 2.0**-100, 2.0**100, 2.0**110


def merge(parts):
    top = functools.reduce(jnp.maximum, parts)
    return top + LOG2E * jnp.log(sum(jnp.exp2(part - top) for part in parts))


def swapped(rows, size):
    pieces = [rows[start : start + size] for start in range(0, rows.shape[0], size)]
    return jnp.concatenate([pieces[index ^ 1] for index in range(len(pieces))], axis=0)


def source_bias(mass_refs, part_refs):
    own, core, near, cross = (ref[0:16] for ref in part_refs)
    core = swapped(core, 4)
    near = swapped(near, 8)
    cross = swapped(swapped(cross, 4), 8)
    mass = jnp.concatenate([ref[16:20] for ref in mass_refs], axis=0)
    return mass - merge([own, core, near, cross])


def target_bias(chosen, columns, partner, mirrors):
    own_across = far_across = jnp.full((4, columns.shape[1]), very_low, jnp.float32)
    for offset, ref in enumerate(mirrors, 1):
        picked = chosen[8 * offset - 8 : 8 * offset - 4] > 0
        own_across = jnp.where(picked, ref[0:1], own_across)
        far_across = jnp.where(picked, ref[1:2], far_across)
    own = columns[12:16] - merge([columns[0:4], partner[8:12], own_across])
    far = partner[12:16] - merge([columns[8:12], partner[0:4], far_across])
    across = [
        ref[3:4] - merge([ref[2:3], columns[3 + offset : 4 + offset]])
        for offset, ref in enumerate(mirrors, 1)
    ]
    blank = jnp.zeros((1, own.shape[1]), jnp.float32)
    return jnp.concatenate([own, *across, blank, far, *([blank] * 4)], axis=0)


def in_parts(rows):
    high = rows.astype(jnp.bfloat16)
    rest = rows - high.astype(jnp.float32)
    middle = rest.astype(jnp.bfloat16)
    low = (rest - middle.astype(jnp.float32)).astype(jnp.bfloat16)
    return jnp.concatenate([high, middle, low], axis=0)


def spread(rows, bias, used=SOURCE_SLOTS):
    count = rows.shape[0]
    shape = (3 * count, used * 128)
    slot = lax.broadcasted_iota(jnp.int32, shape, 0) & (count - 1)
    place = lax.broadcasted_iota(jnp.int32, shape, 1) >> 7
    chosen = jnp.where(slot == place, 1.0, 0.0).astype(jnp.bfloat16)
    turned = lax.dot_general(
        in_parts(rows), chosen, (((0,), (0,)), ((), ())), preferred_element_type=jnp.float32
    )
    for index in range(used):
        bias[index] = turned[:, 128 * index : 128 * (index + 1)]


def score(summed, kept):
    product = lax.dot_general(summed, kept, (((1,), (1,)), ((), ())), preferred_element_type=jnp.float32)
    return product * TO_LOGIT


def wide(values):
    return jnp.concatenate([values, values], axis=1)


def exact_pass(lists, by_rows, sections, sources, targets, tops, sums, ids):
    summed_row, kept_row = (1, 0) if by_rows else (0, 1)
    ids[...] = jnp.full(ids.shape, -1, jnp.int32)
    for source, target, first in sections:
        pair = (sources[source], targets[target])
        for slot in range(first, first + CAPACITY):
            blocks = [array[lists[row, slot]] for row, array in enumerate(pair)]
            exact_tile(lists, by_rows, slot, blocks, None, tops, sums, ids)
    return merge_tiles(by_rows, tops, sums, ids)


def exact_tile(lists, by_rows, slot, blocks, bias, tops, sums, ids):
    summed, kept = blocks[::-1] if by_rows else blocks
    logits = score(summed, kept)
    if bias is not None:
        count = bias.shape[0] - 1
        logits = logits + wide(bias[jnp.minimum(lists[3 if by_rows else 2, slot], count)])
    top = jnp.max(logits, axis=0, keepdims=True)
    tops[pl.ds(slot, 1), :] = top
    sums[pl.ds(slot, 1), :] = jnp.sum(jnp.exp2(logits - top), axis=0, keepdims=True)
    ids[pl.ds(slot, 1), :] = jnp.full((1, ids.shape[1]), lists[2 if by_rows else 3, slot], jnp.int32)


def merge_tiles(by_rows, tops, sums, ids):
    best, total = [], []
    for block in range(SOURCE_SLOTS if by_rows else TARGET_SLOTS):
        mine = ids[...] == block
        top = jnp.max(jnp.where(mine, tops[...], very_low), axis=0, keepdims=True)
        best.append(top)
        total.append(
            jnp.sum(jnp.where(mine, sums[...] * jnp.exp2(tops[...] - top), 0.0), axis=0, keepdims=True)
        )
    best = jnp.concatenate(best, axis=0)
    total = jnp.concatenate(total, axis=0)
    return jnp.where(total > 0, best + LOG2E * jnp.log(jnp.where(total > 0, total, 1.0)), very_low)


def exact_loop(lists, by_rows, first, sources, targets, bias, shift, work):
    tops, sums, ids, packed, semaphore = work
    for index, blocks in enumerate((*sources, *targets)):
        copy = pltpu.make_async_copy(blocks, packed.at[pl.ds(4 * index, 4)], semaphore)
        copy.start()
        copy.wait()
    ids[...] = jnp.full(ids.shape, -1, jnp.int32)

    def visit(slot, carry):
        blocks = packed[lists[4, slot]], packed[lists[5, slot]]
        exact_tile(lists, by_rows, slot, blocks, bias, tops, sums, ids)
        return carry

    lax.fori_loop(first, NO_SLOT, visit, 0)
    result = merge_tiles(by_rows, tops, sums, ids)
    return result if bias is None or shift is None else result - shift


def guarded_pass(lists, present, by_rows, sections, sources, targets, bias, shift, total, work, write):
    summed_row, kept_row = (1, 0) if by_rows else (0, 1)
    total[...] = jnp.zeros(total.shape, jnp.float32)
    for source, target, first in sections:
        pair = (sources[source], targets[target])
        summed, kept = pair[summed_row], pair[kept_row]
        for slot in range(first, first + CAPACITY):
            block = lists[summed_row, slot]
            logits = score(summed[block], kept[lists[kept_row, slot]])
            if bias is None:
                logits = logits + shift
            else:
                if not by_rows:
                    place = 4 * source + block
                elif target == 2:
                    place = lists[3, slot]
                else:
                    place = FAR * target + block
                logits = logits + wide(bias[place])
            terms = jnp.exp2(logits)
            place = lists[2 + kept_row, slot]
            total[place] = total[place] + jnp.sum(terms.reshape(-1, 8, terms.shape[1]), axis=0)
    count = SOURCE_SLOTS if by_rows else TARGET_SLOTS
    sums_of = jnp.concatenate(
        [jnp.sum(total[block], axis=0, keepdims=True) for block in range(count)], axis=0
    )
    here = wide(present[0:count]) > 0
    result = LOG2E * jnp.log(jnp.where(here, sums_of, 1.0))
    if shift is not None:
        result = result - shift
    write(jnp.where(here, result, very_low))
    fine = jnp.logical_and(sums_of > SMALL, sums_of < LARGE)
    worst = jnp.min(jnp.where(jnp.logical_or(fine, jnp.logical_not(here)), 1.0, 0.0))

    @pl.when(worst < 0.5)
    def _():
        write(exact_loop(lists, by_rows, sections[0][2], sources, targets, bias, shift, work))


def middle(pieces):
    top = functools.reduce(jnp.maximum, [jnp.max(piece, axis=(0, 1), keepdims=True) for piece in pieces])
    bottom = functools.reduce(jnp.minimum, [jnp.min(piece, axis=(0, 1), keepdims=True) for piece in pieces])
    return 0.5 * (top + bottom)


def early_kernel(lists, wait, own, core, target, mirrors, out, reference, tops, sums, ids):
    wait()
    result = exact_pass(lists, True, EARLY, (own, core), (target, None, mirrors), tops, sums, ids)
    out[...] = result
    largest = jnp.max(result, axis=(0, 1), keepdims=True)
    reference[...] = jnp.broadcast_to(-largest, reference.shape)


def first_kernel(lists, wait, present, cross, *refs):
    near_sources, targets = refs[0:3], refs[3:6]
    reference, early, mass, out, far_source, total, *work = refs[6:]
    far_source[...] = cross[...]
    out[16:20, :] = mass[...]
    out[20:24, :] = jnp.zeros((4, out.shape[1]), jnp.float32)

    def write(result):
        out[0:16, :] = merge([early[...], result])

    wait()
    guarded_pass(
        lists,
        present,
        True,
        LATE,
        (*near_sources, cross),
        targets,
        None,
        reference[0:1, 0:1],
        total,
        work,
        write,
    )


def columns_kernel(last_pass, lists, wait, present, *refs):
    sources, targets = refs[0:4], refs[4:7]
    masses, target_mass, rest = refs[7:11], refs[11], refs[12:]
    parts, shift = masses, None
    if last_pass:
        parts, (shift, *rest) = rest[:4], rest[4:]
        shift = shift[0:1, 0:1]
    out, second, bias, total, *work = rest
    rows = source_bias(masses, parts)
    spread(rows + shift if last_pass else rows, bias)
    if last_pass:
        for block in range(4):
            for half in range(2):
                second[2 * block + half : 2 * block + half + 1, :] = (
                    rows[block : block + 1, 128 * half : 128 * (half + 1)]
                )
    else:
        second[...] = jnp.broadcast_to(middle([rows]), second.shape)
    out[12:16, :] = target_mass[0:4]

    def write(result):
        out[0:TARGET_SLOTS, :] = result

    wait()
    guarded_pass(
        lists, present, False, SECTIONS, sources, targets, bias, shift, total, work, write
    )


def rows_kernel(lists, wait, present, *refs):
    sources, targets = refs[0:4], refs[4:7]
    chosen, shift, columns, partner, *mirrors = refs[7:14]
    out, second, bias, total, *work = refs[14:]
    rows = target_bias(chosen, columns, partner, mirrors)
    shift = shift[0:1, 0:1]
    spread(rows + shift, bias, TARGET_SLOTS)
    second[...] = jnp.broadcast_to(middle([rows[0:7], rows[8:12]]), second.shape)

    def write(result):
        out[...] = result

    wait()
    guarded_pass(lists, present, True, SECTIONS, sources, targets, bias, shift, total, work, write)


def forward_kernel(chosen, columns, partner, *outs):
    totals = merge([columns[0:4], partner[8:12]])
    masses = columns[12:16]
    for offset, out in enumerate(outs, 1):
        picked = chosen[8 * offset - 8 : 8 * offset - 4] > 0
        out[0:1, :] = columns[3 + offset : 4 + offset]
        out[1:2, :] = partner[3 + offset : 4 + offset]
        out[2:3, :] = jnp.sum(jnp.where(picked, totals, 0.0), axis=0, keepdims=True)
        out[3:4, :] = jnp.sum(jnp.where(picked, masses, 0.0), axis=0, keepdims=True)


def finish_kernel(chosen, columns, partner, *rest):
    *mirrors, out = rest
    across = jnp.full((4, columns.shape[1]), very_low, jnp.float32)
    for offset, ref in enumerate(mirrors, 1):
        picked = chosen[8 * offset - 8 : 8 * offset - 4] > 0
        across = jnp.where(picked, ref[3 + offset : 4 + offset], across)
    rows = columns[12:16] - merge([columns[0:4], partner[8:12], across])
    for block in range(4):
        for half in range(2):
            out[2 * block + half : 2 * block + half + 1, :] = (
                TO_POTENTIAL * rows[block : block + 1, 128 * half : 128 * (half + 1)]
            )


SMEM, VMEM = pltpu.SMEM, pltpu.VMEM


def call(kernel, inputs, outs, scratch=(), scalar=True):
    whole = pl.BlockSpec(memory_space=VMEM)
    first = pl.BlockSpec(memory_space=SMEM) if scalar and inputs[0].dtype == jnp.int32 else whole
    return pl.pallas_call(
        kernel,
        out_shape=outs,
        in_specs=[first] + [whole] * (len(inputs) - 1),
        out_specs=[whole] * len(outs),
        scratch_shapes=list(scratch),
        compiler_params=pltpu.CompilerParams(vmem_limit_bytes=16 << 20),
    )(*inputs)


def call_tiles(kernel, lists, inputs, outs, scratch=(), early=True):
    def body(origin, *refs):
        *refs, scalars, semaphore = refs
        copy = pltpu.make_async_copy(origin, scalars, semaphore)
        copy.start()
        kernel(scalars, copy.wait, *refs)

    def plain(scalars, *refs):
        kernel(scalars, lambda: None, *refs)

    if early:
        return call(plain, [lists, *inputs], outs, scratch)
    extra = [SMEM(lists.shape, lists.dtype), pltpu.SemaphoreType.DMA]
    return call(body, [lists, *inputs], outs, [*scratch, *extra], False)


def swap(values, axis, size, bit):
    return lax.ppermute(values, axis, [(index, index ^ bit) for index in range(size)])


def tile_lists(table, group, member):
    count = table.shape[1]
    row = jnp.arange(table.shape[0], dtype=jnp.int32)[:, None]
    source = row >> 2
    pick = jnp.arange(count, dtype=jnp.int32)[None, :]
    is_last = pick == count - 1
    apart = ((table >> 2) & 7) ^ member
    far = jnp.logical_and(~is_last, apart == 4)
    other = table >> 5
    starts = {(source, target): first for source, target, first in SECTIONS}

    def first_of(target):
        return functools.reduce(
            lambda value, index: jnp.where(source == index, starts[index, target], value),
            range(1, 4),
            jnp.full(source.shape, starts[0, target], jnp.int32),
        )

    section = jnp.where(apart == 0, first_of(0), jnp.where(apart == 4, first_of(1), -1))
    section = jnp.where(is_last, jnp.where(source == 0, starts[0, 2], -1), section)
    local = table & 3
    block = jnp.where(is_last, other, local)
    slot = jnp.where(is_last, jnp.where(other == group, local, 3 + (other ^ group)), local)
    slot = slot + jnp.where(far, FAR, 0)
    array = jnp.where(is_last, 6, jnp.where(far, 5, 4))
    code = (row & 3) + 4 * block + 16 * row + 512 * slot + 16384 * (4 * array + block)
    section, code = section.reshape(-1), code.reshape(-1)
    order = jnp.arange(section.shape[0], dtype=jnp.int32)
    earlier = jnp.logical_and(order[None, :] < order[:, None], section[None, :] == section[:, None])
    place = jnp.where(section >= 0, section + jnp.sum(earlier.astype(jnp.int32), axis=1), -1)
    slots = jnp.arange(TILE_SLOTS, dtype=jnp.int32)
    hits = place[None, :] == slots[:, None]
    found = jnp.sum(jnp.where(hits, code[None, :] + 1, 0), axis=1)
    found = jnp.where(found > 0, found - 1, SOURCE_SLOTS * 16 + TARGET_SLOTS * 512 + 16 * 16384)
    source_slots, target_slots = (found >> 4) & 31, (found >> 9) & 31
    blocks = jnp.minimum(source_slots, SOURCE_SLOTS - 1), found >> 14
    lists = jnp.stack(
        [
            jnp.where(slots == GROUP_AT, group, found & 3),
            (found >> 2) & 3,
            source_slots,
            target_slots,
            *blocks,
        ]
    )
    late_slots = jnp.where(slots >= LATE_SLOT, source_slots, SOURCE_SLOTS)
    rows = jnp.arange(16, dtype=jnp.int32)
    present = [
        jnp.broadcast_to(
            jnp.any(taken[None, :] == rows[:, None], axis=1).astype(jnp.float32)[:, None], (16, 128)
        )
        for taken in (source_slots, target_slots, late_slots)
    ]
    return lists, *present


def shards_quad(source_vectors, target_vectors, source_mass, target_mass, candidates):
    members = lax.axis_size("member")
    groups = lax.axis_size("group")
    own_group = lax.axis_index("group")
    own_member = lax.axis_index("member")
    per_device, cand_count = candidates.shape
    block_rows = source_vectors.shape[0] // per_device
    width = source_vectors.shape[1]
    blocked = (per_device, block_rows, width)
    member_swap = lambda values, bit: swap(values, "member", members, bit)
    group_swap = lambda values, bit: swap(values, "group", groups, bit)

    source_own = source_vectors.reshape(blocked)
    target_own = target_vectors.reshape(blocked)
    target_far = member_swap(target_own, 4)
    source_near = member_swap(source_own, 2)
    named = jnp.concatenate([candidates, member_swap(candidates, 2)])
    source_late, target_late, named = lax.optimization_barrier((source_own, target_own, named))
    source_core = member_swap(source_late, 1)
    named_core = member_swap(named, 1)
    mirrors = lax.all_to_all(target_late, "group", split_axis=0, concat_axis=0, tiled=True)
    lists, has_source, has_target, has_late = tile_lists(
        jnp.concatenate([named[0:4], named_core[0:4], named[4:8], named_core[4:8]]),
        own_group.astype(jnp.int32),
        own_member.astype(jnp.int32),
    )
    own_source_mass = LOG2E * source_mass.reshape(per_device, block_rows)
    marked = jnp.arange(24, dtype=jnp.int32)
    marked = (marked & 7) == (own_group.astype(jnp.int32) ^ ((marked >> 3) + 1))
    chosen = jnp.broadcast_to(marked.astype(jnp.float32)[:, None], (24, block_rows))
    own_mass = LOG2E * target_mass.reshape(per_device, block_rows)

    side = jax.ShapeDtypeStruct((16, block_rows), jnp.float32)
    flat = jax.ShapeDtypeStruct((8, 128), jnp.float32)
    tile_rows = [VMEM((TILE_SLOTS, block_rows), kind) for kind in (jnp.float32, jnp.float32, jnp.int32)]
    pass_buffers = [
        VMEM((SOURCE_SLOTS + 1, 8, block_rows), jnp.float32),
        *tile_rows,
        VMEM((28, block_rows, width), source_vectors.dtype),
        pltpu.SemaphoreType.DMA,
    ]
    bias_buffer = VMEM((SOURCE_SLOTS, block_rows, 128), jnp.float32)

    early, reference = call_tiles(
        early_kernel, lists, [source_own, source_core, target_own, mirrors], [side, flat], tile_rows
    )
    source_near, early = lax.optimization_barrier((source_near, early))
    source_cross = member_swap(source_near, 1)
    nothing = jnp.minimum(candidates[0, 0], 0).astype(source_cross.dtype)
    target_far, source_cross = lax.optimization_barrier((target_far, source_cross + nothing))
    sources, targets = [source_own, source_core, source_near], [target_own, target_far, mirrors]
    parts, source_cross = call_tiles(
        first_kernel,
        lists,
        [has_late, source_cross, *sources, *targets, reference, early, own_source_mass],
        [
            jax.ShapeDtypeStruct((24, block_rows), jnp.float32),
            jax.ShapeDtypeStruct(blocked, source_vectors.dtype),
        ],
        pass_buffers,
    )
    blocks = [*sources, source_cross, *targets]
    masses, extra = [], []
    for step in range(ITERS):
        last_pass = step == ITERS - 1
        parts = [parts] + [member_swap(parts, bit) for bit in (1, 2, 3)]
        masses = masses or parts
        columns, potential = call_tiles(
            functools.partial(columns_kernel, last_pass),
            lists,
            [has_target, *blocks, *masses, own_mass, *(parts + extra if last_pass else [])],
            [side, flat],
            [bias_buffer, *pass_buffers],
            early=not last_pass,
        )
        partner = member_swap(columns, 4)
        if last_pass:
            break
        sent = call(
            forward_kernel,
            [chosen, columns, partner],
            [jax.ShapeDtypeStruct((4, block_rows), jnp.float32)] * 3,
        )
        received = [group_swap(values, bit) for bit, values in enumerate(sent, 1)]
        parts, shift = call_tiles(
            rows_kernel,
            lists,
            [has_source, *blocks, chosen, potential, columns, partner, *received],
            [side, flat],
            [bias_buffer, *pass_buffers],
            early=False,
        )
        extra = [shift]
    received = [group_swap(columns, bit) for bit in (1, 2, 3)]
    (final,) = call(
        finish_kernel,
        [chosen, columns, partner, *received],
        [flat],
    )
    return (TO_POTENTIAL * potential).reshape(source_mass.shape), final.reshape(target_mass.shape)


def shards(source_vectors, target_vectors, source_mass, target_mass, candidates):
    quad = lax.axis_size("member") == 8 and lax.axis_size("group") == 4 and candidates.shape == (4, 8)
    plan = shards_quad if quad else shards_any
    return plan(source_vectors, target_vectors, source_mass, target_mass, candidates)


def solution(mesh):
    placed = (
        P(("group", "member"), None),
        P(("group", "member"), None),
        P(("group", "member")),
        P(("group", "member")),
        P(("group", "member"), None),
    )
    return jax.shard_map(
        shards,
        mesh=mesh,
        in_specs=placed,
        out_specs=(P(("group", "member")), P(("group", "member"))),
        check_vma=False,
    )
```
